32 devices in a mesh: batch: 4 (over y, x), lat: 2 (over core), lon: 4 (over z).
Axes of the slice: x: 2, y: 2, z: 4, core: 2. Of those that a mesh axis runs over, the one named last changes fastest.
Arguments:
- patches: bfloat16 [4, 4, 12, 128, 640], P('batch', 'lat', 'lon'), may hold values from -6 to 6
- kept_index: int32 [4, 4, 12, 64], P('batch', 'lat', 'lon'), may hold values from 0 to 127, as said below
- kept_count: int32 [4, 4, 12], P('batch', 'lat', 'lon'), may hold values from 32 to 64, as said below
- embed_weight: bfloat16 [640, 1280], P('batch'), may hold values from -0.25 to 0.25
- local_qkv: bfloat16 [1280, 3840], P('batch'), may hold values from -6 to 6
- local_out: bfloat16 [1280, 1280], P('batch'), may hold values from -0.15625 to 0.15625
- global_qkv: bfloat16 [1280, 3840], P('batch'), may hold values from -6 to 6
Outputs:
- mixed: bfloat16 [4, 4, 12, 64, 1280], P('batch', 'lat', 'lon')
The draws below stay inside these ranges and needn't reach their ends.
Inputs may be any that keep to these rules, and one draw needn't show every extreme that they name: `kept_index`: in each window all 64 entries are distinct offsets; the first kept_count of them are the kept tokens in rising order. `kept_count`: every device holds, in its sample, a window with exactly 64 kept tokens.
All inputs are finite; a program needn't handle non-finite values.
Results may differ from the reference program's by a relative error of at most 0.023.
Values may be sent and summed in bfloat16 or wider, within the bound.
No kernel may reach another device: no remote copies, remote signals or barrier semaphores. Data moves between devices by JAX's collectives and lax.ppermute only.
A program may use at most 128 MiB of HBM per device.

```python
import jax
import jax.numpy as jnp
from jax import lax

PIN = 640
D = 1280
HEADS = 8
HD = 160
INNER = 1280
WT = 128
KMAX = 64
WLAT = 2
WLON = 3
SAMPLES = 4
NWLAT = 4
NWLON = 12


def kept_counts(key):
    base = jax.random.fold_in(key, 17)
    counts = jax.random.randint(base, (SAMPLES, NWLAT, NWLON), KMAX // 2, KMAX + 1)
    lat_first = (jnp.arange(NWLAT) % WLAT == 0)[None, :, None]
    lon_first = (jnp.arange(NWLON) % WLON == 0)[None, None, :]
    return jnp.where(lat_first & lon_first, KMAX, counts).astype(jnp.int32)


def draw_kept_count(key, part):
    return kept_counts(key)


def shuffle(sub_key):
    return jax.random.permutation(sub_key, WT)


def draw_kept_index(key, part):
    counts = kept_counts(key)
    total_windows = SAMPLES * NWLAT * NWLON
    sub_keys = jax.random.split(jax.random.fold_in(key, 29), total_windows)
    orders = jax.vmap(shuffle)(sub_keys).astype(jnp.int32)
    positions = jnp.arange(WT, dtype=jnp.int32)[None, :]
    chosen = positions < counts.reshape(total_windows, 1)
    ranked = jnp.sort(jnp.where(chosen, orders, orders + WT), axis=1)
    ranked = jnp.where(ranked >= WT, ranked - WT, ranked)
    return ranked[:, :KMAX].reshape(SAMPLES, NWLAT, NWLON, KMAX).astype(jnp.int32)


def drawn_qkv(key):
    base = jax.random.normal(jax.random.fold_in(key, 3), (D, 3, INNER), jnp.float32) * D ** (-0.5)
    base = jnp.clip(base, -6.0, 6.0)
    return base.reshape(D, 3 * INNER).astype(jnp.bfloat16)


def draw_local_qkv(key, part):
    return drawn_qkv(jax.random.fold_in(key, 41))


def draw_global_qkv(key, part):
    return drawn_qkv(jax.random.fold_in(key, 43))


def block_scale(own_key, dims, pieces, smallest, high):
    factor_of = 1.0
    for axis_at, parts in pieces:
        steps = jax.random.uniform(jax.random.fold_in(jax.random.fold_in(own_key, 6), axis_at), (parts,), jnp.float32, smallest / len(pieces), high / len(pieces))
        factor_of = factor_of * jnp.repeat(jnp.exp(steps), dims[axis_at] // parts).reshape((-1,) + (1,) * (len(dims) - 1 - axis_at))
    return factor_of


def noise(own_key, dims, scale, most, cuts=(), kind=jnp.bfloat16):
    drawn = scale * jax.random.normal(own_key, dims, jnp.float32)
    if cuts:
        drawn = drawn * block_scale(own_key, dims, cuts, -0.22, 0.18)
    return jnp.clip(drawn, -most, most).astype(kind)


def setup_inputs(seed: int = 0) -> dict:
    arg_keys = jax.random.split(jax.random.key(seed), 8)
    return {
        "patches": noise(arg_keys[0], (SAMPLES, NWLAT, NWLON, WT, PIN), 1.0, 6.0, ((0, 4), (1, 2), (2, 4))),
        "kept_index": draw_kept_index(jax.random.fold_in(arg_keys[7], 71), 0),
        "kept_count": draw_kept_count(jax.random.fold_in(arg_keys[7], 71), 0),
        "embed_weight": noise(arg_keys[3], (PIN, D), PIN ** -0.5, 0.25, ((0, 4),)),
        "local_qkv": draw_local_qkv(jax.random.fold_in(arg_keys[7], 71), 0),
        "local_out": noise(arg_keys[5], (INNER, D), INNER ** -0.5, 0.15625, ((0, 4),)),
        "global_qkv": draw_global_qkv(jax.random.fold_in(arg_keys[7], 71), 0),
    }


norm_eps = 1e-05
mask_floor = -1e+30

def rounded(values):
    return lax.optimization_barrier(values.astype(jnp.bfloat16))

def layer_norm(values):
    centre = values - lax.optimization_barrier(jnp.mean(values, axis=-1, keepdims=True))
    spread = lax.optimization_barrier(jnp.mean(centre * centre, axis=-1, keepdims=True))
    return centre * lax.rsqrt(spread + norm_eps)

def attend(query_rows, key_rows, value_rows, keep_mask):
    scores = jnp.einsum('bnhd,bmhd->bhnm', query_rows.astype(jnp.float32), key_rows.astype(jnp.float32)) * HD ** (-0.5)
    scores = jnp.where(keep_mask[:, None, None, :], scores, mask_floor)
    scores = scores - lax.optimization_barrier(jnp.max(scores, axis=-1, keepdims=True))
    weights = jnp.exp(scores)
    probabilities = rounded(weights / lax.optimization_barrier(jnp.sum(weights, axis=-1, keepdims=True)))
    blended = jnp.einsum('bhnm,bmhd->bnhd', probabilities.astype(jnp.float32), value_rows.astype(jnp.float32))
    return rounded(blended).reshape(query_rows.shape[0], query_rows.shape[1], HEADS * HD)

def reference(patches, kept_index, kept_count, embed_weight, local_qkv, local_out, global_qkv):

    def one_sample(inputs):
        patch_all, index_all, count_all = inputs
        windows = NWLAT * NWLON
        patch_rows = patch_all.reshape(windows, WT, PIN)
        index_rows = index_all.reshape(windows, KMAX)
        kept_mask = jnp.arange(KMAX, dtype=jnp.int32)[None, :] < count_all.reshape(windows, 1)
        picked = jnp.take_along_axis(patch_rows, index_rows[:, :, None], axis=1).reshape(windows * KMAX, PIN)
        embedded = rounded(jnp.dot(picked, embed_weight, preferred_element_type=jnp.float32))
        normed = rounded(layer_norm(embedded.astype(jnp.float32)))
        local_proj = rounded(jnp.dot(normed, local_qkv, preferred_element_type=jnp.float32))
        local_proj = local_proj.reshape(windows, KMAX, 3, HEADS, HD)
        local_mix = attend(local_proj[:, :, 0], local_proj[:, :, 1], local_proj[:, :, 2], kept_mask)
        local_mix = local_mix.reshape(windows * KMAX, HEADS * HD)
        hidden = rounded(embedded.astype(jnp.float32) + jnp.dot(local_mix, local_out, preferred_element_type=jnp.float32))
        normed_global = rounded(layer_norm(hidden.astype(jnp.float32)))
        global_proj = rounded(jnp.dot(normed_global, global_qkv, preferred_element_type=jnp.float32))
        global_proj = global_proj.reshape(windows, KMAX, 3 * HEADS * HD)
        window_ids = jnp.broadcast_to(jnp.arange(windows, dtype=jnp.int32)[:, None], (windows, KMAX))
        slot_rows = jnp.zeros((WT, windows, 3 * HEADS * HD), global_proj.dtype).at[index_rows, window_ids].set(global_proj)
        slot_keep = jnp.zeros((WT, windows), bool).at[index_rows, window_ids].set(kept_mask)
        block_rows = slot_rows.reshape(WT // 8, 8, windows, 3, HEADS, HD)
        block_keep = slot_keep.reshape(WT // 8, 8, windows)

        def offset_block(pair):
            rows_here, keep_here = pair
            return attend(rows_here[:, :, 0], rows_here[:, :, 1], rows_here[:, :, 2], keep_here)
        blended = lax.map(offset_block, (block_rows, block_keep)).reshape(WT, windows, HEADS * HD)
        gathered = blended[index_rows, window_ids]
        result = jnp.where(kept_mask[:, :, None], gathered, jnp.zeros_like(gathered))
        return result.reshape(NWLAT, NWLON, KMAX, HEADS * HD)
    return lax.map(one_sample, (patches, kept_index, kept_count))
```

```python
import functools

import jax
import jax.numpy as jnp
from jax import lax
from jax.experimental import pallas as pl
from jax.experimental.pallas import tpu as pltpu
from jax.sharding import PartitionSpec as P

HEADS = 8
HD = 160


norm_eps = 1e-05
mask_floor = -1e30
vmem_limit = 56 * 1024 * 1024
exp2_scale = HD ** (-0.5) * 1.4426950408889634


def layer_norm(values):
    centre = values - jnp.mean(values, axis=-1, keepdims=True)
    spread = jnp.mean(centre * centre, axis=-1, keepdims=True)
    return centre * lax.rsqrt(spread + norm_eps)


def fold_product(left_rows, shard_rows):
    return jnp.dot(left_rows, shard_rows, preferred_element_type=jnp.float32)


def attend(query_rows, key_rows, value_rows, keep_mask):
    scores = jnp.einsum(
        "bnhd,bmhd->bhnm", query_rows, key_rows, preferred_element_type=jnp.float32
    ) * HD ** (-0.5)
    scores = jnp.where(keep_mask[:, None, None, :], scores, mask_floor)
    scores = scores - jnp.max(scores, axis=-1, keepdims=True)
    weights = jnp.exp(scores)
    probabilities = (weights / jnp.sum(weights, axis=-1, keepdims=True)).astype(jnp.bfloat16)
    blended = jnp.einsum(
        "bhnm,bmhd->bnhd", probabilities, value_rows, preferred_element_type=jnp.float32
    )
    return blended.astype(jnp.bfloat16).reshape(
        query_rows.shape[0], query_rows.shape[1], HEADS * HD
    )


def owner_work(received, flag_rows, whole_global):
    item_count = received.shape[0]
    slot_values = received.reshape(item_count, -1, received.shape[-1])
    projected = jnp.dot(
        slot_values.reshape(-1, slot_values.shape[-1]),
        whole_global,
        preferred_element_type=jnp.float32,
    )
    slot_values = projected.astype(jnp.bfloat16).reshape(item_count, -1, 3 * HEADS * HD)
    heads_split = slot_values.reshape(item_count, slot_values.shape[1], 3, HEADS, HD)
    keep_mask = flag_rows.reshape(item_count, -1) > 0
    return attend(heads_split[:, :, 0], heads_split[:, :, 1], heads_split[:, :, 2], keep_mask)


def owner_body(patches, kept_index, kept_count, embed_weight, local_qkv, local_out, global_qkv):
    lat_windows = patches.shape[1]
    lon_windows = patches.shape[2]
    windows = lat_windows * lon_windows
    window_tokens = patches.shape[3]
    kept_most = kept_index.shape[3]
    row_count = windows * kept_most
    inner_width = HEADS * HD
    patch_rows = patches.reshape(windows, window_tokens, patches.shape[4])
    index_rows = kept_index.reshape(windows, kept_most)
    kept_mask = lax.broadcasted_iota(jnp.int32, (windows, kept_most), 1) < kept_count.reshape(
        windows, 1
    )
    picked = jnp.take_along_axis(patch_rows, index_rows[:, :, None], axis=1).reshape(row_count, -1)
    embedded = fold_product(
        picked, lax.all_gather(embed_weight, "batch", axis=0, tiled=True)
    ).astype(jnp.bfloat16)
    normed = layer_norm(embedded.astype(jnp.float32)).astype(jnp.bfloat16)
    local_proj = fold_product(
        normed, lax.all_gather(local_qkv, "batch", axis=0, tiled=True)
    ).astype(jnp.bfloat16)
    local_split = local_proj.reshape(windows, kept_most, 3, HEADS, HD)
    local_mix = attend(
        local_split[:, :, 0], local_split[:, :, 1], local_split[:, :, 2], kept_mask
    ).reshape(row_count, inner_width)
    back_sum = fold_product(local_mix, lax.all_gather(local_out, "batch", axis=0, tiled=True))
    hidden = (embedded.astype(jnp.float32) + back_sum).astype(jnp.bfloat16)
    normed_global = layer_norm(hidden.astype(jnp.float32)).astype(jnp.bfloat16)
    whole_global = lax.all_gather(global_qkv, "batch", axis=0, tiled=True)
    sent_width = normed_global.shape[1]
    window_ids = lax.broadcasted_iota(jnp.int32, (windows, kept_most), 0)
    slot_rows = (
        jnp.zeros((window_tokens, windows, sent_width), jnp.bfloat16)
        .at[index_rows, window_ids]
        .set(normed_global.reshape(windows, kept_most, sent_width))
    )
    flag_slots = (
        jnp.zeros((window_tokens, windows), jnp.bfloat16)
        .at[index_rows, window_ids]
        .set(kept_mask.astype(jnp.bfloat16))
    )
    owners = lax.axis_size("lat") * lax.axis_size("lon")
    owned_count = window_tokens // owners
    blended = owner_work(
        lax.all_to_all(
            slot_rows.reshape(owned_count, owners, windows, sent_width),
            ("lat", "lon"),
            split_axis=1,
            concat_axis=2,
            tiled=True,
        ),
        lax.all_to_all(
            flag_slots.reshape(owned_count, owners, windows),
            ("lat", "lon"),
            split_axis=1,
            concat_axis=2,
            tiled=True,
        ),
        whole_global,
    )
    shaped = blended.reshape(blended.shape[0], 1, -1, inner_width)
    returned = lax.all_to_all(shaped, ("lat", "lon"), split_axis=2, concat_axis=1, tiled=True)
    out_slots = returned.reshape(window_tokens, windows, inner_width)
    gathered = out_slots[index_rows, window_ids]
    result = jnp.where(kept_mask[:, :, None], gathered, jnp.zeros_like(gathered))
    return result.reshape(1, lat_windows, lon_windows, kept_most, inner_width)


def whole_block(array):
    zeros = (0,) * array.ndim
    return pl.BlockSpec(array.shape, lambda *_: zeros)


def assemble(offset_ref, piece_refs, weight_ref):
    for at, piece in enumerate(piece_refs):
        start = pl.multiple_of(offset_ref[at], 16)
        weight_ref[pl.ds(start, piece.shape[0]), :] = piece[...]


def call(kernel, steps, offsets, row_inputs, whole_inputs, pieces, outs, scratch, flops, name):
    specs = [pl.BlockSpec((rows, a.shape[1]), lambda i, _: (i, 0)) for a, rows in row_inputs]
    specs += [whole_block(a) for a in whole_inputs]
    specs += [whole_block(a) for a in pieces]
    arrays = [a for a, _ in row_inputs] + list(whole_inputs) + list(pieces)
    out_shapes = [jax.ShapeDtypeStruct(s, jnp.bfloat16) for s, _ in outs]
    moved = sum(a.size * a.dtype.itemsize for a in arrays) + sum(2 * s.size for s in out_shapes)
    return pl.pallas_call(
        kernel,
        grid_spec=pltpu.PrefetchScalarGridSpec(
            num_scalar_prefetch=1,
            grid=(steps,),
            in_specs=specs,
            out_specs=[pl.BlockSpec((rows, s[1]), lambda i, _: (i, 0)) for s, rows in outs],
            scratch_shapes=scratch,
        ),
        out_shape=out_shapes,
        compiler_params=pltpu.CompilerParams(vmem_limit_bytes=vmem_limit),
        cost_estimate=pl.CostEstimate(flops=flops, bytes_accessed=moved, transcendentals=0),
        name=name,
    )(offsets, *arrays)


def embed_kernel(piece_count, offset_ref, picked_ref, *refs):
    pieces, (embedded_ref, normed_ref, weight_ref) = refs[:piece_count], refs[piece_count:]

    @pl.when(pl.program_id(0) == 0)
    def _():
        assemble(offset_ref, pieces, weight_ref)

    embedded = fold_product(picked_ref[...], weight_ref[...]).astype(jnp.bfloat16)
    embedded_ref[...] = embedded
    normed_ref[...] = layer_norm(embedded.astype(jnp.float32)).astype(jnp.bfloat16)


def masked_mix(query, key, value, mask):
    scores = lax.dot_general(
        query, key, (((1,), (1,)), ((), ())), preferred_element_type=jnp.float32
    )
    scores = jnp.where(mask, scores, mask_floor)
    top = jnp.max(scores, axis=-1, keepdims=True)
    weights = jnp.exp2((scores - top) * exp2_scale)
    total = jnp.sum(weights, axis=-1, keepdims=True)
    mixed = fold_product(weights.astype(jnp.bfloat16), value)
    return mixed / total


def window_kernel(piece_count, kept_most, rows_at_once, offset_ref, normed_ref, code_ref, *refs):
    pieces, (mix_ref, weight_ref, proj_ref) = refs[:piece_count], refs[piece_count:]

    @pl.when(pl.program_id(0) == 0)
    def _():
        assemble(offset_ref, pieces, weight_ref)

    proj_ref[...] = fold_product(normed_ref[...], weight_ref[...]).astype(jnp.bfloat16)
    width = mix_ref.shape[1]
    rows = normed_ref.shape[0]
    own_window = lax.broadcasted_iota(jnp.int32, (rows_at_once, 1), 0) // kept_most
    for start in range(0, rows, rows_at_once):
        part = pl.ds(start, rows_at_once)
        mask = own_window == code_ref[0, :, part]
        for head in range(width // HD):
            query, key, value = (
                proj_ref[part, pl.ds(which * width + head * HD, HD)] for which in range(3)
            )
            mix_ref[part, pl.ds(head * HD, HD)] = masked_mix(query, key, value, mask).astype(
                jnp.bfloat16
            )


def out_kernel(piece_count, mix_count, offset_ref, embedded_ref, *refs):
    mixes, refs = refs[:mix_count], refs[mix_count:]
    pieces, (normed_ref, weight_ref) = refs[:piece_count], refs[piece_count:]

    @pl.when(pl.program_id(0) == 0)
    def _():
        assemble(offset_ref, pieces, weight_ref)

    hidden = embedded_ref[...].astype(jnp.float32)
    at = 0
    for mix in mixes:
        width = mix.shape[1]
        hidden += fold_product(mix[...], weight_ref[pl.ds(at, width), :])
        at += width
    hidden = hidden.astype(jnp.bfloat16).astype(jnp.float32)
    normed_ref[...] = layer_norm(hidden).astype(jnp.bfloat16)


def project_kernel(piece_count, offset_ref, normed_ref, *refs):
    pieces, (proj_ref, weight_ref) = refs[:piece_count], refs[piece_count:]

    @pl.when(pl.program_id(0) == 0)
    def _():
        assemble(offset_ref, pieces, weight_ref)

    proj_ref[...] = fold_product(normed_ref[...], weight_ref[...]).astype(jnp.bfloat16)


def group_kernel(
    query_ref,
    code_ref,
    key_code_ref,
    key_own_ref,
    key_other_ref,
    value_own_ref,
    value_other_ref,
    mixed_ref,
):
    width = mixed_ref.shape[1]
    half = key_own_ref.shape[0]
    codes = code_ref[...]
    masks = [codes == key_code_ref[:, pl.ds(at, half)] for at in (0, half)]
    for head in range(width // HD):
        part = pl.ds(head * HD, HD)
        query = query_ref[:, part]
        scores = [
            jnp.where(
                mask,
                lax.dot_general(
                    query, key[:, part], (((1,), (1,)), ((), ())), preferred_element_type=jnp.float32
                ),
                mask_floor,
            )
            for key, mask in zip((key_own_ref, key_other_ref), masks)
        ]
        top = functools.reduce(
            jnp.maximum, [jnp.max(s, axis=-1, keepdims=True) for s in scores]
        )
        total = 0.0
        mixed = 0.0
        for s, value in zip(scores, (value_own_ref, value_other_ref)):
            weights = jnp.exp2((s - top) * exp2_scale)
            total += jnp.sum(weights, axis=-1, keepdims=True)
            mixed += fold_product(weights.astype(jnp.bfloat16), value[:, part])
        mixed_ref[:, part] = jnp.where(codes >= 0, mixed / total, 0.0).astype(jnp.bfloat16)


def swap_perm(size, mask):
    return [(i, i ^ mask) for i in range(size)]


def after(value, earlier):
    return lax.optimization_barrier((value, earlier))[0]


def sample_body(patches, kept_index, kept_count, embed_weight, local_qkv, local_out, global_qkv):
    lat_windows, lon_windows, window_tokens, pin = patches.shape[1:]
    windows = lat_windows * lon_windows
    kept_most = kept_index.shape[3]
    rows = windows * kept_most
    inner = HEADS * HD
    half_inner = inner // 2
    lon_size = lax.axis_size("lon")
    batch_size = lax.axis_size("batch")
    core = lax.axis_index("lat")
    chip = lax.axis_index("batch")
    z = lax.axis_index("lon")

    index_rows = kept_index.reshape(windows, kept_most)
    kept_mask = lax.broadcasted_iota(jnp.int32, (windows, kept_most), 1) < kept_count.reshape(
        windows, 1
    )
    codes = jnp.where(kept_mask, index_rows, -1).reshape(rows)
    picked = jnp.take_along_axis(
        patches.reshape(windows, window_tokens, pin), index_rows[:, :, None], axis=1
    ).reshape(rows, pin)

    ring = [(i, (i + 1) % lon_size) for i in range(lon_size)]
    picked_parts = [picked]
    for _ in range(lon_size - 1):
        picked_parts.append(lax.ppermute(picked_parts[-1], "lon", ring))
    picked_all = jnp.concatenate(picked_parts, axis=0)
    all_rows = picked_all.shape[0]
    all_codes = lax.all_gather(codes, ("lat", "lon"), axis=0, tiled=False).reshape(
        2, lon_size, rows
    )
    order = (z - jnp.arange(lon_size, dtype=jnp.int32)) % lon_size
    all_codes = all_codes[:, order].reshape(2, all_rows)
    own_codes = all_codes[core]
    other_codes = all_codes[1 - core]

    diagonal = []
    for b in range(batch_size):
        diagonal += [(2 * b, 2 * (b ^ 1)), (2 * b + 1, 2 * (b ^ 2) + 1)]

    def fetch(part):
        along_x = lax.ppermute(part, "batch", swap_perm(batch_size, 1))
        along_y = lax.ppermute(part, "batch", swap_perm(batch_size, 2))
        forwarded = jnp.where(core == 0, along_y, along_x)
        across = lax.ppermute(forwarded, ("batch", "lat"), diagonal)
        return along_x, along_y, across

    def other_core(value):
        return lax.ppermute(value, "lat", swap_perm(2, 1))

    def shared(shard, got):
        high = shard.shape[0]
        part = high // 2
        pieces, offsets = [shard], [chip * high]
        for which, value in zip((1, 2, 3), got):
            pieces += [value, other_core(value)]
            base = (chip ^ which) * high
            offsets += [base + core * part, base + (1 - core) * part]
        return pieces, jnp.stack(offsets).astype(jnp.int32)

    def single(shard, got):
        high = shard.shape[0]
        offsets = [(chip ^ which) * high for which in range(4)]
        return [shard, *got], jnp.stack(offsets).astype(jnp.int32)

    def own_rows(shard):
        part = shard.shape[0] // 2
        return lax.dynamic_slice_in_dim(shard, core * part, part, axis=0)

    def head_columns(weight, group):
        return jnp.concatenate(
            [
                weight[:, which * inner + group * half_inner : which * inner + (group + 1) * half_inner]
                for which in range(3)
            ],
            axis=1,
        )

    local_shards = [head_columns(local_qkv, group) for group in range(2)]
    global_shards = [
        lax.dynamic_slice_in_dim(
            global_qkv, which * inner + core * half_inner, half_inner, axis=1
        )
        for which in range(3)
    ]
    sent = [own_rows(embed_weight)]
    sent += [own_rows(s) for s in local_shards]
    sent += [own_rows(local_out)]
    sent += [global_shards[1], global_shards[0], global_shards[2]]
    fetched = []
    for at, part in enumerate(sent):
        if at >= 2:
            part = after(part, fetched[at - 2][:2])
        fetched.append(fetch(part))

    block = all_rows // 3 if all_rows % 3 == 0 else all_rows
    steps = all_rows // block
    weight_scratch = lambda high, wide: pltpu.VMEM((high, wide), jnp.bfloat16)
    full = pin

    pieces, offsets = shared(embed_weight, fetched[0])
    width = embed_weight.shape[1]
    embedded, normed = call(
        functools.partial(embed_kernel, len(pieces)),
        steps,
        offsets,
        [(picked_all, block)],
        [],
        pieces,
        [((all_rows, width), block)] * 2,
        [weight_scratch(full, width)],
        2 * all_rows * full * width,
        "embed",
    )

    at_once = 4 * kept_most if block % (4 * kept_most) == 0 else kept_most
    window_codes = jnp.where(
        own_codes >= 0, (jnp.arange(all_rows, dtype=jnp.int32) // kept_most) % (at_once // kept_most), -1
    ).reshape(steps, 1, block)
    code_spec = [window_codes]
    mixes = []
    for group in range(2):
        pieces, offsets = shared(local_shards[group], fetched[1 + group])
        specs = [pl.BlockSpec((block, width), lambda i, _: (i, 0))]
        specs += [pl.BlockSpec((1, 1, block), lambda i, _: (i, 0, 0))]
        specs += [whole_block(a) for a in pieces]
        flops = 2 * all_rows * width * 3 * half_inner
        mixes.append(
            pl.pallas_call(
                functools.partial(window_kernel, len(pieces), kept_most, at_once),
                grid_spec=pltpu.PrefetchScalarGridSpec(
                    num_scalar_prefetch=1,
                    grid=(steps,),
                    in_specs=specs,
                    out_specs=pl.BlockSpec((block, half_inner), lambda i, _: (i, 0)),
                    scratch_shapes=[
                        weight_scratch(width, 3 * half_inner),
                        weight_scratch(block, 3 * half_inner),
                    ],
                ),
                out_shape=jax.ShapeDtypeStruct((all_rows, half_inner), jnp.bfloat16),
                compiler_params=pltpu.CompilerParams(vmem_limit_bytes=vmem_limit),
                cost_estimate=pl.CostEstimate(
                    flops=flops, bytes_accessed=16 * 1024 * 1024, transcendentals=0
                ),
                name="windows",
            )(offsets, normed, window_codes, *pieces)
        )

    pieces, offsets = shared(local_out, fetched[3])
    (normed_own,) = call(
        functools.partial(out_kernel, len(pieces), len(mixes)),
        steps,
        offsets,
        [(embedded, block)] + [(m, block) for m in mixes],
        [],
        pieces,
        [((all_rows, width), block)],
        [weight_scratch(inner, width)],
        2 * all_rows * inner * width,
        "local_out",
    )
    normed_other = other_core(normed_own)

    def project(which, got, values, name):
        pieces, offsets = single(global_shards[which], got)
        many = values.shape[0]
        size = block if many % block == 0 else many
        (result,) = call(
            functools.partial(project_kernel, len(pieces)),
            many // size,
            offsets,
            [(values, size)],
            [],
            pieces,
            [((many, half_inner), size)],
            [weight_scratch(width, half_inner)],
            2 * many * width * half_inner,
            name,
        )
        return result

    keys = [project(1, fetched[4], v, "keys") for v in (normed_own, normed_other)]
    queries = project(
        0, fetched[5], jnp.concatenate([normed_own[:rows], normed_other[:rows]], axis=0), "queries"
    )
    values = [project(2, fetched[6], v, "values") for v in (normed_own, normed_other)]

    key_codes = jnp.concatenate([own_codes, other_codes]).reshape(1, 2 * all_rows)
    query_codes = jnp.concatenate([own_codes[:rows], other_codes[:rows]]).reshape(2 * rows, 1)
    query_codes = jnp.where(query_codes >= 0, query_codes, -2)
    query_block = 256 if (2 * rows) % 256 == 0 else 2 * rows
    resident = [key_codes, *keys, *values]
    mixed = pl.pallas_call(
        group_kernel,
        grid=(2 * rows // query_block,),
        in_specs=[
            pl.BlockSpec((query_block, half_inner), lambda i: (i, 0)),
            pl.BlockSpec((query_block, 1), lambda i: (i, 0)),
            *[whole_block(a) for a in resident],
        ],
        out_specs=pl.BlockSpec((query_block, half_inner), lambda i: (i, 0)),
        out_shape=jax.ShapeDtypeStruct((2 * rows, half_inner), jnp.bfloat16),
        compiler_params=pltpu.CompilerParams(vmem_limit_bytes=vmem_limit),
        cost_estimate=pl.CostEstimate(
            flops=4 * 2 * rows * 2 * all_rows * half_inner,
            bytes_accessed=16 * 1024 * 1024,
            transcendentals=0,
        ),
        name="groups",
    )(queries, query_codes, *resident)

    mine, theirs = mixed[:rows], other_core(mixed[rows:])
    result = jnp.where(
        core == 0,
        jnp.concatenate([mine, theirs], axis=1),
        jnp.concatenate([theirs, mine], axis=1),
    )
    return result.reshape(1, lat_windows, lon_windows, kept_most, inner)


def body(patches, kept_index, *weights):
    rows = patches.shape[1] * patches.shape[2] * kept_index.shape[3]
    sample_rows = rows * lax.axis_size("lat") * lax.axis_size("lon")
    fits = sample_rows * HEADS * HD * 2 <= vmem_limit // 4
    if lax.axis_size("batch") == 4 and lax.axis_size("lat") == 2 and fits:
        return sample_body(patches, kept_index, *weights)
    return owner_body(patches, kept_index, *weights)


def solution(mesh):
    return jax.shard_map(
        body,
        mesh=mesh,
        in_specs=(
            P("batch", "lat", "lon", None, None),
            P("batch", "lat", "lon", None),
            P("batch", "lat", "lon"),
            P("batch", None),
            P("batch", None),
            P("batch", None),
            P("batch", None),
        ),
        out_specs=P("batch", "lat", "lon", None, None),
        check_vma=False,
    )
```

```python
import functools

import jax
import jax.numpy as jnp
from jax import lax
from jax.experimental import pallas as pl
from jax.experimental.pallas import tpu as pltpu
from jax.sharding import PartitionSpec as P

HEADS = 8
HD = 160


norm_eps = 1e-05
mask_floor = -1e30
vmem_limit = 56 * 1024 * 1024
exp2_scale = HD ** (-0.5) * 1.4426950408889634


def layer_norm(values):
    centre = values - jnp.mean(values, axis=-1, keepdims=True)
    spread = jnp.mean(centre * centre, axis=-1, keepdims=True)
    return centre * lax.rsqrt(spread + norm_eps)


def fold_product(left_rows, shard_rows):
    return jnp.dot(left_rows, shard_rows, preferred_element_type=jnp.float32)


def attend(query_rows, key_rows, value_rows, keep_mask):
    scores = jnp.einsum(
        "bnhd,bmhd->bhnm", query_rows, key_rows, preferred_element_type=jnp.float32
    ) * HD ** (-0.5)
    scores = jnp.where(keep_mask[:, None, None, :], scores, mask_floor)
    scores = scores - jnp.max(scores, axis=-1, keepdims=True)
    weights = jnp.exp(scores)
    probabilities = (weights / jnp.sum(weights, axis=-1, keepdims=True)).astype(jnp.bfloat16)
    blended = jnp.einsum(
        "bhnm,bmhd->bnhd", probabilities, value_rows, preferred_element_type=jnp.float32
    )
    return blended.astype(jnp.bfloat16).reshape(
        query_rows.shape[0], query_rows.shape[1], HEADS * HD
    )


def owner_work(received, flag_rows, whole_global):
    item_count = received.shape[0]
    slot_values = received.reshape(item_count, -1, received.shape[-1])
    projected = jnp.dot(
        slot_values.reshape(-1, slot_values.shape[-1]),
        whole_global,
        preferred_element_type=jnp.float32,
    )
    slot_values = projected.astype(jnp.bfloat16).reshape(item_count, -1, 3 * HEADS * HD)
    heads_split = slot_values.reshape(item_count, slot_values.shape[1], 3, HEADS, HD)
    keep_mask = flag_rows.reshape(item_count, -1) > 0
    return attend(heads_split[:, :, 0], heads_split[:, :, 1], heads_split[:, :, 2], keep_mask)


def owner_body(patches, kept_index, kept_count, embed_weight, local_qkv, local_out, global_qkv):
    lat_windows = patches.shape[1]
    lon_windows = patches.shape[2]
    windows = lat_windows * lon_windows
    window_tokens = patches.shape[3]
    kept_most = kept_index.shape[3]
    row_count = windows * kept_most
    inner_width = HEADS * HD
    patch_rows = patches.reshape(windows, window_tokens, patches.shape[4])
    index_rows = kept_index.reshape(windows, kept_most)
    kept_mask = lax.broadcasted_iota(jnp.int32, (windows, kept_most), 1) < kept_count.reshape(
        windows, 1
    )
    picked = jnp.take_along_axis(patch_rows, index_rows[:, :, None], axis=1).reshape(row_count, -1)
    embedded = fold_product(
        picked, lax.all_gather(embed_weight, "batch", axis=0, tiled=True)
    ).astype(jnp.bfloat16)
    normed = layer_norm(embedded.astype(jnp.float32)).astype(jnp.bfloat16)
    local_proj = fold_product(
        normed, lax.all_gather(local_qkv, "batch", axis=0, tiled=True)
    ).astype(jnp.bfloat16)
    local_split = local_proj.reshape(windows, kept_most, 3, HEADS, HD)
    local_mix = attend(
        local_split[:, :, 0], local_split[:, :, 1], local_split[:, :, 2], kept_mask
    ).reshape(row_count, inner_width)
    back_sum = fold_product(local_mix, lax.all_gather(local_out, "batch", axis=0, tiled=True))
    hidden = (embedded.astype(jnp.float32) + back_sum).astype(jnp.bfloat16)
    normed_global = layer_norm(hidden.astype(jnp.float32)).astype(jnp.bfloat16)
    whole_global = lax.all_gather(global_qkv, "batch", axis=0, tiled=True)
    sent_width = normed_global.shape[1]
    window_ids = lax.broadcasted_iota(jnp.int32, (windows, kept_most), 0)
    slot_rows = (
        jnp.zeros((window_tokens, windows, sent_width), jnp.bfloat16)
        .at[index_rows, window_ids]
        .set(normed_global.reshape(windows, kept_most, sent_width))
    )
    flag_slots = (
        jnp.zeros((window_tokens, windows), jnp.bfloat16)
        .at[index_rows, window_ids]
        .set(kept_mask.astype(jnp.bfloat16))
    )
    owners = lax.axis_size("lat") * lax.axis_size("lon")
    owned_count = window_tokens // owners
    blended = owner_work(
        lax.all_to_all(
            slot_rows.reshape(owned_count, owners, windows, sent_width),
            ("lat", "lon"),
            split_axis=1,
            concat_axis=2,
            tiled=True,
        ),
        lax.all_to_all(
            flag_slots.reshape(owned_count, owners, windows),
            ("lat", "lon"),
            split_axis=1,
            concat_axis=2,
            tiled=True,
        ),
        whole_global,
    )
    shaped = blended.reshape(blended.shape[0], 1, -1, inner_width)
    returned = lax.all_to_all(shaped, ("lat", "lon"), split_axis=2, concat_axis=1, tiled=True)
    out_slots = returned.reshape(window_tokens, windows, inner_width)
    gathered = out_slots[index_rows, window_ids]
    result = jnp.where(kept_mask[:, :, None], gathered, jnp.zeros_like(gathered))
    return result.reshape(1, lat_windows, lon_windows, kept_most, inner_width)


def whole_block(array):
    zeros = (0,) * array.ndim
    return pl.BlockSpec(array.shape, lambda *_: zeros)


def assemble(offset_ref, piece_refs, weight_ref):
    for at, piece in enumerate(piece_refs):
        start = pl.multiple_of(offset_ref[at], 16)
        weight_ref[pl.ds(start, piece.shape[0]), :] = piece[...]


def call(kernel, steps, offsets, row_inputs, whole_inputs, pieces, outs, scratch, flops, name):
    specs = [pl.BlockSpec((rows, a.shape[1]), lambda i, _: (i, 0)) for a, rows in row_inputs]
    specs += [whole_block(a) for a in whole_inputs]
    specs += [whole_block(a) for a in pieces]
    arrays = [a for a, _ in row_inputs] + list(whole_inputs) + list(pieces)
    out_shapes = [jax.ShapeDtypeStruct(s, jnp.bfloat16) for s, _ in outs]
    moved = sum(a.size * a.dtype.itemsize for a in arrays) + sum(2 * s.size for s in out_shapes)
    return pl.pallas_call(
        kernel,
        grid_spec=pltpu.PrefetchScalarGridSpec(
            num_scalar_prefetch=1,
            grid=(steps,),
            in_specs=specs,
            out_specs=[pl.BlockSpec((rows, s[1]), lambda i, _: (i, 0)) for s, rows in outs],
            scratch_shapes=scratch,
        ),
        out_shape=out_shapes,
        compiler_params=pltpu.CompilerParams(vmem_limit_bytes=vmem_limit),
        cost_estimate=pl.CostEstimate(flops=flops, bytes_accessed=moved, transcendentals=0),
        name=name,
    )(offsets, *arrays)


def embed_kernel(piece_count, offset_ref, picked_ref, *refs):
    pieces, (embedded_ref, normed_ref, weight_ref) = refs[:piece_count], refs[piece_count:]

    @pl.when(pl.program_id(0) == 0)
    def _():
        assemble(offset_ref, pieces, weight_ref)

    embedded = fold_product(picked_ref[...], weight_ref[...]).astype(jnp.bfloat16)
    embedded_ref[...] = embedded
    normed_ref[...] = layer_norm(embedded.astype(jnp.float32)).astype(jnp.bfloat16)


def masked_mix(query, key, value, mask):
    scores = lax.dot_general(
        query, key, (((1,), (1,)), ((), ())), preferred_element_type=jnp.float32
    )
    scores = jnp.where(mask, scores, mask_floor)
    top = jnp.max(scores, axis=-1, keepdims=True)
    weights = jnp.exp2((scores - top) * exp2_scale)
    total = jnp.sum(weights, axis=-1, keepdims=True)
    mixed = fold_product(weights.astype(jnp.bfloat16), value)
    return mixed / total


def window_kernel(piece_count, kept_most, rows_at_once, offset_ref, normed_ref, code_ref, *refs):
    pieces, (mix_ref, weight_ref, proj_ref) = refs[:piece_count], refs[piece_count:]

    @pl.when(pl.program_id(0) == 0)
    def _():
        assemble(offset_ref, pieces, weight_ref)

    proj_ref[...] = fold_product(normed_ref[...], weight_ref[...]).astype(jnp.bfloat16)
    width = mix_ref.shape[1]
    rows = normed_ref.shape[0]
    own_window = lax.broadcasted_iota(jnp.int32, (rows_at_once, 1), 0) // kept_most
    for start in range(0, rows, rows_at_once):
        part = pl.ds(start, rows_at_once)
        mask = own_window == code_ref[0, :, part]
        for head in range(width // HD):
            query, key, value = (
                proj_ref[part, pl.ds(which * width + head * HD, HD)] for which in range(3)
            )
            mix_ref[part, pl.ds(head * HD, HD)] = masked_mix(query, key, value, mask).astype(
                jnp.bfloat16
            )


def out_kernel(piece_count, mix_count, offset_ref, embedded_ref, *refs):
    mixes, refs = refs[:mix_count], refs[mix_count:]
    pieces, (normed_ref, weight_ref) = refs[:piece_count], refs[piece_count:]

    @pl.when(pl.program_id(0) == 0)
    def _():
        assemble(offset_ref, pieces, weight_ref)

    hidden = embedded_ref[...].astype(jnp.float32)
    at = 0
    for mix in mixes:
        width = mix.shape[1]
        hidden += fold_product(mix[...], weight_ref[pl.ds(at, width), :])
        at += width
    hidden = hidden.astype(jnp.bfloat16).astype(jnp.float32)
    normed_ref[...] = layer_norm(hidden).astype(jnp.bfloat16)


def project_kernel(piece_count, offset_ref, normed_ref, *refs):
    pieces, (proj_ref, weight_ref) = refs[:piece_count], refs[piece_count:]

    @pl.when(pl.program_id(0) == 0)
    def _():
        assemble(offset_ref, pieces, weight_ref)

    proj_ref[...] = fold_product(normed_ref[...], weight_ref[...]).astype(jnp.bfloat16)


def group_kernel(
    query_ref,
    code_ref,
    key_code_ref,
    key_own_ref,
    key_other_ref,
    value_own_ref,
    value_other_ref,
    mixed_ref,
):
    width = mixed_ref.shape[1]
    half = key_own_ref.shape[0]
    codes = code_ref[...]
    masks = [codes == key_code_ref[:, pl.ds(at, half)] for at in (0, half)]
    for head in range(width // HD):
        part = pl.ds(head * HD, HD)
        query = query_ref[:, part]
        scores = [
            jnp.where(
                mask,
                lax.dot_general(
                    query, key[:, part], (((1,), (1,)), ((), ())), preferred_element_type=jnp.float32
                ),
                mask_floor,
            )
            for key, mask in zip((key_own_ref, key_other_ref), masks)
        ]
        top = functools.reduce(
            jnp.maximum, [jnp.max(s, axis=-1, keepdims=True) for s in scores]
        )
        total = 0.0
        mixed = 0.0
        for s, value in zip(scores, (value_own_ref, value_other_ref)):
            weights = jnp.exp2((s - top) * exp2_scale)
            total += jnp.sum(weights, axis=-1, keepdims=True)
            mixed += fold_product(weights.astype(jnp.bfloat16), value[:, part])
        mixed_ref[:, part] = jnp.where(codes >= 0, mixed / total, 0.0).astype(jnp.bfloat16)


def swap_perm(size, mask):
    return [(i, i ^ mask) for i in range(size)]


def after(value, earlier):
    return lax.optimization_barrier((value, earlier))[0]


def sample_body(patches, kept_index, kept_count, embed_weight, local_qkv, local_out, global_qkv):
    lat_windows, lon_windows, window_tokens, pin = patches.shape[1:]
    windows = lat_windows * lon_windows
    kept_most = kept_index.shape[3]
    rows = windows * kept_most
    inner = HEADS * HD
    half_inner = inner // 2
    lon_size = lax.axis_size("lon")
    batch_size = lax.axis_size("batch")
    core = lax.axis_index("lat")
    chip = lax.axis_index("batch")

    index_rows = kept_index.reshape(windows, kept_most)
    kept_mask = lax.broadcasted_iota(jnp.int32, (windows, kept_most), 1) < kept_count.reshape(
        windows, 1
    )
    codes = jnp.where(kept_mask, index_rows, -1).reshape(rows)
    picked = jnp.take_along_axis(
        patches.reshape(windows, window_tokens, pin), index_rows[:, :, None], axis=1
    ).reshape(rows, pin)

    ring = [(i, (i + 1) % lon_size) for i in range(lon_size)]
    code_rows = -(-rows // pin)
    code_tile = -(-code_rows // 16) * 16
    code_part = jnp.pad(codes, (0, code_tile * pin - rows)).reshape(code_tile, pin)
    picked_parts = [jnp.concatenate([picked, code_part.astype(jnp.bfloat16)], axis=0)]
    for _ in range(lon_size - 1):
        picked_parts.append(lax.ppermute(picked_parts[-1], "lon", ring))
    picked_all = jnp.concatenate([part[:rows] for part in picked_parts], axis=0)
    all_rows = picked_all.shape[0]
    own_codes = jnp.concatenate(
        [part[rows : rows + code_rows].reshape(-1)[:rows] for part in picked_parts]
    ).astype(jnp.int32)
    other_codes = lax.ppermute(own_codes, "lat", swap_perm(2, 1))

    diagonal = []
    for b in range(batch_size):
        diagonal += [(2 * b, 2 * (b ^ 1)), (2 * b + 1, 2 * (b ^ 2) + 1)]

    def fetch(part):
        along_x = lax.ppermute(part, "batch", swap_perm(batch_size, 1))
        along_y = lax.ppermute(part, "batch", swap_perm(batch_size, 2))
        forwarded = jnp.where(core == 0, along_y, along_x)
        across = lax.ppermute(forwarded, ("batch", "lat"), diagonal)
        return along_x, along_y, across

    def other_core(value):
        return lax.ppermute(value, "lat", swap_perm(2, 1))

    def shared(shard, got):
        high = shard.shape[0]
        part = high // 2
        pieces, offsets = [shard], [chip * high]
        for which, value in zip((1, 2, 3), got):
            pieces += [value, other_core(value)]
            base = (chip ^ which) * high
            offsets += [base + core * part, base + (1 - core) * part]
        return pieces, jnp.stack(offsets).astype(jnp.int32)

    def single(shard, got):
        high = shard.shape[0]
        offsets = [(chip ^ which) * high for which in range(4)]
        return [shard, *got], jnp.stack(offsets).astype(jnp.int32)

    def own_rows(shard):
        part = shard.shape[0] // 2
        return lax.dynamic_slice_in_dim(shard, core * part, part, axis=0)

    def head_columns(weight, group):
        return jnp.concatenate(
            [
                weight[:, which * inner + group * half_inner : which * inner + (group + 1) * half_inner]
                for which in range(3)
            ],
            axis=1,
        )

    local_shards = [head_columns(local_qkv, group) for group in range(2)]
    global_shards = [
        lax.dynamic_slice_in_dim(
            global_qkv, which * inner + core * half_inner, half_inner, axis=1
        )
        for which in range(3)
    ]
    sent = [own_rows(embed_weight)]
    sent += [own_rows(s) for s in local_shards]
    sent += [own_rows(local_out)]
    sent += [global_shards[1], global_shards[0], global_shards[2]]
    fetched = []
    for at, part in enumerate(sent):
        if at >= 2:
            part = after(part, fetched[at - 2][:2])
        fetched.append(fetch(part))

    block = all_rows // 3 if all_rows % 3 == 0 else all_rows
    steps = all_rows // block
    weight_scratch = lambda high, wide: pltpu.VMEM((high, wide), jnp.bfloat16)
    full = pin

    pieces, offsets = shared(embed_weight, fetched[0])
    width = embed_weight.shape[1]
    embedded, normed = call(
        functools.partial(embed_kernel, len(pieces)),
        steps,
        offsets,
        [(picked_all, block)],
        [],
        pieces,
        [((all_rows, width), block)] * 2,
        [weight_scratch(full, width)],
        2 * all_rows * full * width,
        "embed",
    )

    at_once = 4 * kept_most if block % (4 * kept_most) == 0 else kept_most
    window_codes = jnp.where(
        own_codes >= 0, (jnp.arange(all_rows, dtype=jnp.int32) // kept_most) % (at_once // kept_most), -1
    ).reshape(steps, 1, block)
    code_spec = [window_codes]
    mixes = []
    for group in range(2):
        pieces, offsets = shared(local_shards[group], fetched[1 + group])
        if group == 1:
            pieces = after(pieces, fetched[3][:2])
        specs = [pl.BlockSpec((block, width), lambda i, _: (i, 0))]
        specs += [pl.BlockSpec((1, 1, block), lambda i, _: (i, 0, 0))]
        specs += [whole_block(a) for a in pieces]
        flops = 2 * all_rows * width * 3 * half_inner
        mixes.append(
            pl.pallas_call(
                functools.partial(window_kernel, len(pieces), kept_most, at_once),
                grid_spec=pltpu.PrefetchScalarGridSpec(
                    num_scalar_prefetch=1,
                    grid=(steps,),
                    in_specs=specs,
                    out_specs=pl.BlockSpec((block, half_inner), lambda i, _: (i, 0)),
                    scratch_shapes=[
                        weight_scratch(width, 3 * half_inner),
                        weight_scratch(block, 3 * half_inner),
                    ],
                ),
                out_shape=jax.ShapeDtypeStruct((all_rows, half_inner), jnp.bfloat16),
                compiler_params=pltpu.CompilerParams(vmem_limit_bytes=vmem_limit),
                cost_estimate=pl.CostEstimate(
                    flops=flops, bytes_accessed=16 * 1024 * 1024, transcendentals=0
                ),
                name="windows",
            )(offsets, normed, window_codes, *pieces)
        )

    pieces, offsets = shared(local_out, fetched[3])
    pieces = after(pieces, (fetched[4][:2], fetched[5][:2]))
    (normed_own,) = call(
        functools.partial(out_kernel, len(pieces), len(mixes)),
        steps,
        offsets,
        [(embedded, block)] + [(m, block) for m in mixes],
        [],
        pieces,
        [((all_rows, width), block)],
        [weight_scratch(inner, width)],
        2 * all_rows * inner * width,
        "local_out",
    )
    normed_other = other_core(normed_own)

    def project(which, got, values, name):
        pieces, offsets = single(global_shards[which], got)
        many = values.shape[0]
        size = block if many % block == 0 else many
        (result,) = call(
            functools.partial(project_kernel, len(pieces)),
            many // size,
            offsets,
            [(values, size)],
            [],
            pieces,
            [((many, half_inner), size)],
            [weight_scratch(width, half_inner)],
            2 * many * width * half_inner,
            name,
        )
        return result

    keys = [project(1, fetched[4], v, "keys") for v in (normed_own, normed_other)]
    queries = project(
        0, fetched[5], jnp.concatenate([normed_own[:rows], normed_other[:rows]], axis=0), "queries"
    )
    values = [project(2, fetched[6], v, "values") for v in (normed_own, normed_other)]

    key_codes = jnp.concatenate([own_codes, other_codes]).reshape(1, 2 * all_rows)
    query_codes = jnp.concatenate([own_codes[:rows], other_codes[:rows]]).reshape(2 * rows, 1)
    query_codes = jnp.where(query_codes >= 0, query_codes, -2)
    query_block = 256 if (2 * rows) % 256 == 0 else 2 * rows
    resident = [key_codes, *keys, *values]
    mixed = pl.pallas_call(
        group_kernel,
        grid=(2 * rows // query_block,),
        in_specs=[
            pl.BlockSpec((query_block, half_inner), lambda i: (i, 0)),
            pl.BlockSpec((query_block, 1), lambda i: (i, 0)),
            *[whole_block(a) for a in resident],
        ],
        out_specs=pl.BlockSpec((query_block, half_inner), lambda i: (i, 0)),
        out_shape=jax.ShapeDtypeStruct((2 * rows, half_inner), jnp.bfloat16),
        compiler_params=pltpu.CompilerParams(vmem_limit_bytes=vmem_limit),
        cost_estimate=pl.CostEstimate(
            flops=4 * 2 * rows * 2 * all_rows * half_inner,
            bytes_accessed=16 * 1024 * 1024,
            transcendentals=0,
        ),
        name="groups",
    )(queries, query_codes, *resident)

    mine, theirs = mixed[:rows], other_core(mixed[rows:])
    result = jnp.where(
        core == 0,
        jnp.concatenate([mine, theirs], axis=1),
        jnp.concatenate([theirs, mine], axis=1),
    )
    return result.reshape(1, lat_windows, lon_windows, kept_most, inner)


def body(patches, kept_index, *weights):
    rows = patches.shape[1] * patches.shape[2] * kept_index.shape[3]
    sample_rows = rows * lax.axis_size("lat") * lax.axis_size("lon")
    fits = patches.shape[3] <= 256 and sample_rows * HEADS * HD * 2 <= vmem_limit // 4
    if lax.axis_size("batch") == 4 and lax.axis_size("lat") == 2 and fits:
        return sample_body(patches, kept_index, *weights)
    return owner_body(patches, kept_index, *weights)


def solution(mesh):
    return jax.shard_map(
        body,
        mesh=mesh,
        in_specs=(
            P("batch", "lat", "lon", None, None),
            P("batch", "lat", "lon", None),
            P("batch", "lat", "lon"),
            P("batch", None),
            P("batch", None),
            P("batch", None),
            P("batch", None),
        ),
        out_specs=P("batch", "lat", "lon", None, None),
        check_vma=False,
    )
```

```python
import functools

import jax
import jax.numpy as jnp
from jax import lax
from jax.experimental import pallas as pl
from jax.experimental.pallas import tpu as pltpu
from jax.sharding import PartitionSpec as P

HEADS = 8
HD = 160


norm_eps = 1e-05
mask_floor = -1e30
vmem_limit = 56 * 1024 * 1024
exp2_scale = HD ** (-0.5) * 1.4426950408889634


def layer_norm(values):
    centre = values - jnp.mean(values, axis=-1, keepdims=True)
    spread = jnp.mean(centre * centre, axis=-1, keepdims=True)
    return centre * lax.rsqrt(spread + norm_eps)


def fold_product(left_rows, shard_rows):
    return jnp.dot(left_rows, shard_rows, preferred_element_type=jnp.float32)


def attend(query_rows, key_rows, value_rows, keep_mask):
    scores = jnp.einsum(
        "bnhd,bmhd->bhnm", query_rows, key_rows, preferred_element_type=jnp.float32
    ) * HD ** (-0.5)
    scores = jnp.where(keep_mask[:, None, None, :], scores, mask_floor)
    scores = scores - jnp.max(scores, axis=-1, keepdims=True)
    weights = jnp.exp(scores)
    probabilities = (weights / jnp.sum(weights, axis=-1, keepdims=True)).astype(jnp.bfloat16)
    blended = jnp.einsum(
        "bhnm,bmhd->bnhd", probabilities, value_rows, preferred_element_type=jnp.float32
    )
    return blended.astype(jnp.bfloat16).reshape(
        query_rows.shape[0], query_rows.shape[1], HEADS * HD
    )


def owner_work(received, flag_rows, whole_global):
    item_count = received.shape[0]
    slot_values = received.reshape(item_count, -1, received.shape[-1])
    projected = jnp.dot(
        slot_values.reshape(-1, slot_values.shape[-1]),
        whole_global,
        preferred_element_type=jnp.float32,
    )
    slot_values = projected.astype(jnp.bfloat16).reshape(item_count, -1, 3 * HEADS * HD)
    heads_split = slot_values.reshape(item_count, slot_values.shape[1], 3, HEADS, HD)
    keep_mask = flag_rows.reshape(item_count, -1) > 0
    return attend(heads_split[:, :, 0], heads_split[:, :, 1], heads_split[:, :, 2], keep_mask)


def owner_body(patches, kept_index, kept_count, embed_weight, local_qkv, local_out, global_qkv):
    lat_windows = patches.shape[1]
    lon_windows = patches.shape[2]
    windows = lat_windows * lon_windows
    window_tokens = patches.shape[3]
    kept_most = kept_index.shape[3]
    row_count = windows * kept_most
    inner_width = HEADS * HD
    patch_rows = patches.reshape(windows, window_tokens, patches.shape[4])
    index_rows = kept_index.reshape(windows, kept_most)
    kept_mask = lax.broadcasted_iota(jnp.int32, (windows, kept_most), 1) < kept_count.reshape(
        windows, 1
    )
    picked = jnp.take_along_axis(patch_rows, index_rows[:, :, None], axis=1).reshape(row_count, -1)
    embedded = fold_product(
        picked, lax.all_gather(embed_weight, "batch", axis=0, tiled=True)
    ).astype(jnp.bfloat16)
    normed = layer_norm(embedded.astype(jnp.float32)).astype(jnp.bfloat16)
    local_proj = fold_product(
        normed, lax.all_gather(local_qkv, "batch", axis=0, tiled=True)
    ).astype(jnp.bfloat16)
    local_split = local_proj.reshape(windows, kept_most, 3, HEADS, HD)
    local_mix = attend(
        local_split[:, :, 0], local_split[:, :, 1], local_split[:, :, 2], kept_mask
    ).reshape(row_count, inner_width)
    back_sum = fold_product(local_mix, lax.all_gather(local_out, "batch", axis=0, tiled=True))
    hidden = (embedded.astype(jnp.float32) + back_sum).astype(jnp.bfloat16)
    normed_global = layer_norm(hidden.astype(jnp.float32)).astype(jnp.bfloat16)
    whole_global = lax.all_gather(global_qkv, "batch", axis=0, tiled=True)
    sent_width = normed_global.shape[1]
    window_ids = lax.broadcasted_iota(jnp.int32, (windows, kept_most), 0)
    slot_rows = (
        jnp.zeros((window_tokens, windows, sent_width), jnp.bfloat16)
        .at[index_rows, window_ids]
        .set(normed_global.reshape(windows, kept_most, sent_width))
    )
    flag_slots = (
        jnp.zeros((window_tokens, windows), jnp.bfloat16)
        .at[index_rows, window_ids]
        .set(kept_mask.astype(jnp.bfloat16))
    )
    owners = lax.axis_size("lat") * lax.axis_size("lon")
    owned_count = window_tokens // owners
    blended = owner_work(
        lax.all_to_all(
            slot_rows.reshape(owned_count, owners, windows, sent_width),
            ("lat", "lon"),
            split_axis=1,
            concat_axis=2,
            tiled=True,
        ),
        lax.all_to_all(
            flag_slots.reshape(owned_count, owners, windows),
            ("lat", "lon"),
            split_axis=1,
            concat_axis=2,
            tiled=True,
        ),
        whole_global,
    )
    shaped = blended.reshape(blended.shape[0], 1, -1, inner_width)
    returned = lax.all_to_all(shaped, ("lat", "lon"), split_axis=2, concat_axis=1, tiled=True)
    out_slots = returned.reshape(window_tokens, windows, inner_width)
    gathered = out_slots[index_rows, window_ids]
    result = jnp.where(kept_mask[:, :, None], gathered, jnp.zeros_like(gathered))
    return result.reshape(1, lat_windows, lon_windows, kept_most, inner_width)


MAIN = 128
TAIL = HD - MAIN
GROUP = MAIN // TAIL
WIDE = GROUP * HD


def whole_block(array):
    zeros = (0,) * array.ndim
    return pl.BlockSpec(array.shape, lambda *_: zeros)


def assemble(offset_ref, piece_refs, weight_ref):
    for at, piece in enumerate(piece_refs):
        start = pl.multiple_of(offset_ref[at], 16)
        weight_ref[pl.ds(start, piece.shape[0]), :] = piece[...]


def reorder(source, start, target, at):
    for head in range(GROUP):
        first = start + head * HD
        target[:, pl.ds(at + head * MAIN, MAIN)] = source[:, pl.ds(first, MAIN)]
        target[:, pl.ds(at + GROUP * MAIN + head * TAIL, TAIL)] = source[:, pl.ds(first + MAIN, TAIL)]


def prepare_local_kernel(core_ref, weight_ref, *refs):
    groups = len(refs) // 2
    inner = weight_ref.shape[1] // 3
    for group in range(groups):
        full, half = refs[group], refs[groups + group]
        for which in range(3):
            reorder(weight_ref, which * inner + group * WIDE, full, which * WIDE)
        high = half.shape[0]
        half[...] = full[pl.ds(pl.multiple_of(core_ref[0] * high, 16), high), :]


def prepare_global_kernel(core_ref, query_ref, key_ref, value_ref, first_ref, second_ref):
    reorder(key_ref, 0, first_ref, 0)
    reorder(query_ref, 0, first_ref, WIDE)
    reorder(value_ref, 0, second_ref, 0)


def lane_head():
    return lax.broadcasted_iota(jnp.int32, (1, MAIN), 1) // TAIL


def head_tiles(ref, rows, at, head):
    main = ref[rows, pl.ds(at + head * MAIN, MAIN)]
    tail = ref[rows, pl.ds(at + GROUP * MAIN, MAIN)]
    return main, tail


def head_query(ref, rows, at, head):
    main, tail = head_tiles(ref, rows, at, head)
    return jnp.concatenate([main, jnp.where(lane_head() == head, tail, jnp.zeros_like(tail))], axis=1)


def head_pair(ref, rows, at, head):
    return jnp.concatenate(head_tiles(ref, rows, at, head), axis=1)


def masked_scores(query, key, mask):
    scores = lax.dot_general(
        query, key, (((1,), (1,)), ((), ())), preferred_element_type=jnp.float32
    )
    return jnp.where(mask, scores, mask_floor)


def mix_heads(proj_ref, code_ref, mix_ref, at_once, kept_most):
    rows = proj_ref.shape[0]
    own_window = lax.broadcasted_iota(jnp.int32, (at_once, 1), 0) // kept_most
    for start in range(0, rows, at_once):
        part = pl.ds(start, at_once)
        mask = own_window == code_ref[0, :, part]
        tails = None
        for head in range(GROUP):
            scores = masked_scores(
                head_query(proj_ref, part, 0, head), head_pair(proj_ref, part, WIDE, head), mask
            )
            top = jnp.max(scores, axis=-1, keepdims=True)
            weights = jnp.exp2((scores - top) * exp2_scale)
            total = jnp.sum(weights, axis=-1, keepdims=True)
            mixed = (
                fold_product(
                    weights.astype(jnp.bfloat16), head_pair(proj_ref, part, 2 * WIDE, head)
                )
                / total
            )
            mix_ref[part, pl.ds(head * MAIN, MAIN)] = mixed[:, :MAIN].astype(jnp.bfloat16)
            tail = mixed[:, MAIN:]
            tails = tail if tails is None else jnp.where(lane_head() == head, tail, tails)
        mix_ref[part, pl.ds(GROUP * MAIN, MAIN)] = tails.astype(jnp.bfloat16)


def embed_window_kernel(
    at_once,
    kept_most,
    offset_ref,
    picked_ref,
    code_ref,
    embed_ref,
    *refs,
):
    *pieces, embedded_ref, normed_ref, mix_ref, weight_ref, proj_ref = refs

    @pl.when(pl.program_id(0) == 0)
    def _():
        assemble(offset_ref, pieces, weight_ref)

    embedded = fold_product(picked_ref[...], embed_ref[...]).astype(jnp.bfloat16)
    embedded_ref[...] = embedded
    normed = layer_norm(embedded.astype(jnp.float32)).astype(jnp.bfloat16)
    normed_ref[...] = normed
    proj_ref[...] = fold_product(normed, weight_ref[...]).astype(jnp.bfloat16)
    mix_heads(proj_ref, code_ref, mix_ref, at_once, kept_most)


def window_out_kernel(
    at_once,
    kept_most,
    offset_ref,
    embedded_ref,
    normed_ref,
    mix_ref,
    code_ref,
    out_ref,
    *refs,
):
    *pieces, result_ref, weight_ref, proj_ref, own_mix_ref, row_ref = refs
    inner = out_ref.shape[0]

    @pl.when(pl.program_id(0) == 0)
    def _():
        assemble(offset_ref, pieces, weight_ref)
        for start in range(0, inner, WIDE):
            for head in range(GROUP):
                first = start + head * HD
                row_ref[pl.ds(start + head * MAIN, MAIN), :] = out_ref[pl.ds(first, MAIN), :]
                row_ref[pl.ds(start + GROUP * MAIN + head * TAIL, TAIL), :] = out_ref[
                    pl.ds(first + MAIN, TAIL), :
                ]

    proj_ref[...] = fold_product(normed_ref[...], weight_ref[...]).astype(jnp.bfloat16)
    mix_heads(proj_ref, code_ref, own_mix_ref, at_once, kept_most)
    hidden = embedded_ref[...].astype(jnp.float32)
    hidden += fold_product(mix_ref[...], row_ref[pl.ds(0, WIDE), :])
    hidden += fold_product(own_mix_ref[...], row_ref[pl.ds(WIDE, WIDE), :])
    hidden = hidden.astype(jnp.bfloat16).astype(jnp.float32)
    result_ref[...] = layer_norm(hidden).astype(jnp.bfloat16)


def group_kernel(
    steps,
    rows,
    key_chunk,
    offset_ref,
    own_ref,
    other_ref,
    code_ref,
    key_code_ref,
    *refs,
):
    *pieces, mixed_ref, first_ref, second_ref, key_ref, query_ref, value_ref = refs
    step = pl.program_id(0)
    block = own_ref.shape[0]
    query_block = mixed_ref.shape[0]

    @pl.when(step == 0)
    def _():
        assemble(offset_ref, pieces[:4], first_ref)
        assemble(offset_ref, pieces[4:], second_ref)

    def project(source_ref, at):
        normed = source_ref[...]
        part = pl.ds(pl.multiple_of(step * block, 16), block)
        key_ref[part, :] = fold_product(normed, first_ref[:, pl.ds(0, WIDE)]).astype(jnp.bfloat16)
        value_ref[part, :] = fold_product(normed, second_ref[...]).astype(jnp.bfloat16)

        @pl.when(step == at * steps)
        def _():
            query_ref[pl.ds(at * rows, rows), :] = fold_product(
                source_ref[pl.ds(0, rows), :], first_ref[:, pl.ds(WIDE, WIDE)]
            ).astype(jnp.bfloat16)

    @pl.when(step < steps)
    def _():
        project(own_ref, 0)

    @pl.when((step >= steps) & (step < 2 * steps))
    def _():
        project(other_ref, 1)

    @pl.when(step >= 2 * steps)
    def _():
        part = pl.ds(pl.multiple_of((step - 2 * steps) * query_block, 16), query_block)
        codes = code_ref[...]
        key_parts = [pl.ds(at, key_chunk) for at in range(0, key_ref.shape[0], key_chunk)]
        for head in range(GROUP):
            query = head_query(query_ref, part, 0, head)
            scores = [
                masked_scores(query, head_pair(key_ref, p, 0, head), codes == key_code_ref[:, p])
                for p in key_parts
            ]
            top = functools.reduce(
                jnp.maximum, [jnp.max(s, axis=-1, keepdims=True) for s in scores]
            )
            total = 0.0
            mixed = 0.0
            for p, s in zip(key_parts, scores):
                weights = jnp.exp2((s - top) * exp2_scale)
                total += jnp.sum(weights, axis=-1, keepdims=True)
                mixed += fold_product(
                    weights.astype(jnp.bfloat16), head_pair(value_ref, p, 0, head)
                )
            mixed = jnp.where(codes >= 0, mixed / total, 0.0).astype(jnp.bfloat16)
            mixed_ref[:, pl.ds(head * HD, MAIN)] = mixed[:, :MAIN]
            at = MAIN + head * TAIL
            mixed_ref[:, pl.ds(head * HD + MAIN, TAIL)] = mixed[:, at : at + TAIL]


def swap_perm(size, mask):
    return [(i, i ^ mask) for i in range(size)]


def after(value, earlier):
    return lax.optimization_barrier((value, earlier))[0]


def run(kernel, steps, scalars, specs, arrays, outs, out_specs, scratch, flops, name):
    moved = sum(a.size * a.dtype.itemsize for a in arrays)
    return pl.pallas_call(
        kernel,
        grid_spec=pltpu.PrefetchScalarGridSpec(
            num_scalar_prefetch=1,
            grid=(steps,),
            in_specs=specs,
            out_specs=out_specs,
            scratch_shapes=[pltpu.VMEM(shape, jnp.bfloat16) for shape in scratch],
        ),
        out_shape=[jax.ShapeDtypeStruct(shape, jnp.bfloat16) for shape in outs],
        compiler_params=pltpu.CompilerParams(vmem_limit_bytes=vmem_limit),
        cost_estimate=pl.CostEstimate(flops=flops, bytes_accessed=moved, transcendentals=0),
        name=name,
    )(scalars, *arrays)


def sample_body(patches, kept_index, kept_count, embed_weight, local_qkv, local_out, global_qkv):
    lat_windows, lon_windows, window_tokens, pin = patches.shape[1:]
    windows = lat_windows * lon_windows
    kept_most = kept_index.shape[3]
    rows = windows * kept_most
    inner = HEADS * HD
    width = embed_weight.shape[1]
    lon_size = lax.axis_size("lon")
    batch_size = lax.axis_size("batch")
    core = lax.axis_index("lat")
    chip = lax.axis_index("batch")
    core_scalar = core.reshape(1).astype(jnp.int32)

    def own_rows(shard):
        part = shard.shape[0] // 2
        return lax.dynamic_slice_in_dim(shard, core * part, part, axis=0)

    whole_embed = lax.all_gather(own_rows(embed_weight), ("batch", "lat"), axis=0, tiled=True)
    whole_out = lax.all_gather(own_rows(local_out), ("batch", "lat"), axis=0, tiled=True)

    diagonal = []
    for b in range(batch_size):
        diagonal += [(2 * b, 2 * (b ^ 1)), (2 * b + 1, 2 * (b ^ 2) + 1)]

    def sides(part):
        along_x = lax.ppermute(part, "batch", swap_perm(batch_size, 1))
        along_y = lax.ppermute(part, "batch", swap_perm(batch_size, 2))
        return along_x, along_y

    def across(along_x, along_y):
        forwarded = jnp.where(core == 0, along_y, along_x)
        return lax.ppermute(forwarded, ("batch", "lat"), diagonal)

    def other_core(value):
        return lax.ppermute(value, "lat", swap_perm(2, 1))

    high = local_qkv.shape[0]
    half = high // 2
    *local_full, half_first, half_second = run(
        prepare_local_kernel,
        1,
        core_scalar,
        [whole_block(local_qkv)],
        [local_qkv],
        [(high, 3 * WIDE)] * 2 + [(half, 3 * WIDE)] * 2,
        [pl.BlockSpec((h, 3 * WIDE), lambda *_: (0, 0)) for h in (high, high, half, half)],
        [],
        0,
        "order_local",
    )
    local_sides = [sides(half_first), sides(half_second)]
    global_first, global_second = run(
        prepare_global_kernel,
        1,
        core_scalar,
        [
            pl.BlockSpec((high, WIDE), lambda i, c, which=which: (0, 2 * which + c[0]))
            for which in range(3)
        ],
        [global_qkv] * 3,
        [(high, 2 * WIDE), (high, WIDE)],
        [pl.BlockSpec((high, w), lambda *_: (0, 0)) for w in (2 * WIDE, WIDE)],
        [],
        0,
        "order_global",
    )

    index_rows = kept_index.reshape(windows, kept_most)
    kept_mask = lax.broadcasted_iota(jnp.int32, (windows, kept_most), 1) < kept_count.reshape(
        windows, 1
    )
    codes = jnp.where(kept_mask, index_rows, -1).reshape(rows)
    picked = jnp.take_along_axis(
        patches.reshape(windows, window_tokens, pin), index_rows[:, :, None], axis=1
    ).reshape(rows, pin)

    code_rows = -(-rows // pin)
    code_tile = -(-code_rows // 16) * 16
    code_part = jnp.pad(codes, (0, code_tile * pin - rows)).reshape(code_tile, pin)
    sent = jnp.concatenate([picked, code_part.astype(jnp.bfloat16)], axis=0)
    picked_parts = [sent]
    for shift in range(1, lon_size):
        picked_parts.append(
            lax.ppermute(sent, "lon", [(i, (i + shift) % lon_size) for i in range(lon_size)])
        )
    picked_all = jnp.concatenate([part[:rows] for part in picked_parts], axis=0)
    all_rows = picked_all.shape[0]
    own_codes = jnp.concatenate(
        [part[rows : rows + code_rows].reshape(-1)[:rows] for part in picked_parts]
    ).astype(jnp.int32)
    other_codes = other_core(own_codes)

    local_across = [across(*s) for s in local_sides]
    first_sides = sides(after(global_first, local_sides[0]))

    def shared(shard, got):
        pieces, offsets = [shard], [chip * high]
        for which, value in zip((1, 2, 3), got):
            pieces += [value, other_core(value)]
            base = (chip ^ which) * high
            offsets += [base + core * half, base + (1 - core) * half]
        return pieces, jnp.stack(offsets).astype(jnp.int32)

    block = all_rows // 3 if all_rows % (3 * 4 * kept_most) == 0 else all_rows
    steps = all_rows // block
    at_once = 2 * kept_most if block % (2 * kept_most) == 0 else kept_most
    window_codes = jnp.where(
        own_codes >= 0,
        (jnp.arange(all_rows, dtype=jnp.int32) // kept_most) % (at_once // kept_most),
        -1,
    ).reshape(steps, 1, block)
    code_spec = pl.BlockSpec((1, 1, block), lambda i, _: (i, 0, 0))
    row_spec = lambda wide: pl.BlockSpec((block, wide), lambda i, _: (i, 0))

    pieces, offsets = shared(local_full[0], [*local_sides[0], local_across[0]])
    embedded, normed, first_mix = run(
        functools.partial(embed_window_kernel, at_once, kept_most),
        steps,
        offsets,
        [row_spec(pin), code_spec, whole_block(whole_embed), *map(whole_block, pieces)],
        [picked_all, window_codes, whole_embed, *pieces],
        [(all_rows, width), (all_rows, width), (all_rows, WIDE)],
        [row_spec(width), row_spec(width), row_spec(WIDE)],
        [(width, 3 * WIDE), (block, 3 * WIDE)],
        2 * all_rows * (pin * width + width * 3 * WIDE),
        "embed_windows",
    )

    pieces, offsets = shared(local_full[1], [*local_sides[1], local_across[1]])
    pieces = after(pieces, first_sides)
    first_across = across(*first_sides)
    second_sides = sides(after(global_second, first_sides))
    (normed_own,) = run(
        functools.partial(window_out_kernel, at_once, kept_most),
        steps,
        offsets,
        [
            row_spec(width),
            row_spec(width),
            row_spec(WIDE),
            code_spec,
            whole_block(whole_out),
            *map(whole_block, pieces),
        ],
        [embedded, normed, first_mix, window_codes, whole_out, *pieces],
        [(all_rows, width)],
        [row_spec(width)],
        [(width, 3 * WIDE), (block, 3 * WIDE), (block, WIDE), (inner, width)],
        2 * all_rows * (inner * width + width * 3 * WIDE),
        "windows_out",
    )
    normed_other = other_core(normed_own)
    second_across = across(*second_sides)

    key_codes = jnp.concatenate([own_codes, other_codes]).reshape(1, 2 * all_rows)
    query_codes = jnp.concatenate([own_codes[:rows], other_codes[:rows]]).reshape(2 * rows, 1)
    query_codes = jnp.where(query_codes >= 0, query_codes, -2)
    query_block = 256 if (2 * rows) % 256 == 0 else 2 * rows
    query_steps = 2 * rows // query_block
    pieces = [global_first, *first_sides, first_across, global_second, *second_sides, second_across]
    offsets = jnp.stack([(chip ^ which) * high for which in range(4)]).astype(jnp.int32)
    late = lambda i: jnp.clip(i - 2 * steps, 0, query_steps - 1)
    (mixed,) = run(
        functools.partial(group_kernel, steps, rows, block),
        2 * steps + query_steps,
        offsets,
        [
            pl.BlockSpec((block, width), lambda i, _: (jnp.minimum(i, steps - 1), 0)),
            pl.BlockSpec((block, width), lambda i, _: (jnp.clip(i - steps, 0, steps - 1), 0)),
            pl.BlockSpec((query_block, 1), lambda i, _: (late(i), 0)),
            whole_block(key_codes),
            *map(whole_block, pieces),
        ],
        [normed_own, normed_other, query_codes, key_codes, *pieces],
        [(2 * rows, WIDE)],
        [pl.BlockSpec((query_block, WIDE), lambda i, _: (late(i), 0))],
        [
            (width, 2 * WIDE),
            (width, WIDE),
            (2 * all_rows, WIDE),
            (2 * rows, WIDE),
            (2 * all_rows, WIDE),
        ],
        2 * WIDE * (2 * all_rows * 2 * width + 2 * rows * width + 4 * rows * 2 * all_rows),
        "groups",
    )

    mine, theirs = mixed[:rows], other_core(mixed[rows:])
    result = jnp.where(
        core == 0,
        jnp.concatenate([mine, theirs], axis=1),
        jnp.concatenate([theirs, mine], axis=1),
    )
    return result.reshape(1, lat_windows, lon_windows, kept_most, inner)


def body(patches, kept_index, *weights):
    rows = patches.shape[1] * patches.shape[2] * kept_index.shape[3]
    sample_rows = rows * lax.axis_size("lat") * lax.axis_size("lon")
    fits = patches.shape[3] <= 256 and sample_rows * HEADS * HD * 2 <= vmem_limit // 4
    if lax.axis_size("batch") == 4 and lax.axis_size("lat") == HEADS // GROUP == 2 and fits:
        return sample_body(patches, kept_index, *weights)
    return owner_body(patches, kept_index, *weights)


def solution(mesh):
    return jax.shard_map(
        body,
        mesh=mesh,
        in_specs=(
            P("batch", "lat", "lon", None, None),
            P("batch", "lat", "lon", None),
            P("batch", "lat", "lon"),
            P("batch", None),
            P("batch", None),
            P("batch", None),
            P("batch", None),
        ),
        out_specs=P("batch", "lat", "lon", None, None),
        check_vma=False,
    )
```

```python
import functools

import jax
import jax.numpy as jnp
from jax import lax
from jax.experimental import pallas as pl
from jax.experimental.pallas import tpu as pltpu
from jax.sharding import PartitionSpec as P

HEADS = 8
HD = 160


norm_eps = 1e-05
mask_floor = -1e30
vmem_limit = 56 * 1024 * 1024
exp2_scale = HD ** (-0.5) * 1.4426950408889634


def layer_norm(values):
    centre = values - jnp.mean(values, axis=-1, keepdims=True)
    spread = jnp.mean(centre * centre, axis=-1, keepdims=True)
    return centre * lax.rsqrt(spread + norm_eps)


def fold_product(left_rows, shard_rows):
    return jnp.dot(left_rows, shard_rows, preferred_element_type=jnp.float32)


def attend(query_rows, key_rows, value_rows, keep_mask):
    scores = jnp.einsum(
        "bnhd,bmhd->bhnm", query_rows, key_rows, preferred_element_type=jnp.float32
    ) * HD ** (-0.5)
    scores = jnp.where(keep_mask[:, None, None, :], scores, mask_floor)
    scores = scores - jnp.max(scores, axis=-1, keepdims=True)
    weights = jnp.exp(scores)
    probabilities = (weights / jnp.sum(weights, axis=-1, keepdims=True)).astype(jnp.bfloat16)
    blended = jnp.einsum(
        "bhnm,bmhd->bnhd", probabilities, value_rows, preferred_element_type=jnp.float32
    )
    return blended.astype(jnp.bfloat16).reshape(
        query_rows.shape[0], query_rows.shape[1], HEADS * HD
    )


def owner_work(received, flag_rows, whole_global):
    item_count = received.shape[0]
    slot_values = received.reshape(item_count, -1, received.shape[-1])
    projected = jnp.dot(
        slot_values.reshape(-1, slot_values.shape[-1]),
        whole_global,
        preferred_element_type=jnp.float32,
    )
    slot_values = projected.astype(jnp.bfloat16).reshape(item_count, -1, 3 * HEADS * HD)
    heads_split = slot_values.reshape(item_count, slot_values.shape[1], 3, HEADS, HD)
    keep_mask = flag_rows.reshape(item_count, -1) > 0
    return attend(heads_split[:, :, 0], heads_split[:, :, 1], heads_split[:, :, 2], keep_mask)


def owner_body(patches, kept_index, kept_count, embed_weight, local_qkv, local_out, global_qkv):
    lat_windows = patches.shape[1]
    lon_windows = patches.shape[2]
    windows = lat_windows * lon_windows
    window_tokens = patches.shape[3]
    kept_most = kept_index.shape[3]
    row_count = windows * kept_most
    inner_width = HEADS * HD
    patch_rows = patches.reshape(windows, window_tokens, patches.shape[4])
    index_rows = kept_index.reshape(windows, kept_most)
    kept_mask = lax.broadcasted_iota(jnp.int32, (windows, kept_most), 1) < kept_count.reshape(
        windows, 1
    )
    picked = jnp.take_along_axis(patch_rows, index_rows[:, :, None], axis=1).reshape(row_count, -1)
    embedded = fold_product(
        picked, lax.all_gather(embed_weight, "batch", axis=0, tiled=True)
    ).astype(jnp.bfloat16)
    normed = layer_norm(embedded.astype(jnp.float32)).astype(jnp.bfloat16)
    local_proj = fold_product(
        normed, lax.all_gather(local_qkv, "batch", axis=0, tiled=True)
    ).astype(jnp.bfloat16)
    local_split = local_proj.reshape(windows, kept_most, 3, HEADS, HD)
    local_mix = attend(
        local_split[:, :, 0], local_split[:, :, 1], local_split[:, :, 2], kept_mask
    ).reshape(row_count, inner_width)
    back_sum = fold_product(local_mix, lax.all_gather(local_out, "batch", axis=0, tiled=True))
    hidden = (embedded.astype(jnp.float32) + back_sum).astype(jnp.bfloat16)
    normed_global = layer_norm(hidden.astype(jnp.float32)).astype(jnp.bfloat16)
    whole_global = lax.all_gather(global_qkv, "batch", axis=0, tiled=True)
    sent_width = normed_global.shape[1]
    window_ids = lax.broadcasted_iota(jnp.int32, (windows, kept_most), 0)
    slot_rows = (
        jnp.zeros((window_tokens, windows, sent_width), jnp.bfloat16)
        .at[index_rows, window_ids]
        .set(normed_global.reshape(windows, kept_most, sent_width))
    )
    flag_slots = (
        jnp.zeros((window_tokens, windows), jnp.bfloat16)
        .at[index_rows, window_ids]
        .set(kept_mask.astype(jnp.bfloat16))
    )
    owners = lax.axis_size("lat") * lax.axis_size("lon")
    owned_count = window_tokens // owners
    blended = owner_work(
        lax.all_to_all(
            slot_rows.reshape(owned_count, owners, windows, sent_width),
            ("lat", "lon"),
            split_axis=1,
            concat_axis=2,
            tiled=True,
        ),
        lax.all_to_all(
            flag_slots.reshape(owned_count, owners, windows),
            ("lat", "lon"),
            split_axis=1,
            concat_axis=2,
            tiled=True,
        ),
        whole_global,
    )
    shaped = blended.reshape(blended.shape[0], 1, -1, inner_width)
    returned = lax.all_to_all(shaped, ("lat", "lon"), split_axis=2, concat_axis=1, tiled=True)
    out_slots = returned.reshape(window_tokens, windows, inner_width)
    gathered = out_slots[index_rows, window_ids]
    result = jnp.where(kept_mask[:, :, None], gathered, jnp.zeros_like(gathered))
    return result.reshape(1, lat_windows, lon_windows, kept_most, inner_width)


MAIN = 128
TAIL = HD - MAIN
GROUP = MAIN // TAIL
WIDE = GROUP * HD


def whole_block(array):
    zeros = (0,) * array.ndim
    return pl.BlockSpec(array.shape, lambda *_: zeros)


def parts_of(pieces, high):
    return [piece.at[pl.ds(at, high)] for piece in pieces for at in range(0, piece.shape[0], high)]


def first_row(offset_ref, at, unit):
    return pl.multiple_of(offset_ref[at], unit)


def reorder(source, start, target, at):
    for head in range(GROUP):
        first = start + head * HD
        target[:, pl.ds(at + head * MAIN, MAIN)] = source[:, pl.ds(first, MAIN)]
        target[:, pl.ds(at + GROUP * MAIN + head * TAIL, TAIL)] = source[:, pl.ds(first + MAIN, TAIL)]


def pick_kernel(count_ref, patch_ref, index_ref, sent_ref):
    windows, window_tokens, _ = patch_ref.shape
    kept_most = index_ref.shape[1]
    rows = windows * kept_most
    offsets = lax.broadcasted_iota(jnp.int32, (window_tokens, kept_most), 0)
    places = lax.broadcasted_iota(jnp.int32, (1, kept_most), 1)
    sent_ref[0, pl.ds(rows, sent_ref.shape[1] - rows), :] = jnp.zeros(
        (sent_ref.shape[1] - rows, sent_ref.shape[2]), jnp.bfloat16
    )
    codes = []
    for window in range(windows):
        index = index_ref[pl.ds(window, 1), :]
        chosen = (offsets == index).astype(jnp.float32).astype(jnp.bfloat16)
        picked = lax.dot_general(
            chosen, patch_ref[window], (((0,), (0,)), ((), ())), preferred_element_type=jnp.float32
        )
        sent_ref[0, pl.ds(window * kept_most, kept_most), :] = picked.astype(jnp.bfloat16)
        codes.append(jnp.where(places < count_ref[window], index, -1))
    codes = jnp.concatenate(codes, axis=0).astype(jnp.float32).astype(jnp.bfloat16)
    sent_ref[0, pl.ds(rows, windows), pl.ds(0, kept_most)] = codes
    for copy in range(1, sent_ref.shape[0]):
        sent_ref[copy] = sent_ref[0]


def pack_columns(group, weight_ref, full_ref):
    inner = weight_ref.shape[1] // 3
    for which in range(3):
        reorder(weight_ref, which * inner + group * WIDE, full_ref, which * WIDE)


def own_half(core_ref, full_ref, half_ref):
    half = half_ref.shape[0]
    half_ref[...] = full_ref[pl.ds(pl.multiple_of(core_ref[0] * half, 16), half), :]


def pack_first_kernel(core_ref, weight_ref, embed_ref, full_ref, half_ref):
    pack_columns(0, weight_ref, full_ref)
    quarter = half_ref.shape[0] // 2
    wide = embed_ref.shape[1] // 2
    for at in range(4):
        core, side = at // 2, at % 2
        full_ref[pl.ds(at * quarter, quarter), pl.ds(3 * WIDE, wide)] = embed_ref[
            pl.ds(core * quarter, quarter), pl.ds(side * wide, wide)
        ]
    own_half(core_ref, full_ref, half_ref)


def pack_second_kernel(core_ref, weight_ref, out_ref, full_ref, half_ref):
    pack_columns(1, weight_ref, full_ref)
    full_ref[:, pl.ds(3 * WIDE, out_ref.shape[1])] = out_ref[...]
    own_half(core_ref, full_ref, half_ref)


def prepare_global_kernel(core_ref, query_ref, key_ref, value_ref, first_ref, second_ref):
    reorder(key_ref, 0, first_ref, 0)
    reorder(query_ref, 0, first_ref, WIDE)
    reorder(value_ref, 0, second_ref, 0)


def lane_head():
    return lax.broadcasted_iota(jnp.int32, (1, MAIN), 1) // TAIL


def head_tiles(ref, rows, at, head):
    main = ref[rows, pl.ds(at + head * MAIN, MAIN)]
    tail = ref[rows, pl.ds(at + GROUP * MAIN, MAIN)]
    return main, tail


def head_query(ref, rows, at, head):
    main, tail = head_tiles(ref, rows, at, head)
    return jnp.concatenate([main, jnp.where(lane_head() == head, tail, jnp.zeros_like(tail))], axis=1)


def head_pair(ref, rows, at, head):
    return jnp.concatenate(head_tiles(ref, rows, at, head), axis=1)


def masked_scores(query, key, mask):
    scores = lax.dot_general(
        query, key, (((1,), (1,)), ((), ())), preferred_element_type=jnp.float32
    )
    return jnp.where(mask, scores, mask_floor)


def mix_heads(proj_ref, code_ref, mix_ref, at_once, kept_most):
    rows = proj_ref.shape[0]
    own_window = lax.broadcasted_iota(jnp.int32, (at_once, 1), 0) // kept_most
    for start in range(0, rows, at_once):
        part = pl.ds(start, at_once)
        mask = own_window == code_ref[0, :, part]
        tails = None
        for head in range(GROUP):
            scores = masked_scores(
                head_query(proj_ref, part, 0, head), head_pair(proj_ref, part, WIDE, head), mask
            )
            top = jnp.max(scores, axis=-1, keepdims=True)
            weights = jnp.exp2((scores - top) * exp2_scale)
            total = jnp.sum(weights, axis=-1, keepdims=True)
            mixed = (
                fold_product(
                    weights.astype(jnp.bfloat16), head_pair(proj_ref, part, 2 * WIDE, head)
                )
                / total
            )
            mix_ref[part, pl.ds(head * MAIN, MAIN)] = mixed[:, :MAIN].astype(jnp.bfloat16)
            tail = mixed[:, MAIN:]
            tails = tail if tails is None else jnp.where(lane_head() == head, tail, tails)
        mix_ref[part, pl.ds(GROUP * MAIN, MAIN)] = tails.astype(jnp.bfloat16)


def embed_window_kernel(
    at_once,
    kept_most,
    offset_ref,
    picked_ref,
    code_ref,
    *refs,
):
    *pieces, embedded_ref, normed_ref, mix_ref, weight_ref, embed_ref, proj_ref = refs

    @pl.when(pl.program_id(0) == 0)
    def _():
        high = pieces[0].shape[0] // 2
        quarter = high // 2
        wide = embed_ref.shape[1] // 2
        for at, part in enumerate(parts_of(pieces, high)):
            start = first_row(offset_ref, 3 * at, 32)
            weight_ref[pl.ds(start, high), :] = part[:, pl.ds(0, 3 * WIDE)]
            start = pl.multiple_of(start // 2, 16)
            for side in range(2):
                embed_ref[pl.ds(start, quarter), pl.ds(side * wide, wide)] = part[
                    pl.ds(side * quarter, quarter), pl.ds(3 * WIDE, wide)
                ]

    embedded = fold_product(picked_ref[...], embed_ref[...]).astype(jnp.bfloat16)
    embedded_ref[...] = embedded
    normed = layer_norm(embedded.astype(jnp.float32)).astype(jnp.bfloat16)
    normed_ref[...] = normed
    proj_ref[...] = fold_product(normed, weight_ref[...]).astype(jnp.bfloat16)
    mix_heads(proj_ref, code_ref, mix_ref, at_once, kept_most)


def window_out_kernel(
    at_once,
    kept_most,
    offset_ref,
    embedded_ref,
    normed_ref,
    mix_ref,
    code_ref,
    *refs,
):
    *pieces, result_ref, weight_ref, proj_ref, own_mix_ref, row_ref = refs

    @pl.when(pl.program_id(0) == 0)
    def _():
        wide = row_ref.shape[1]
        for at, part in enumerate(parts_of(pieces, HD)):
            weight_ref[pl.ds(first_row(offset_ref, 3 * at, 32), HD), :] = part[:, pl.ds(0, 3 * WIDE)]
            row_ref[pl.ds(first_row(offset_ref, 3 * at + 1, 32), MAIN), :] = part[
                pl.ds(0, MAIN), pl.ds(3 * WIDE, wide)
            ]
            row_ref[pl.ds(first_row(offset_ref, 3 * at + 2, 32), TAIL), :] = part[
                pl.ds(MAIN, TAIL), pl.ds(3 * WIDE, wide)
            ]

    proj_ref[...] = fold_product(normed_ref[...], weight_ref[...]).astype(jnp.bfloat16)
    mix_heads(proj_ref, code_ref, own_mix_ref, at_once, kept_most)
    hidden = embedded_ref[...].astype(jnp.float32)
    hidden += fold_product(mix_ref[...], row_ref[pl.ds(0, WIDE), :])
    hidden += fold_product(own_mix_ref[...], row_ref[pl.ds(WIDE, WIDE), :])
    hidden = hidden.astype(jnp.bfloat16).astype(jnp.float32)
    result_ref[...] = layer_norm(hidden).astype(jnp.bfloat16)


def group_kernel(
    steps,
    key_chunk,
    offset_ref,
    own_ref,
    other_ref,
    code_ref,
    key_code_ref,
    *refs,
):
    *pieces, mixed_ref, first_ref, second_ref, key_ref, query_ref, value_ref = refs
    step = pl.program_id(0)
    block = own_ref.shape[0]
    query_block = mixed_ref.shape[0]

    @pl.when(step == 0)
    def _():
        for target, parts in ((first_ref, pieces[:4]), (second_ref, pieces[4:])):
            for at, part in enumerate(parts):
                target[pl.ds(first_row(offset_ref, at, 32), part.shape[0]), :] = part[...]

    def project(source_ref, at):
        normed = source_ref[...]
        part = pl.ds(pl.multiple_of(step * block, 16), block)
        key_ref[part, :] = fold_product(normed, first_ref[:, pl.ds(0, WIDE)]).astype(jnp.bfloat16)
        value_ref[part, :] = fold_product(normed, second_ref[...]).astype(jnp.bfloat16)

        @pl.when(step == at * steps + offset_ref[4])
        def _():
            query_ref[pl.ds(at * block, block), :] = fold_product(
                normed, first_ref[:, pl.ds(WIDE, WIDE)]
            ).astype(jnp.bfloat16)

    @pl.when(step < steps)
    def _():
        project(own_ref, 0)

    @pl.when((step >= steps) & (step < 2 * steps))
    def _():
        project(other_ref, 1)

    @pl.when(step >= 2 * steps)
    def _():
        part = pl.ds(pl.multiple_of((step - 2 * steps) * query_block, 16), query_block)
        codes = code_ref[...]
        key_parts = [pl.ds(at, key_chunk) for at in range(0, key_ref.shape[0], key_chunk)]
        for head in range(GROUP):
            query = head_query(query_ref, part, 0, head)
            scores = [
                masked_scores(query, head_pair(key_ref, p, 0, head), codes == key_code_ref[:, p])
                for p in key_parts
            ]
            top = functools.reduce(
                jnp.maximum, [jnp.max(s, axis=-1, keepdims=True) for s in scores]
            )
            total = 0.0
            mixed = 0.0
            for p, s in zip(key_parts, scores):
                weights = jnp.exp2((s - top) * exp2_scale)
                total += jnp.sum(weights, axis=-1, keepdims=True)
                mixed += fold_product(
                    weights.astype(jnp.bfloat16), head_pair(value_ref, p, 0, head)
                )
            mixed = jnp.where(codes >= 0, mixed / total, 0.0).astype(jnp.bfloat16)
            mixed_ref[:, pl.ds(head * HD, MAIN)] = mixed[:, :MAIN]
            at = MAIN + head * TAIL
            mixed_ref[:, pl.ds(head * HD + MAIN, TAIL)] = mixed[:, at : at + TAIL]


def swap_perm(size, mask):
    return [(i, i ^ mask) for i in range(size)]


def after(value, earlier):
    return lax.optimization_barrier((value, earlier))[0]


def run(kernel, steps, scalars, specs, arrays, outs, out_specs, scratch, flops, name):
    moved = sum(a.size * a.dtype.itemsize for a in arrays)
    return pl.pallas_call(
        kernel,
        grid_spec=pltpu.PrefetchScalarGridSpec(
            num_scalar_prefetch=1,
            grid=(steps,),
            in_specs=specs,
            out_specs=out_specs,
            scratch_shapes=[pltpu.VMEM(shape, jnp.bfloat16) for shape in scratch],
        ),
        out_shape=[jax.ShapeDtypeStruct(shape, jnp.bfloat16) for shape in outs],
        compiler_params=pltpu.CompilerParams(vmem_limit_bytes=vmem_limit),
        cost_estimate=pl.CostEstimate(flops=flops, bytes_accessed=moved, transcendentals=0),
        name=name,
    )(scalars, *arrays)


def sample_body(patches, kept_index, kept_count, embed_weight, local_qkv, local_out, global_qkv):
    lat_windows, lon_windows, window_tokens, pin = patches.shape[1:]
    windows = lat_windows * lon_windows
    kept_most = kept_index.shape[3]
    rows = windows * kept_most
    inner = HEADS * HD
    width = embed_weight.shape[1]
    lon_size = lax.axis_size("lon")
    batch_size = lax.axis_size("batch")
    core = lax.axis_index("lat")
    chip = lax.axis_index("batch")
    place = lax.axis_index("lon")
    core_scalar = core.reshape(1).astype(jnp.int32)

    def other_core(value):
        return lax.ppermute(value, "lat", swap_perm(2, 1))

    diagonal = []
    for b in range(batch_size):
        diagonal += [(2 * b, 2 * (b ^ 1)), (2 * b + 1, 2 * (b ^ 2) + 1)]

    def sides(part):
        along_x = lax.ppermute(part, "batch", swap_perm(batch_size, 1))
        along_y = lax.ppermute(part, "batch", swap_perm(batch_size, 2))
        return along_x, along_y

    def across(along_x, along_y):
        forwarded = jnp.where(core == 0, along_y, along_x)
        return lax.ppermute(forwarded, ("batch", "lat"), diagonal)

    high = local_qkv.shape[0]
    half = high // 2
    first_wide = 3 * WIDE + width // 2
    second_wide = 3 * WIDE + width

    def pack(kernel, scalar, other, wide, name):
        shapes = [(high, wide), (half, wide)]
        return run(
            kernel,
            1,
            scalar,
            [whole_block(local_qkv), whole_block(other)],
            [local_qkv, other],
            shapes,
            [pl.BlockSpec(shape, lambda *_: (0, 0)) for shape in shapes],
            [],
            0,
            name,
        )

    local_first, half_first = pack(
        pack_first_kernel, core_scalar, embed_weight, first_wide, "pack_first"
    )

    code_tile = -(-windows // 16) * 16
    sent_shape = (lon_size, rows + code_tile, pin)
    patch_rows = patches.reshape(windows, window_tokens, pin)
    index_rows = kept_index.reshape(windows, kept_most)
    (sent,) = run(
        pick_kernel,
        1,
        after(kept_count.reshape(windows), half_first),
        [whole_block(patch_rows), whole_block(index_rows)],
        [patch_rows, index_rows],
        [sent_shape],
        [pl.BlockSpec(sent_shape, lambda *_: (0, 0, 0))],
        [],
        0,
        "pick",
    )
    got = lax.all_to_all(sent, "lon", 0, 0, tiled=True)
    all_rows = lon_size * rows
    own_codes = got[:, rows : rows + windows, :kept_most].reshape(-1).astype(jnp.int32)
    other_codes = other_core(own_codes)

    local_second, half_second = pack(
        pack_second_kernel, after(core_scalar, sent), local_out, second_wide, "pack_second"
    )
    global_first, global_second = run(
        prepare_global_kernel,
        1,
        after(core_scalar, half_second),
        [
            pl.BlockSpec((high, WIDE), lambda i, c, which=which: (0, 2 * which + c[0]))
            for which in range(3)
        ],
        [global_qkv] * 3,
        [(high, 2 * WIDE), (high, WIDE)],
        [pl.BlockSpec((high, w), lambda *_: (0, 0)) for w in (2 * WIDE, WIDE)],
        [],
        0,
        "order_global",
    )
    sides_first = sides(half_first)
    half_second, _ = after((half_second, global_first), sides_first)
    sides_second = sides(half_second)
    across_first = across(*sides_first)
    global_sides = sides(after(global_first, sides_second))
    across_second = across(*sides_second)

    def shared(shard, got, earlier):
        joined = jnp.concatenate(got[:2], axis=0)
        pieces = [shard, joined, other_core(joined), got[2], other_core(after(got[2], earlier))]
        bases = [(chip ^ which) * high for which in (1, 2, 3)]
        firsts = [chip * high, chip * high + half]
        for group in (bases[:2], bases[2:]):
            firsts += [base + core * half for base in group]
            firsts += [base + (1 - core) * half for base in group]
        firsts = jnp.stack(firsts).astype(jnp.int32)
        head = firsts // HD
        group_start = head // GROUP * WIDE
        main = group_start + head % GROUP * MAIN
        tail = group_start + GROUP * MAIN + head % GROUP * TAIL
        return pieces, jnp.stack([firsts, main, tail], axis=1).reshape(-1)

    block, steps = rows, lon_size
    at_once = 2 * kept_most if block % (2 * kept_most) == 0 else kept_most
    window_codes = jnp.where(
        own_codes >= 0,
        (jnp.arange(all_rows, dtype=jnp.int32) // kept_most) % (at_once // kept_most),
        -1,
    ).reshape(steps, 1, block)
    code_spec = pl.BlockSpec((1, 1, block), lambda i, _: (i, 0, 0))
    row_spec = lambda wide: pl.BlockSpec((block, wide), lambda i, _: (i, 0))
    at_home = lambda a: lax.dynamic_slice_in_dim(a, place * rows, rows, axis=0)
    key_codes = jnp.concatenate([own_codes, other_codes]).reshape(1, 2 * all_rows)
    query_codes = jnp.concatenate([at_home(own_codes), at_home(other_codes)]).reshape(2 * rows, 1)
    query_codes = jnp.where(query_codes >= 0, query_codes, -2)
    global_starts = [(chip ^ which) * high for which in range(4)]
    global_offsets = jnp.stack([*global_starts, place]).astype(jnp.int32)

    pieces, offsets = shared(local_first, [*sides_first, across_first], core_scalar)
    window_codes, _ = after((window_codes, 0), (key_codes, query_codes, global_offsets))
    embedded, normed, first_mix = run(
        functools.partial(embed_window_kernel, at_once, kept_most),
        steps,
        offsets,
        [
            pl.BlockSpec((None, rows, pin), lambda i, _: (i, 0, 0)),
            code_spec,
            *map(whole_block, pieces),
        ],
        [got, window_codes, *pieces],
        [(all_rows, width), (all_rows, width), (all_rows, WIDE)],
        [row_spec(width), row_spec(width), row_spec(WIDE)],
        [(width, 3 * WIDE), (pin, width), (block, 3 * WIDE)],
        2 * all_rows * (pin * width + width * 3 * WIDE),
        "embed_windows",
    )

    pieces, offsets = shared(local_second, [*sides_second, across_second], first_mix)
    global_sides, _ = after((global_sides, 0), first_mix)
    global_across = across(*global_sides)
    value_sides = sides(after(global_second, global_sides))
    (normed_own,) = run(
        functools.partial(window_out_kernel, at_once, kept_most),
        steps,
        offsets,
        [row_spec(width), row_spec(width), row_spec(WIDE), code_spec, *map(whole_block, pieces)],
        [embedded, normed, first_mix, window_codes, *pieces],
        [(all_rows, width)],
        [row_spec(width)],
        [(width, 3 * WIDE), (block, 3 * WIDE), (block, WIDE), (inner, width)],
        2 * all_rows * (inner * width + width * 3 * WIDE),
        "windows_out",
    )
    normed_own = after(normed_own, (global_across, value_sides))
    normed_other = other_core(normed_own)
    value_across = across(*value_sides)

    query_block = 256 if (2 * rows) % 256 == 0 else 2 * rows
    query_steps = 2 * rows // query_block
    pieces = [global_first, *global_sides, global_across, global_second, *value_sides, value_across]
    key_chunk = 512 if (2 * all_rows) % 512 == 0 else block
    late = lambda i: jnp.clip(i - 2 * steps, 0, query_steps - 1)
    (mixed,) = run(
        functools.partial(group_kernel, steps, key_chunk),
        2 * steps + query_steps,
        global_offsets,
        [
            pl.BlockSpec((block, width), lambda i, _: (jnp.minimum(i, steps - 1), 0)),
            pl.BlockSpec((block, width), lambda i, _: (jnp.clip(i - steps, 0, steps - 1), 0)),
            pl.BlockSpec((query_block, 1), lambda i, _: (late(i), 0)),
            whole_block(key_codes),
            *map(whole_block, pieces),
        ],
        [normed_own, normed_other, query_codes, key_codes, *pieces],
        [(2 * rows, WIDE)],
        [pl.BlockSpec((query_block, WIDE), lambda i, _: (late(i), 0))],
        [
            (width, 2 * WIDE),
            (width, WIDE),
            (2 * all_rows, WIDE),
            (2 * rows, WIDE),
            (2 * all_rows, WIDE),
        ],
        2 * WIDE * (2 * all_rows * 2 * width + 2 * rows * width + 4 * rows * 2 * all_rows),
        "groups",
    )

    mine, theirs = mixed[:rows], other_core(mixed[rows:])
    result = jnp.where(
        core == 0,
        jnp.concatenate([mine, theirs], axis=1),
        jnp.concatenate([theirs, mine], axis=1),
    )
    return result.reshape(1, lat_windows, lon_windows, kept_most, inner)


def body(patches, kept_index, kept_count, embed_weight, local_qkv, local_out, global_qkv):
    args = (patches, kept_index, kept_count, embed_weight, local_qkv, local_out, global_qkv)
    windows = patches.shape[1] * patches.shape[2]
    rows = windows * kept_index.shape[3]
    sample_rows = rows * lax.axis_size("lat") * lax.axis_size("lon")
    fits = patches.shape[3] <= 256 and windows <= 16 and sample_rows * HEADS * HD * 2 <= vmem_limit // 4
    shards = embed_weight.shape[0] * 2 == local_qkv.shape[0] == local_out.shape[0] == 2 * HD
    if lax.axis_size("batch") == 4 and lax.axis_size("lat") == HEADS // GROUP == 2 and fits and shards:
        return sample_body(*args)
    return owner_body(*args)


def solution(mesh):
    return jax.shard_map(
        body,
        mesh=mesh,
        in_specs=(
            P("batch", "lat", "lon", None, None),
            P("batch", "lat", "lon", None),
            P("batch", "lat", "lon"),
            P("batch", None),
            P("batch", None),
            P("batch", None),
            P("batch", None),
        ),
        out_specs=P("batch", "lat", "lon", None, None),
        check_vma=False,
    )
```

```python
import functools

import jax
import jax.numpy as jnp
from jax import lax
from jax.experimental import pallas as pl
from jax.experimental.pallas import tpu as pltpu
from jax.sharding import PartitionSpec as P

HEADS = 8
HD = 160


norm_eps = 1e-05
mask_floor = -1e30
vmem_limit = 56 * 1024 * 1024
exp2_scale = HD ** (-0.5) * 1.4426950408889634


def layer_norm(values):
    centre = values - jnp.mean(values, axis=-1, keepdims=True)
    spread = jnp.mean(centre * centre, axis=-1, keepdims=True)
    return centre * lax.rsqrt(spread + norm_eps)


def fold_product(left_rows, shard_rows):
    return jnp.dot(left_rows, shard_rows, preferred_element_type=jnp.float32)


def attend(query_rows, key_rows, value_rows, keep_mask):
    scores = jnp.einsum(
        "bnhd,bmhd->bhnm", query_rows, key_rows, preferred_element_type=jnp.float32
    ) * HD ** (-0.5)
    scores = jnp.where(keep_mask[:, None, None, :], scores, mask_floor)
    scores = scores - jnp.max(scores, axis=-1, keepdims=True)
    weights = jnp.exp(scores)
    probabilities = (weights / jnp.sum(weights, axis=-1, keepdims=True)).astype(jnp.bfloat16)
    blended = jnp.einsum(
        "bhnm,bmhd->bnhd", probabilities, value_rows, preferred_element_type=jnp.float32
    )
    return blended.astype(jnp.bfloat16).reshape(
        query_rows.shape[0], query_rows.shape[1], HEADS * HD
    )


def owner_work(received, flag_rows, whole_global):
    item_count = received.shape[0]
    slot_values = received.reshape(item_count, -1, received.shape[-1])
    projected = jnp.dot(
        slot_values.reshape(-1, slot_values.shape[-1]),
        whole_global,
        preferred_element_type=jnp.float32,
    )
    slot_values = projected.astype(jnp.bfloat16).reshape(item_count, -1, 3 * HEADS * HD)
    heads_split = slot_values.reshape(item_count, slot_values.shape[1], 3, HEADS, HD)
    keep_mask = flag_rows.reshape(item_count, -1) > 0
    return attend(heads_split[:, :, 0], heads_split[:, :, 1], heads_split[:, :, 2], keep_mask)


def owner_body(patches, kept_index, kept_count, embed_weight, local_qkv, local_out, global_qkv):
    lat_windows = patches.shape[1]
    lon_windows = patches.shape[2]
    windows = lat_windows * lon_windows
    window_tokens = patches.shape[3]
    kept_most = kept_index.shape[3]
    row_count = windows * kept_most
    inner_width = HEADS * HD
    patch_rows = patches.reshape(windows, window_tokens, patches.shape[4])
    index_rows = kept_index.reshape(windows, kept_most)
    kept_mask = lax.broadcasted_iota(jnp.int32, (windows, kept_most), 1) < kept_count.reshape(
        windows, 1
    )
    picked = jnp.take_along_axis(patch_rows, index_rows[:, :, None], axis=1).reshape(row_count, -1)
    embedded = fold_product(
        picked, lax.all_gather(embed_weight, "batch", axis=0, tiled=True)
    ).astype(jnp.bfloat16)
    normed = layer_norm(embedded.astype(jnp.float32)).astype(jnp.bfloat16)
    local_proj = fold_product(
        normed, lax.all_gather(local_qkv, "batch", axis=0, tiled=True)
    ).astype(jnp.bfloat16)
    local_split = local_proj.reshape(windows, kept_most, 3, HEADS, HD)
    local_mix = attend(
        local_split[:, :, 0], local_split[:, :, 1], local_split[:, :, 2], kept_mask
    ).reshape(row_count, inner_width)
    back_sum = fold_product(local_mix, lax.all_gather(local_out, "batch", axis=0, tiled=True))
    hidden = (embedded.astype(jnp.float32) + back_sum).astype(jnp.bfloat16)
    normed_global = layer_norm(hidden.astype(jnp.float32)).astype(jnp.bfloat16)
    whole_global = lax.all_gather(global_qkv, "batch", axis=0, tiled=True)
    sent_width = normed_global.shape[1]
    window_ids = lax.broadcasted_iota(jnp.int32, (windows, kept_most), 0)
    slot_rows = (
        jnp.zeros((window_tokens, windows, sent_width), jnp.bfloat16)
        .at[index_rows, window_ids]
        .set(normed_global.reshape(windows, kept_most, sent_width))
    )
    flag_slots = (
        jnp.zeros((window_tokens, windows), jnp.bfloat16)
        .at[index_rows, window_ids]
        .set(kept_mask.astype(jnp.bfloat16))
    )
    owners = lax.axis_size("lat") * lax.axis_size("lon")
    owned_count = window_tokens // owners
    blended = owner_work(
        lax.all_to_all(
            slot_rows.reshape(owned_count, owners, windows, sent_width),
            ("lat", "lon"),
            split_axis=1,
            concat_axis=2,
            tiled=True,
        ),
        lax.all_to_all(
            flag_slots.reshape(owned_count, owners, windows),
            ("lat", "lon"),
            split_axis=1,
            concat_axis=2,
            tiled=True,
        ),
        whole_global,
    )
    shaped = blended.reshape(blended.shape[0], 1, -1, inner_width)
    returned = lax.all_to_all(shaped, ("lat", "lon"), split_axis=2, concat_axis=1, tiled=True)
    out_slots = returned.reshape(window_tokens, windows, inner_width)
    gathered = out_slots[index_rows, window_ids]
    result = jnp.where(kept_mask[:, :, None], gathered, jnp.zeros_like(gathered))
    return result.reshape(1, lat_windows, lon_windows, kept_most, inner_width)


MAIN = 128
TAIL = HD - MAIN
GROUP = MAIN // TAIL
WIDE = GROUP * HD


def whole_block(array):
    zeros = (0,) * array.ndim
    return pl.BlockSpec(array.shape, lambda *_: zeros)


def parts_of(pieces, high):
    return [piece.at[pl.ds(at, high)] for piece in pieces for at in range(0, piece.shape[0], high)]


def first_row(offset_ref, at, unit):
    return pl.multiple_of(offset_ref[at], unit)


def reorder(source, start, target, at):
    for head in range(GROUP):
        first = start + head * HD
        target[:, pl.ds(at + head * MAIN, MAIN)] = source[:, pl.ds(first, MAIN)]
        target[:, pl.ds(at + GROUP * MAIN + head * TAIL, TAIL)] = source[:, pl.ds(first + MAIN, TAIL)]


def pick_kernel(_, patch_ref, code_ref, partner_ref, *sent_refs):
    window_tokens = patch_ref.shape[1]
    windows, kept_most = code_ref.shape
    count = windows // len(sent_refs)
    rows = count * kept_most
    offsets = lax.broadcasted_iota(jnp.int32, (window_tokens, kept_most), 0)
    for which, sent_ref in enumerate(sent_refs):
        tile = sent_ref.shape[1] - rows
        sent_ref[0, pl.ds(rows, tile), :] = jnp.zeros((tile, sent_ref.shape[2]), jnp.bfloat16)
        for at in range(count):
            window = which * count + at
            chosen = (offsets == code_ref[pl.ds(window, 1), :]).astype(jnp.float32)
            picked = lax.dot_general(
                chosen.astype(jnp.bfloat16),
                patch_ref[window],
                (((0,), (0,)), ((), ())),
                preferred_element_type=jnp.float32,
            )
            sent_ref[0, pl.ds(at * kept_most, kept_most), :] = picked.astype(jnp.bfloat16)
        part = pl.ds(which * count, count)
        codes = jnp.concatenate([code_ref[part, :], partner_ref[part, :]], axis=0)
        sent_ref[0, pl.ds(rows, 2 * count), pl.ds(0, kept_most)] = codes.astype(jnp.float32).astype(
            jnp.bfloat16
        )
        for copy in range(1, sent_ref.shape[0]):
            sent_ref[copy] = sent_ref[0]


def pack_columns(group, weight_ref, full_ref):
    inner = weight_ref.shape[1] // 3
    for which in range(3):
        reorder(weight_ref, which * inner + group * WIDE, full_ref, which * WIDE)


def own_half(core_ref, full_ref, half_ref):
    half = half_ref.shape[0]
    half_ref[...] = full_ref[pl.ds(pl.multiple_of(core_ref[0] * half, 16), half), :]


def pack_first_kernel(core_ref, weight_ref, embed_ref, full_ref, half_ref):
    pack_columns(0, weight_ref, full_ref)
    quarter = half_ref.shape[0] // 2
    wide = embed_ref.shape[1] // 2
    for at in range(4):
        core, side = at // 2, at % 2
        full_ref[pl.ds(at * quarter, quarter), pl.ds(3 * WIDE, wide)] = embed_ref[
            pl.ds(core * quarter, quarter), pl.ds(side * wide, wide)
        ]
    own_half(core_ref, full_ref, half_ref)


def pack_second_kernel(core_ref, weight_ref, out_ref, full_ref, half_ref):
    pack_columns(1, weight_ref, full_ref)
    full_ref[:, pl.ds(3 * WIDE, out_ref.shape[1])] = out_ref[...]
    own_half(core_ref, full_ref, half_ref)


def prepare_global_kernel(core_ref, query_ref, key_ref, value_ref, first_ref, second_ref):
    reorder(key_ref, 0, first_ref, 0)
    reorder(query_ref, 0, first_ref, WIDE)
    reorder(value_ref, 0, second_ref, 0)


def lane_head():
    return lax.broadcasted_iota(jnp.int32, (1, MAIN), 1) // TAIL


def head_tiles(ref, rows, at, head):
    main = ref[rows, pl.ds(at + head * MAIN, MAIN)]
    tail = ref[rows, pl.ds(at + GROUP * MAIN, MAIN)]
    return main, tail


def head_query(ref, rows, at, head):
    main, tail = head_tiles(ref, rows, at, head)
    return jnp.concatenate([main, jnp.where(lane_head() == head, tail, jnp.zeros_like(tail))], axis=1)


def head_pair(ref, rows, at, head):
    return jnp.concatenate(head_tiles(ref, rows, at, head), axis=1)


def masked_scores(query, key, mask):
    scores = lax.dot_general(
        query, key, (((1,), (1,)), ((), ())), preferred_element_type=jnp.float32
    )
    return jnp.where(mask, scores, mask_floor)


def code_row(tile, at, kept_most):
    return tile[at : at + 1, :kept_most]


def mix_heads(proj_ref, code_ref, mix_ref, count, kept_most, at_once):
    rows = proj_ref.shape[0]
    own_window = lax.broadcasted_iota(jnp.int32, (at_once, 1), 0) // kept_most
    key_window = lax.broadcasted_iota(jnp.int32, (1, at_once), 1) // kept_most
    tiles = [code_ref[at].astype(jnp.float32) for at in range(code_ref.shape[0])]
    codes = [code_row(tile, at, kept_most) for tile in tiles for at in range(count)]
    for start in range(0, rows, at_once):
        part = pl.ds(start, at_once)
        first = start // kept_most
        key_codes = jnp.concatenate(codes[first : first + at_once // kept_most], axis=1)
        mask = own_window == jnp.where(key_codes >= 0, key_window, -1)
        tails = None
        for head in range(GROUP):
            scores = masked_scores(
                head_query(proj_ref, part, 0, head), head_pair(proj_ref, part, WIDE, head), mask
            )
            top = jnp.max(scores, axis=-1, keepdims=True)
            weights = jnp.exp2((scores - top) * exp2_scale)
            total = jnp.sum(weights, axis=-1, keepdims=True)
            mixed = (
                fold_product(
                    weights.astype(jnp.bfloat16), head_pair(proj_ref, part, 2 * WIDE, head)
                )
                / total
            )
            mix_ref[part, pl.ds(head * MAIN, MAIN)] = mixed[:, :MAIN].astype(jnp.bfloat16)
            tail = mixed[:, MAIN:]
            tails = tail if tails is None else jnp.where(lane_head() == head, tail, tails)
        mix_ref[part, pl.ds(GROUP * MAIN, MAIN)] = tails.astype(jnp.bfloat16)


def embed_window_kernel(
    mix,
    offset_ref,
    picked_ref,
    code_ref,
    *refs,
):
    *pieces, embedded_ref, normed_ref, mix_ref, weight_ref, embed_ref, proj_ref = refs

    @pl.when(pl.program_id(0) == 0)
    def _():
        high = pieces[0].shape[0] // 2
        quarter = high // 2
        wide = embed_ref.shape[1] // 2
        for at, part in enumerate(parts_of(pieces, high)):
            start = first_row(offset_ref, 3 * at, 32)
            weight_ref[pl.ds(start, high), :] = part[:, pl.ds(0, 3 * WIDE)]
            start = pl.multiple_of(start // 2, 16)
            for side in range(2):
                embed_ref[pl.ds(start, quarter), pl.ds(side * wide, wide)] = part[
                    pl.ds(side * quarter, quarter), pl.ds(3 * WIDE, wide)
                ]

    picked = picked_ref[...].reshape(proj_ref.shape[0], picked_ref.shape[2])
    embedded = fold_product(picked, embed_ref[...]).astype(jnp.bfloat16)
    embedded_ref[...] = embedded
    normed = layer_norm(embedded.astype(jnp.float32)).astype(jnp.bfloat16)
    normed_ref[...] = normed
    proj_ref[...] = fold_product(normed, weight_ref[...]).astype(jnp.bfloat16)
    mix(proj_ref, code_ref, mix_ref)


def window_out_kernel(
    mix,
    offset_ref,
    embedded_ref,
    normed_ref,
    mix_ref,
    code_ref,
    *refs,
):
    *pieces, result_ref, weight_ref, proj_ref, own_mix_ref, row_ref = refs

    @pl.when(pl.program_id(0) == 0)
    def _():
        wide = row_ref.shape[1]
        for at, part in enumerate(parts_of(pieces, HD)):
            weight_ref[pl.ds(first_row(offset_ref, 3 * at, 32), HD), :] = part[:, pl.ds(0, 3 * WIDE)]
            row_ref[pl.ds(first_row(offset_ref, 3 * at + 1, 32), MAIN), :] = part[
                pl.ds(0, MAIN), pl.ds(3 * WIDE, wide)
            ]
            row_ref[pl.ds(first_row(offset_ref, 3 * at + 2, 32), TAIL), :] = part[
                pl.ds(MAIN, TAIL), pl.ds(3 * WIDE, wide)
            ]

    proj_ref[...] = fold_product(normed_ref[...], weight_ref[...]).astype(jnp.bfloat16)
    mix(proj_ref, code_ref, own_mix_ref)
    hidden = embedded_ref[...].astype(jnp.float32)
    hidden += fold_product(mix_ref[...], row_ref[pl.ds(0, WIDE), :])
    hidden += fold_product(own_mix_ref[...], row_ref[pl.ds(WIDE, WIDE), :])
    hidden = hidden.astype(jnp.bfloat16).astype(jnp.float32)
    result_ref[...] = layer_norm(hidden).astype(jnp.bfloat16)


def group_kernel(steps, parts, count, kept_most, key_chunk, offset_ref, *refs):
    many = 2 * parts
    normed_refs, refs = refs[:many], refs[many:]
    tile_refs, refs = refs[:parts], refs[parts:]
    code_ref, *pieces, mixed_ref, first_ref, second_ref, key_ref, query_ref, value_ref, key_code_ref = refs
    step = pl.program_id(0)
    block = normed_refs[0].shape[0]
    query_block = mixed_ref.shape[0]
    part_rows = count * kept_most
    shared = block // part_rows

    @pl.when(step == 0)
    def _():
        for target, arrays in ((first_ref, pieces[:4]), (second_ref, pieces[4:])):
            for at, array in enumerate(arrays):
                target[pl.ds(first_row(offset_ref, at, 32), array.shape[0]), :] = array[...]
        at = 0
        for core in range(2):
            for tile_ref in tile_refs:
                for device in range(tile_ref.shape[0]):
                    tile = tile_ref[device].astype(jnp.float32)
                    for window in range(count):
                        key_code_ref[:, pl.ds(at, kept_most)] = code_row(
                            tile, core * count + window, kept_most
                        )
                        at += kept_most

    for which, normed_ref in enumerate(normed_refs):

        @pl.when((step >= which * steps) & (step < (which + 1) * steps))
        def _():
            normed = normed_ref[...]
            part = pl.ds(pl.multiple_of(step * block, 16), block)
            key_ref[part, :] = fold_product(normed, first_ref[:, pl.ds(0, WIDE)]).astype(jnp.bfloat16)
            value_ref[part, :] = fold_product(normed, second_ref[...]).astype(jnp.bfloat16)

        @pl.when(step == which * steps + offset_ref[4] // shared)
        def _():
            start = pl.multiple_of(offset_ref[4] % shared * part_rows, 16)
            query_ref[pl.ds(which * part_rows, part_rows), :] = fold_product(
                normed_ref[pl.ds(start, part_rows), :], first_ref[:, pl.ds(WIDE, WIDE)]
            ).astype(jnp.bfloat16)

    @pl.when(step >= many * steps)
    def _():
        part = pl.ds(pl.multiple_of((step - many * steps) * query_block, 16), query_block)
        codes = code_ref[...]
        key_parts = [pl.ds(at, key_chunk) for at in range(0, key_ref.shape[0], key_chunk)]
        for head in range(GROUP):
            query = head_query(query_ref, part, 0, head)
            scores = [
                masked_scores(query, head_pair(key_ref, p, 0, head), codes == key_code_ref[:, p])
                for p in key_parts
            ]
            top = functools.reduce(
                jnp.maximum, [jnp.max(s, axis=-1, keepdims=True) for s in scores]
            )
            total = 0.0
            mixed = 0.0
            for p, s in zip(key_parts, scores):
                weights = jnp.exp2((s - top) * exp2_scale)
                total += jnp.sum(weights, axis=-1, keepdims=True)
                mixed += fold_product(
                    weights.astype(jnp.bfloat16), head_pair(value_ref, p, 0, head)
                )
            mixed = jnp.where(codes >= 0, mixed / total, 0.0).astype(jnp.bfloat16)
            mixed_ref[:, pl.ds(head * HD, MAIN)] = mixed[:, :MAIN]
            at = MAIN + head * TAIL
            mixed_ref[:, pl.ds(head * HD + MAIN, TAIL)] = mixed[:, at : at + TAIL]


def swap_perm(size, mask):
    return [(i, i ^ mask) for i in range(size)]


def after(value, earlier):
    return lax.optimization_barrier((value, earlier))[0]


def run(kernel, steps, scalars, specs, arrays, outs, out_specs, scratch, flops, name):
    moved = sum(a.size * a.dtype.itemsize for a in arrays)
    return pl.pallas_call(
        kernel,
        grid_spec=pltpu.PrefetchScalarGridSpec(
            num_scalar_prefetch=1,
            grid=(steps,),
            in_specs=specs,
            out_specs=out_specs,
            scratch_shapes=[
                pltpu.VMEM(shape, jnp.bfloat16) if isinstance(shape, tuple) else shape
                for shape in scratch
            ],
        ),
        out_shape=[jax.ShapeDtypeStruct(shape, jnp.bfloat16) for shape in outs],
        compiler_params=pltpu.CompilerParams(vmem_limit_bytes=vmem_limit),
        cost_estimate=pl.CostEstimate(flops=flops, bytes_accessed=moved, transcendentals=0),
        name=name,
    )(scalars, *arrays)


def sample_body(patches, kept_index, kept_count, embed_weight, local_qkv, local_out, global_qkv):
    lat_windows, lon_windows, window_tokens, pin = patches.shape[1:]
    windows = lat_windows * lon_windows
    kept_most = kept_index.shape[3]
    rows = windows * kept_most
    inner = HEADS * HD
    width = embed_weight.shape[1]
    lon_size = lax.axis_size("lon")
    batch_size = lax.axis_size("batch")
    core = lax.axis_index("lat")
    chip = lax.axis_index("batch")
    place = lax.axis_index("lon")
    core_scalar = core.reshape(1).astype(jnp.int32)

    def other_core(value):
        return lax.ppermute(value, "lat", swap_perm(2, 1))

    diagonal = []
    for b in range(batch_size):
        diagonal += [(2 * b, 2 * (b ^ 1)), (2 * b + 1, 2 * (b ^ 2) + 1)]

    def sides(part):
        along_x = lax.ppermute(part, "batch", swap_perm(batch_size, 1))
        along_y = lax.ppermute(part, "batch", swap_perm(batch_size, 2))
        return along_x, along_y

    def across(along_x, along_y):
        forwarded = jnp.where(core == 0, along_y, along_x)
        return lax.ppermute(forwarded, ("batch", "lat"), diagonal)

    high = local_qkv.shape[0]
    half = high // 2
    first_wide = 3 * WIDE + width // 2
    second_wide = 3 * WIDE + width

    def pack(kernel, scalar, other, wide, name):
        shapes = [(high, wide), (half, wide)]
        return run(
            kernel,
            1,
            scalar,
            [whole_block(local_qkv), whole_block(other)],
            [local_qkv, other],
            shapes,
            [pl.BlockSpec(shape, lambda *_: (0, 0)) for shape in shapes],
            [],
            0,
            name,
        )

    local_first, half_first = pack(
        pack_first_kernel, core_scalar, embed_weight, first_wide, "pack_first"
    )

    parts = 1
    count = windows // parts
    part_rows = count * kept_most
    code_tile = -(-2 * count // 16) * 16
    sent_shape = (lon_size, part_rows + code_tile, pin)
    patch_rows = patches.reshape(windows, window_tokens, pin)
    kept_mask = lax.broadcasted_iota(jnp.int32, (windows, kept_most), 1) < kept_count.reshape(
        windows, 1
    )
    codes = jnp.where(kept_mask, kept_index.reshape(windows, kept_most), -1)
    partner_codes = other_core(codes)
    query_codes = jnp.concatenate([codes, partner_codes], axis=0).astype(jnp.float32)
    query_codes = query_codes.reshape(2 * rows, 1)
    global_starts = [(chip ^ which) * high for which in range(4)]
    global_offsets = jnp.stack([*global_starts, place]).astype(jnp.int32)
    sent = run(
        pick_kernel,
        1,
        after(core_scalar, half_first),
        [whole_block(patch_rows), whole_block(codes), whole_block(partner_codes)],
        [patch_rows, codes, partner_codes],
        [sent_shape] * parts,
        [pl.BlockSpec(sent_shape, lambda *_: (0, 0, 0))] * parts,
        [],
        0,
        "pick",
    )
    query_codes, global_offsets = after((query_codes, global_offsets), sent)
    got = []
    for value in sent:
        value = after(value, got[-1]) if got else value
        got.append(lax.all_to_all(value, "lon", 0, 0, tiled=True))

    local_second, half_second = pack(
        pack_second_kernel, after(core_scalar, sent), local_out, second_wide, "pack_second"
    )
    global_first, global_second = run(
        prepare_global_kernel,
        1,
        after(core_scalar, half_second),
        [
            pl.BlockSpec((high, WIDE), lambda i, c, which=which: (0, 2 * which + c[0]))
            for which in range(3)
        ],
        [global_qkv] * 3,
        [(high, 2 * WIDE), (high, WIDE)],
        [pl.BlockSpec((high, w), lambda *_: (0, 0)) for w in (2 * WIDE, WIDE)],
        [],
        0,
        "order_global",
    )
    sides_first = sides(half_first)
    sides_first = after(sides_first, (sent, global_first))
    sides_second = sides(after(half_second, sides_first))
    across_first = across(*sides_first)
    global_sides = sides(after(global_first, sides_second))
    across_second = across(*sides_second)

    def shared(shard, got, earlier):
        joined = jnp.concatenate(got[:2], axis=0)
        pieces = [shard, joined, other_core(joined), got[2], other_core(after(got[2], earlier))]
        bases = [(chip ^ which) * high for which in (1, 2, 3)]
        firsts = [chip * high, chip * high + half]
        for group in (bases[:2], bases[2:]):
            firsts += [base + core * half for base in group]
            firsts += [base + (1 - core) * half for base in group]
        firsts = jnp.stack(firsts).astype(jnp.int32)
        head = firsts // HD
        group_start = head // GROUP * WIDE
        main = group_start + head % GROUP * MAIN
        tail = group_start + GROUP * MAIN + head % GROUP * TAIL
        return pieces, jnp.stack([firsts, main, tail], axis=1).reshape(-1)

    shared_by = 2 if lon_size % 2 == 0 else 1
    block = shared_by * part_rows
    steps = lon_size // shared_by
    many_rows = lon_size * part_rows
    at_once = 2 * kept_most if block % (2 * kept_most) == 0 else kept_most
    mix = functools.partial(mix_heads, count=count, kept_most=kept_most, at_once=at_once)
    row_spec = lambda wide: pl.BlockSpec((block, wide), lambda i, _: (i, 0))
    tile_spec = pl.BlockSpec((shared_by, code_tile, MAIN), lambda i, _: (i, part_rows // code_tile, 0))

    pieces, offsets = shared(local_first, [*sides_first, across_first], core_scalar)
    embedded, normed, mixes = [], [], []
    for which in range(parts):
        if which == parts - 1:
            pieces = after(pieces, (sides_second, mixes))
        result = run(
            functools.partial(embed_window_kernel, mix),
            steps,
            offsets,
            [
                pl.BlockSpec((shared_by, part_rows, pin), lambda i, _: (i, 0, 0)),
                tile_spec,
                *map(whole_block, pieces),
            ],
            [got[which], got[which], *pieces],
            [(many_rows, width), (many_rows, width), (many_rows, WIDE)],
            [row_spec(width), row_spec(width), row_spec(WIDE)],
            [(width, 3 * WIDE), (pin, width), (block, 3 * WIDE)],
            2 * many_rows * (pin * width + width * 3 * WIDE),
            "embed_windows",
        )
        for values, value in zip((embedded, normed, mixes), result):
            values.append(value)

    pieces, offsets = shared(local_second, [*sides_second, across_second], mixes[0])
    own, partner = [], []
    for which in range(parts):
        if which == parts - 1:
            pieces = after(pieces, (global_sides, own))
            global_sides, _ = after((global_sides, 0), own or mixes)
            global_across = across(*global_sides)
            value_sides = sides(after(global_second, global_sides))
        (result,) = run(
            functools.partial(window_out_kernel, mix),
            steps,
            offsets,
            [row_spec(width), row_spec(width), row_spec(WIDE), tile_spec, *map(whole_block, pieces)],
            [embedded[which], normed[which], mixes[which], got[which], *pieces],
            [(many_rows, width)],
            [row_spec(width)],
            [(width, 3 * WIDE), (block, 3 * WIDE), (block, WIDE), (inner, width)],
            2 * many_rows * (inner * width + width * 3 * WIDE),
            "windows_out",
        )
        own.append(result)
        if which == parts - 1:
            result = after(result, (global_across, value_sides))
        partner.append(other_core(result))
    value_across = across(*value_sides)

    all_rows = lon_size * rows
    query_block = 256 if (2 * rows) % 256 == 0 else 2 * rows
    query_steps = 2 * rows // query_block
    project_steps = 2 * parts * steps
    pieces = [global_first, *global_sides, global_across, global_second, *value_sides, value_across]
    key_chunk = 512 if (2 * all_rows) % 512 == 0 else block
    late = lambda i: jnp.clip(i - project_steps, 0, query_steps - 1)
    normed_specs = [
        pl.BlockSpec((block, width), lambda i, _, at=at: (jnp.clip(i - at * steps, 0, steps - 1), 0))
        for at in range(2 * parts)
    ]
    whole_tile = pl.BlockSpec(
        (lon_size, code_tile, MAIN), lambda *_: (0, part_rows // code_tile, 0)
    )
    (mixed,) = run(
        functools.partial(group_kernel, steps, parts, count, kept_most, key_chunk),
        project_steps + query_steps,
        global_offsets,
        [
            *normed_specs,
            *[whole_tile] * parts,
            pl.BlockSpec((query_block, 1), lambda i, _: (late(i), 0)),
            *map(whole_block, pieces),
        ],
        [*own, *partner, *got, query_codes, *pieces],
        [(2 * rows, WIDE)],
        [pl.BlockSpec((query_block, WIDE), lambda i, _: (late(i), 0))],
        [
            (width, 2 * WIDE),
            (width, WIDE),
            (2 * all_rows, WIDE),
            (2 * rows, WIDE),
            (2 * all_rows, WIDE),
            pltpu.VMEM((1, 2 * all_rows), jnp.float32),
        ],
        2 * WIDE * (2 * all_rows * 2 * width + 2 * rows * width + 4 * rows * 2 * all_rows),
        "groups",
    )

    mine, theirs = mixed[:rows], other_core(mixed[rows:])
    result = jnp.where(
        core == 0,
        jnp.concatenate([mine, theirs], axis=1),
        jnp.concatenate([theirs, mine], axis=1),
    )
    return result.reshape(1, lat_windows, lon_windows, kept_most, inner)


def body(patches, kept_index, kept_count, embed_weight, local_qkv, local_out, global_qkv):
    args = (patches, kept_index, kept_count, embed_weight, local_qkv, local_out, global_qkv)
    windows = patches.shape[1] * patches.shape[2]
    rows = windows * kept_index.shape[3]
    sample_rows = rows * lax.axis_size("lat") * lax.axis_size("lon")
    fits = patches.shape[3] <= 256 and windows % 2 == 0 and windows * kept_index.shape[3] % 32 == 0 and sample_rows * HEADS * HD * 2 <= vmem_limit // 4
    shards = embed_weight.shape[0] * 2 == local_qkv.shape[0] == local_out.shape[0] == 2 * HD
    if lax.axis_size("batch") == 4 and lax.axis_size("lat") == HEADS // GROUP == 2 and fits and shards:
        return sample_body(*args)
    return owner_body(*args)


def solution(mesh):
    return jax.shard_map(
        body,
        mesh=mesh,
        in_specs=(
            P("batch", "lat", "lon", None, None),
            P("batch", "lat", "lon", None),
            P("batch", "lat", "lon"),
            P("batch", None),
            P("batch", None),
            P("batch", None),
            P("batch", None),
        ),
        out_specs=P("batch", "lat", "lon", None, None),
        check_vma=False,
    )
```

```python
import functools

import jax
import jax.numpy as jnp
from jax import lax
from jax.experimental import pallas as pl
from jax.experimental.pallas import tpu as pltpu
from jax.sharding import PartitionSpec as P

HEADS = 8
HD = 160


norm_eps = 1e-05
mask_floor = -1e30
vmem_limit = 60 * 1024 * 1024
exp2_scale = HD ** (-0.5) * 1.4426950408889634


def layer_norm(values):
    centre = values - jnp.mean(values, axis=-1, keepdims=True)
    spread = jnp.mean(centre * centre, axis=-1, keepdims=True)
    return centre * lax.rsqrt(spread + norm_eps)


def fold_product(left_rows, shard_rows):
    return jnp.dot(left_rows, shard_rows, preferred_element_type=jnp.float32)


def attend(query_rows, key_rows, value_rows, keep_mask):
    scores = jnp.einsum(
        "bnhd,bmhd->bhnm", query_rows, key_rows, preferred_element_type=jnp.float32
    ) * HD ** (-0.5)
    scores = jnp.where(keep_mask[:, None, None, :], scores, mask_floor)
    scores = scores - jnp.max(scores, axis=-1, keepdims=True)
    weights = jnp.exp(scores)
    probabilities = (weights / jnp.sum(weights, axis=-1, keepdims=True)).astype(jnp.bfloat16)
    blended = jnp.einsum(
        "bhnm,bmhd->bnhd", probabilities, value_rows, preferred_element_type=jnp.float32
    )
    return blended.astype(jnp.bfloat16).reshape(
        query_rows.shape[0], query_rows.shape[1], HEADS * HD
    )


def owner_work(received, flag_rows, whole_global):
    item_count = received.shape[0]
    slot_values = received.reshape(item_count, -1, received.shape[-1])
    projected = jnp.dot(
        slot_values.reshape(-1, slot_values.shape[-1]),
        whole_global,
        preferred_element_type=jnp.float32,
    )
    slot_values = projected.astype(jnp.bfloat16).reshape(item_count, -1, 3 * HEADS * HD)
    heads_split = slot_values.reshape(item_count, slot_values.shape[1], 3, HEADS, HD)
    keep_mask = flag_rows.reshape(item_count, -1) > 0
    return attend(heads_split[:, :, 0], heads_split[:, :, 1], heads_split[:, :, 2], keep_mask)


def owner_body(patches, kept_index, kept_count, embed_weight, local_qkv, local_out, global_qkv):
    lat_windows = patches.shape[1]
    lon_windows = patches.shape[2]
    windows = lat_windows * lon_windows
    window_tokens = patches.shape[3]
    kept_most = kept_index.shape[3]
    row_count = windows * kept_most
    inner_width = HEADS * HD
    patch_rows = patches.reshape(windows, window_tokens, patches.shape[4])
    index_rows = kept_index.reshape(windows, kept_most)
    kept_mask = lax.broadcasted_iota(jnp.int32, (windows, kept_most), 1) < kept_count.reshape(
        windows, 1
    )
    picked = jnp.take_along_axis(patch_rows, index_rows[:, :, None], axis=1).reshape(row_count, -1)
    embedded = fold_product(
        picked, lax.all_gather(embed_weight, "batch", axis=0, tiled=True)
    ).astype(jnp.bfloat16)
    normed = layer_norm(embedded.astype(jnp.float32)).astype(jnp.bfloat16)
    local_proj = fold_product(
        normed, lax.all_gather(local_qkv, "batch", axis=0, tiled=True)
    ).astype(jnp.bfloat16)
    local_split = local_proj.reshape(windows, kept_most, 3, HEADS, HD)
    local_mix = attend(
        local_split[:, :, 0], local_split[:, :, 1], local_split[:, :, 2], kept_mask
    ).reshape(row_count, inner_width)
    back_sum = fold_product(local_mix, lax.all_gather(local_out, "batch", axis=0, tiled=True))
    hidden = (embedded.astype(jnp.float32) + back_sum).astype(jnp.bfloat16)
    normed_global = layer_norm(hidden.astype(jnp.float32)).astype(jnp.bfloat16)
    whole_global = lax.all_gather(global_qkv, "batch", axis=0, tiled=True)
    sent_width = normed_global.shape[1]
    window_ids = lax.broadcasted_iota(jnp.int32, (windows, kept_most), 0)
    slot_rows = (
        jnp.zeros((window_tokens, windows, sent_width), jnp.bfloat16)
        .at[index_rows, window_ids]
        .set(normed_global.reshape(windows, kept_most, sent_width))
    )
    flag_slots = (
        jnp.zeros((window_tokens, windows), jnp.bfloat16)
        .at[index_rows, window_ids]
        .set(kept_mask.astype(jnp.bfloat16))
    )
    owners = lax.axis_size("lat") * lax.axis_size("lon")
    owned_count = window_tokens // owners
    blended = owner_work(
        lax.all_to_all(
            slot_rows.reshape(owned_count, owners, windows, sent_width),
            ("lat", "lon"),
            split_axis=1,
            concat_axis=2,
            tiled=True,
        ),
        lax.all_to_all(
            flag_slots.reshape(owned_count, owners, windows),
            ("lat", "lon"),
            split_axis=1,
            concat_axis=2,
            tiled=True,
        ),
        whole_global,
    )
    shaped = blended.reshape(blended.shape[0], 1, -1, inner_width)
    returned = lax.all_to_all(shaped, ("lat", "lon"), split_axis=2, concat_axis=1, tiled=True)
    out_slots = returned.reshape(window_tokens, windows, inner_width)
    gathered = out_slots[index_rows, window_ids]
    result = jnp.where(kept_mask[:, :, None], gathered, jnp.zeros_like(gathered))
    return result.reshape(1, lat_windows, lon_windows, kept_most, inner_width)


MAIN = 128
TAIL = HD - MAIN
GROUP = MAIN // TAIL
WIDE = GROUP * HD


def whole_block(array):
    zeros = (0,) * array.ndim
    return pl.BlockSpec(array.shape, lambda *_: zeros, pipeline_mode=pl.Buffered(1))


def parts_of(pieces, high):
    return [piece.at[pl.ds(at, high)] for piece in pieces for at in range(0, piece.shape[0], high)]


def first_row(offset_ref, at, unit):
    return pl.multiple_of(offset_ref[at], unit)


def reorder(source, start, target, at):
    for head in range(GROUP):
        first = start + head * HD
        target[:, pl.ds(at + head * MAIN, MAIN)] = source[:, pl.ds(first, MAIN)]
        target[:, pl.ds(at + GROUP * MAIN + head * TAIL, TAIL)] = source[:, pl.ds(first + MAIN, TAIL)]


def pick_kernel(_, patch_ref, code_ref, partner_ref, *sent_refs):
    window_tokens = patch_ref.shape[1]
    windows, kept_most = code_ref.shape
    count = windows // len(sent_refs)
    rows = count * kept_most
    offsets = lax.broadcasted_iota(jnp.int32, (window_tokens, kept_most), 0)
    for which, sent_ref in enumerate(sent_refs):
        tile = sent_ref.shape[1] - rows
        sent_ref[0, pl.ds(rows, tile), :] = jnp.zeros((tile, sent_ref.shape[2]), jnp.bfloat16)
        for at in range(count):
            window = which * count + at
            chosen = (offsets == code_ref[pl.ds(window, 1), :]).astype(jnp.float32)
            picked = lax.dot_general(
                chosen.astype(jnp.bfloat16),
                patch_ref[window],
                (((0,), (0,)), ((), ())),
                preferred_element_type=jnp.float32,
            )
            sent_ref[0, pl.ds(at * kept_most, kept_most), :] = picked.astype(jnp.bfloat16)
        part = pl.ds(which * count, count)
        codes = jnp.concatenate([code_ref[part, :], partner_ref[part, :]], axis=0)
        sent_ref[0, pl.ds(rows, 2 * count), pl.ds(0, kept_most)] = codes.astype(jnp.float32).astype(
            jnp.bfloat16
        )
        for copy in range(1, sent_ref.shape[0]):
            sent_ref[copy] = sent_ref[0]


def pack_columns(column_refs, full_ref):
    for which, column_ref in enumerate(column_refs):
        reorder(column_ref, 0, full_ref, which * WIDE)


def own_half(core_ref, full_ref, half_ref):
    half = half_ref.shape[0]
    half_ref[...] = full_ref[pl.ds(pl.multiple_of(core_ref[0] * half, 16), half), :]


def pack_first_kernel(core_ref, query_ref, key_ref, value_ref, embed_ref, full_ref, half_ref):
    pack_columns((query_ref, key_ref, value_ref), full_ref)
    quarter = half_ref.shape[0] // 2
    wide = embed_ref.shape[1] // 2
    for at in range(4):
        core, side = at // 2, at % 2
        full_ref[pl.ds(at * quarter, quarter), pl.ds(3 * WIDE, wide)] = embed_ref[
            pl.ds(core * quarter, quarter), pl.ds(side * wide, wide)
        ]
    own_half(core_ref, full_ref, half_ref)


def pack_second_kernel(core_ref, query_ref, key_ref, value_ref, out_ref, full_ref, half_ref):
    pack_columns((query_ref, key_ref, value_ref), full_ref)
    full_ref[:, pl.ds(3 * WIDE, out_ref.shape[1])] = out_ref[...]
    own_half(core_ref, full_ref, half_ref)


def prepare_global_kernel(core_ref, query_ref, key_ref, value_ref, first_ref, second_ref):
    reorder(key_ref, 0, first_ref, 0)
    reorder(query_ref, 0, first_ref, WIDE)
    reorder(value_ref, 0, second_ref, 0)


def lane_head():
    return lax.broadcasted_iota(jnp.int32, (1, MAIN), 1) // TAIL


def head_tiles(ref, rows, at, head):
    main = ref[rows, pl.ds(at + head * MAIN, MAIN)]
    tail = ref[rows, pl.ds(at + GROUP * MAIN, MAIN)]
    return main, tail


def head_query(ref, rows, at, head):
    main, tail = head_tiles(ref, rows, at, head)
    return jnp.concatenate([main, jnp.where(lane_head() == head, tail, jnp.zeros_like(tail))], axis=1)


def head_pair(ref, rows, at, head):
    return jnp.concatenate(head_tiles(ref, rows, at, head), axis=1)


def masked_scores(query, key, mask):
    scores = lax.dot_general(
        query, key, (((1,), (1,)), ((), ())), preferred_element_type=jnp.float32
    )
    return jnp.where(mask, scores, mask_floor)


def code_row(tile, at, kept_most):
    return tile[at : at + 1, :kept_most]


def mix_heads(proj_ref, code_ref, mix_ref, count, kept_most, at_once):
    rows = proj_ref.shape[0]
    own_window = lax.broadcasted_iota(jnp.int32, (at_once, 1), 0) // kept_most
    key_window = lax.broadcasted_iota(jnp.int32, (1, at_once), 1) // kept_most
    tiles = [code_ref[at].astype(jnp.float32) for at in range(code_ref.shape[0])]
    codes = [code_row(tile, at, kept_most) for tile in tiles for at in range(count)]
    for start in range(0, rows, at_once):
        part = pl.ds(start, at_once)
        first = start // kept_most
        key_codes = jnp.concatenate(codes[first : first + at_once // kept_most], axis=1)
        mask = own_window == jnp.where(key_codes >= 0, key_window, -1)
        tails = None
        for head in range(GROUP):
            scores = masked_scores(
                head_query(proj_ref, part, 0, head), head_pair(proj_ref, part, WIDE, head), mask
            )
            top = jnp.max(scores, axis=-1, keepdims=True)
            weights = jnp.exp2((scores - top) * exp2_scale)
            total = jnp.sum(weights, axis=-1, keepdims=True)
            mixed = (
                fold_product(
                    weights.astype(jnp.bfloat16), head_pair(proj_ref, part, 2 * WIDE, head)
                )
                / total
            )
            mix_ref[part, pl.ds(head * MAIN, MAIN)] = mixed[:, :MAIN].astype(jnp.bfloat16)
            tail = mixed[:, MAIN:]
            tails = tail if tails is None else jnp.where(lane_head() == head, tail, tails)
        mix_ref[part, pl.ds(GROUP * MAIN, MAIN)] = tails.astype(jnp.bfloat16)


def embed_window_kernel(
    mix,
    offset_ref,
    picked_ref,
    code_ref,
    *refs,
):
    *pieces, embedded_ref, normed_ref, mix_ref, weight_ref, embed_ref, proj_ref = refs

    @pl.when(pl.program_id(0) == 0)
    def _():
        high = pieces[0].shape[0] // 2
        quarter = high // 2
        wide = embed_ref.shape[1] // 2
        for at, part in enumerate(parts_of(pieces, high)):
            start = first_row(offset_ref, 3 * at, 32)
            weight_ref[pl.ds(start, high), :] = part[:, pl.ds(0, 3 * WIDE)]
            start = pl.multiple_of(start // 2, 16)
            for side in range(2):
                embed_ref[pl.ds(start, quarter), pl.ds(side * wide, wide)] = part[
                    pl.ds(side * quarter, quarter), pl.ds(3 * WIDE, wide)
                ]

    picked = picked_ref[...].reshape(proj_ref.shape[0], picked_ref.shape[2])
    embedded = fold_product(picked, embed_ref[...]).astype(jnp.bfloat16)
    embedded_ref[...] = embedded
    normed = layer_norm(embedded.astype(jnp.float32)).astype(jnp.bfloat16)
    normed_ref[...] = normed
    proj_ref[...] = fold_product(normed, weight_ref[...]).astype(jnp.bfloat16)
    mix(proj_ref, code_ref, mix_ref)


def window_out_kernel(
    mix,
    offset_ref,
    embedded_ref,
    normed_ref,
    mix_ref,
    code_ref,
    *refs,
):
    *pieces, result_ref, weight_ref, proj_ref, own_mix_ref, row_ref = refs

    @pl.when(pl.program_id(0) == 0)
    def _():
        wide = row_ref.shape[1]
        for at, part in enumerate(parts_of(pieces, HD)):
            weight_ref[pl.ds(first_row(offset_ref, 3 * at, 32), HD), :] = part[:, pl.ds(0, 3 * WIDE)]
            row_ref[pl.ds(first_row(offset_ref, 3 * at + 1, 32), MAIN), :] = part[
                pl.ds(0, MAIN), pl.ds(3 * WIDE, wide)
            ]
            row_ref[pl.ds(first_row(offset_ref, 3 * at + 2, 32), TAIL), :] = part[
                pl.ds(MAIN, TAIL), pl.ds(3 * WIDE, wide)
            ]

    proj_ref[...] = fold_product(normed_ref[...], weight_ref[...]).astype(jnp.bfloat16)
    mix(proj_ref, code_ref, own_mix_ref)
    hidden = embedded_ref[...].astype(jnp.float32)
    hidden += fold_product(mix_ref[...], row_ref[pl.ds(0, WIDE), :])
    hidden += fold_product(own_mix_ref[...], row_ref[pl.ds(WIDE, WIDE), :])
    hidden = hidden.astype(jnp.bfloat16).astype(jnp.float32)
    result_ref[...] = layer_norm(hidden).astype(jnp.bfloat16)


def group_kernel(steps, parts, count, kept_most, key_chunk, offset_ref, *refs):
    many = 2 * parts
    normed_refs, refs = refs[:many], refs[many:]
    tile_refs, refs = refs[:parts], refs[parts:]
    code_ref, *pieces, mixed_ref, first_ref, second_ref, key_ref, query_ref, value_ref, key_code_ref = refs
    step = pl.program_id(0)
    block = normed_refs[0].shape[0]
    query_block = mixed_ref.shape[0]
    part_rows = count * kept_most
    shared = block // part_rows

    @pl.when(step == 0)
    def _():
        for target, arrays in ((first_ref, pieces[:4]), (second_ref, pieces[4:])):
            for at, array in enumerate(arrays):
                target[pl.ds(first_row(offset_ref, at, 32), array.shape[0]), :] = array[...]
        at = 0
        for core in range(2):
            for tile_ref in tile_refs:
                for device in range(tile_ref.shape[0]):
                    tile = tile_ref[device].astype(jnp.float32)
                    for window in range(count):
                        key_code_ref[:, pl.ds(at, kept_most)] = code_row(
                            tile, core * count + window, kept_most
                        )
                        at += kept_most

    for which, normed_ref in enumerate(normed_refs):

        @pl.when((step >= which * steps) & (step < (which + 1) * steps))
        def _():
            normed = normed_ref[...]
            part = pl.ds(pl.multiple_of(step * block, 16), block)
            key_ref[part, :] = fold_product(normed, first_ref[:, pl.ds(0, WIDE)]).astype(jnp.bfloat16)
            value_ref[part, :] = fold_product(normed, second_ref[...]).astype(jnp.bfloat16)

        @pl.when(step == which * steps + offset_ref[4] // shared)
        def _():
            start = pl.multiple_of(offset_ref[4] % shared * part_rows, 16)
            query_ref[pl.ds(which * part_rows, part_rows), :] = fold_product(
                normed_ref[pl.ds(start, part_rows), :], first_ref[:, pl.ds(WIDE, WIDE)]
            ).astype(jnp.bfloat16)

    @pl.when(step >= many * steps)
    def _():
        part = pl.ds(pl.multiple_of((step - many * steps) * query_block, 16), query_block)
        codes = code_ref[...]
        key_parts = [pl.ds(at, key_chunk) for at in range(0, key_ref.shape[0], key_chunk)]
        for head in range(GROUP):
            query = head_query(query_ref, part, 0, head)
            scores = [
                masked_scores(query, head_pair(key_ref, p, 0, head), codes == key_code_ref[:, p])
                for p in key_parts
            ]
            top = functools.reduce(
                jnp.maximum, [jnp.max(s, axis=-1, keepdims=True) for s in scores]
            )
            total = 0.0
            mixed = 0.0
            for p, s in zip(key_parts, scores):
                weights = jnp.exp2((s - top) * exp2_scale)
                total += jnp.sum(weights, axis=-1, keepdims=True)
                mixed += fold_product(
                    weights.astype(jnp.bfloat16), head_pair(value_ref, p, 0, head)
                )
            mixed = jnp.where(codes >= 0, mixed / total, 0.0).astype(jnp.bfloat16)
            mixed_ref[:, pl.ds(head * HD, MAIN)] = mixed[:, :MAIN]
            at = MAIN + head * TAIL
            mixed_ref[:, pl.ds(head * HD + MAIN, TAIL)] = mixed[:, at : at + TAIL]


def swap_perm(size, mask):
    return [(i, i ^ mask) for i in range(size)]


def after(value, earlier):
    return lax.optimization_barrier((value, earlier))[0]


def run(kernel, steps, scalars, specs, arrays, outs, out_specs, scratch, flops, name):
    moved = sum(a.size * a.dtype.itemsize for a in arrays)
    return pl.pallas_call(
        kernel,
        grid_spec=pltpu.PrefetchScalarGridSpec(
            num_scalar_prefetch=1,
            grid=(steps,),
            in_specs=specs,
            out_specs=out_specs,
            scratch_shapes=[
                pltpu.VMEM(shape, jnp.bfloat16) if isinstance(shape, tuple) else shape
                for shape in scratch
            ],
        ),
        out_shape=[jax.ShapeDtypeStruct(shape, jnp.bfloat16) for shape in outs],
        compiler_params=pltpu.CompilerParams(vmem_limit_bytes=vmem_limit),
        cost_estimate=pl.CostEstimate(flops=flops, bytes_accessed=moved, transcendentals=0),
        name=name,
    )(scalars, *arrays)


def sample_body(patches, kept_index, kept_count, embed_weight, local_qkv, local_out, global_qkv):
    lat_windows, lon_windows, window_tokens, pin = patches.shape[1:]
    windows = lat_windows * lon_windows
    kept_most = kept_index.shape[3]
    rows = windows * kept_most
    inner = HEADS * HD
    width = embed_weight.shape[1]
    lon_size = lax.axis_size("lon")
    batch_size = lax.axis_size("batch")
    core = lax.axis_index("lat")
    chip = lax.axis_index("batch")
    place = lax.axis_index("lon")
    core_scalar = core.reshape(1).astype(jnp.int32)

    def other_core(value):
        return lax.ppermute(value, "lat", swap_perm(2, 1))

    diagonal = []
    for b in range(batch_size):
        diagonal += [(2 * b, 2 * (b ^ 1)), (2 * b + 1, 2 * (b ^ 2) + 1)]

    def sides(part):
        along_x = lax.ppermute(part, "batch", swap_perm(batch_size, 1))
        along_y = lax.ppermute(part, "batch", swap_perm(batch_size, 2))
        return along_x, along_y

    def across(along_x, along_y):
        forwarded = jnp.where(core == 0, along_y, along_x)
        return lax.ppermute(forwarded, ("batch", "lat"), diagonal)

    def across_of(joined):
        forwarded = lax.dynamic_slice_in_dim(joined, (1 - core) * half, half, axis=0)
        return lax.ppermute(forwarded, ("batch", "lat"), diagonal)

    high = local_qkv.shape[0]
    half = high // 2
    first_wide = 3 * WIDE + width // 2
    second_wide = 3 * WIDE + width

    def pack(kernel, group, scalar, other, wide, name):
        shapes = [(high, wide), (half, wide)]
        return run(
            kernel,
            1,
            scalar,
            [
                *[
                    pl.BlockSpec((high, WIDE), lambda i, c, at=2 * which + group: (0, at))
                    for which in range(3)
                ],
                whole_block(other),
            ],
            [local_qkv] * 3 + [other],
            shapes,
            [pl.BlockSpec(shape, lambda *_: (0, 0)) for shape in shapes],
            [],
            0,
            name,
        )

    local_first, half_first = pack(
        pack_first_kernel, 0, core_scalar, embed_weight, first_wide, "pack_first"
    )

    parts = 1
    count = windows // parts
    part_rows = count * kept_most
    code_tile = -(-2 * count // 16) * 16
    sent_shape = (lon_size, part_rows + code_tile, pin)
    patch_rows = patches.reshape(windows, window_tokens, pin)
    kept_mask = lax.broadcasted_iota(jnp.int32, (windows, kept_most), 1) < kept_count.reshape(
        windows, 1
    )
    codes = jnp.where(kept_mask, kept_index.reshape(windows, kept_most), -1)
    partner_codes = other_core(codes)
    query_codes = jnp.concatenate([codes, partner_codes], axis=0).astype(jnp.float32)
    query_codes = query_codes.reshape(2 * rows, 1)
    global_starts = [(chip ^ which) * high for which in range(4)]
    global_offsets = jnp.stack([*global_starts, place]).astype(jnp.int32)
    sent = run(
        pick_kernel,
        1,
        after(core_scalar, half_first),
        [whole_block(patch_rows), whole_block(codes), whole_block(partner_codes)],
        [patch_rows, codes, partner_codes],
        [sent_shape] * parts,
        [pl.BlockSpec(sent_shape, lambda *_: (0, 0, 0))] * parts,
        [],
        0,
        "pick",
    )
    query_codes, global_offsets = after((query_codes, global_offsets), sent)
    got = []
    for value in sent:
        value = after(value, got[-1]) if got else value
        got.append(lax.all_to_all(value, "lon", 0, 0, tiled=True))

    local_second, half_second = pack(
        pack_second_kernel, 1, after(core_scalar, sent), local_out, second_wide, "pack_second"
    )
    global_first, global_second = run(
        prepare_global_kernel,
        1,
        after(core_scalar, half_second),
        [
            pl.BlockSpec((high, WIDE), lambda i, c, which=which: (0, 2 * which + c[0]))
            for which in range(3)
        ],
        [global_qkv] * 3,
        [(high, 2 * WIDE), (high, WIDE)],
        [pl.BlockSpec((high, w), lambda *_: (0, 0)) for w in (2 * WIDE, WIDE)],
        [],
        0,
        "order_global",
    )
    sides_first = sides(half_first)
    sides_first = after(sides_first, (sent, global_first))
    sides_second = sides(after(half_second, sides_first))
    joined_first = lax.optimization_barrier(jnp.concatenate(sides_first, axis=0))
    across_first = across_of(joined_first)
    global_sides = sides(after(global_first, sides_second))
    joined_second = lax.optimization_barrier(jnp.concatenate(sides_second, axis=0))
    across_second = across_of(joined_second)

    def shared(shard, joined, diagonal_part, earlier):
        pieces = [shard, joined, other_core(joined), diagonal_part]
        pieces.append(other_core(after(diagonal_part, earlier)))
        bases = [(chip ^ which) * high for which in (1, 2, 3)]
        firsts = [chip * high, chip * high + half]
        for group in (bases[:2], bases[2:]):
            firsts += [base + core * half for base in group]
            firsts += [base + (1 - core) * half for base in group]
        firsts = jnp.stack(firsts).astype(jnp.int32)
        head = firsts // HD
        group_start = head // GROUP * WIDE
        main = group_start + head % GROUP * MAIN
        tail = group_start + GROUP * MAIN + head % GROUP * TAIL
        return pieces, jnp.stack([firsts, main, tail], axis=1).reshape(-1)

    shared_by = 1
    block = shared_by * part_rows
    steps = lon_size // shared_by
    many_rows = lon_size * part_rows
    at_once = 2 * kept_most if block % (2 * kept_most) == 0 else kept_most
    mix = functools.partial(mix_heads, count=count, kept_most=kept_most, at_once=at_once)
    row_spec = lambda wide: pl.BlockSpec((block, wide), lambda i, _: (i, 0))
    tile_spec = pl.BlockSpec((shared_by, code_tile, MAIN), lambda i, _: (i, part_rows // code_tile, 0))

    pieces, offsets = shared(local_first, joined_first, across_first, core_scalar)
    embedded, normed, mixes = [], [], []
    for which in range(parts):
        if which == parts - 1:
            pieces = after(pieces, (joined_second, mixes))
        result = run(
            functools.partial(embed_window_kernel, mix),
            steps,
            offsets,
            [
                pl.BlockSpec((shared_by, part_rows, pin), lambda i, _: (i, 0, 0)),
                tile_spec,
                *map(whole_block, pieces),
            ],
            [got[which], got[which], *pieces],
            [(many_rows, width), (many_rows, width), (many_rows, WIDE)],
            [row_spec(width), row_spec(width), row_spec(WIDE)],
            [(width, 3 * WIDE), (pin, width), (block, 3 * WIDE)],
            2 * many_rows * (pin * width + width * 3 * WIDE),
            "embed_windows",
        )
        for values, value in zip((embedded, normed, mixes), result):
            values.append(value)

    pieces, offsets = shared(local_second, joined_second, across_second, mixes[0])
    own, partner = [], []
    for which in range(parts):
        if which == parts - 1:
            pieces = after(pieces, (global_sides, own))
            global_sides, _ = after((global_sides, 0), own or mixes)
            global_across = across(*global_sides)
            value_sides = sides(after(global_second, global_sides))
        (result,) = run(
            functools.partial(window_out_kernel, mix),
            steps,
            offsets,
            [row_spec(width), row_spec(width), row_spec(WIDE), tile_spec, *map(whole_block, pieces)],
            [embedded[which], normed[which], mixes[which], got[which], *pieces],
            [(many_rows, width)],
            [row_spec(width)],
            [(width, 3 * WIDE), (block, 3 * WIDE), (block, WIDE), (inner, width)],
            2 * many_rows * (inner * width + width * 3 * WIDE),
            "windows_out",
        )
        own.append(result)
        if which == parts - 1:
            result = after(result, (global_across, value_sides))
        partner.append(other_core(result))
    value_across = across(*value_sides)

    all_rows = lon_size * rows
    query_block = 256 if (2 * rows) % 256 == 0 else 2 * rows
    query_steps = 2 * rows // query_block
    project_steps = 2 * parts * steps
    pieces = [global_first, *global_sides, global_across, global_second, *value_sides, value_across]
    key_chunk = 512 if (2 * all_rows) % 512 == 0 else block
    late = lambda i: jnp.clip(i - project_steps, 0, query_steps - 1)
    normed_specs = [
        pl.BlockSpec((block, width), lambda i, _, at=at: (jnp.clip(i - at * steps, 0, steps - 1), 0))
        for at in range(2 * parts)
    ]
    whole_tile = pl.BlockSpec(
        (lon_size, code_tile, MAIN), lambda *_: (0, part_rows // code_tile, 0)
    )
    (mixed,) = run(
        functools.partial(group_kernel, steps, parts, count, kept_most, key_chunk),
        project_steps + query_steps,
        global_offsets,
        [
            *normed_specs,
            *[whole_tile] * parts,
            pl.BlockSpec((query_block, 1), lambda i, _: (late(i), 0)),
            *map(whole_block, pieces),
        ],
        [*own, *partner, *got, query_codes, *pieces],
        [(2 * rows, WIDE)],
        [pl.BlockSpec((query_block, WIDE), lambda i, _: (late(i), 0))],
        [
            (width, 2 * WIDE),
            (width, WIDE),
            (2 * all_rows, WIDE),
            (2 * rows, WIDE),
            (2 * all_rows, WIDE),
            pltpu.VMEM((1, 2 * all_rows), jnp.float32),
        ],
        2 * WIDE * (2 * all_rows * 2 * width + 2 * rows * width + 4 * rows * 2 * all_rows),
        "groups",
    )

    mine, theirs = mixed[:rows], other_core(mixed[rows:])
    result = jnp.where(
        core == 0,
        jnp.concatenate([mine, theirs], axis=1),
        jnp.concatenate([theirs, mine], axis=1),
    )
    return result.reshape(1, lat_windows, lon_windows, kept_most, inner)


def body(patches, kept_index, kept_count, embed_weight, local_qkv, local_out, global_qkv):
    args = (patches, kept_index, kept_count, embed_weight, local_qkv, local_out, global_qkv)
    windows = patches.shape[1] * patches.shape[2]
    rows = windows * kept_index.shape[3]
    sample_rows = rows * lax.axis_size("lat") * lax.axis_size("lon")
    fits = patches.shape[3] <= 256 and windows % 2 == 0 and windows * kept_index.shape[3] % 32 == 0 and sample_rows * HEADS * HD * 2 <= vmem_limit // 4
    shards = embed_weight.shape[0] * 2 == local_qkv.shape[0] == local_out.shape[0] == 2 * HD
    if lax.axis_size("batch") == 4 and lax.axis_size("lat") == HEADS // GROUP == 2 and fits and shards:
        return sample_body(*args)
    return owner_body(*args)


def solution(mesh):
    return jax.shard_map(
        body,
        mesh=mesh,
        in_specs=(
            P("batch", "lat", "lon", None, None),
            P("batch", "lat", "lon", None),
            P("batch", "lat", "lon"),
            P("batch", None),
            P("batch", None),
            P("batch", None),
            P("batch", None),
        ),
        out_specs=P("batch", "lat", "lon", None, None),
        check_vma=False,
    )
```

```python
import functools

import jax
import jax.numpy as jnp
from jax import lax
from jax.experimental import pallas as pl
from jax.experimental.pallas import tpu as pltpu
from jax.sharding import PartitionSpec as P

HEADS = 8
HD = 160


norm_eps = 1e-05
mask_floor = -1e30
vmem_limit = 60 * 1024 * 1024
exp2_scale = HD ** (-0.5) * 1.4426950408889634


def layer_norm(values):
    centre = values - jnp.mean(values, axis=-1, keepdims=True)
    spread = jnp.mean(centre * centre, axis=-1, keepdims=True)
    return centre * lax.rsqrt(spread + norm_eps)


def fold_product(left_rows, shard_rows):
    return jnp.dot(left_rows, shard_rows, preferred_element_type=jnp.float32)


def attend(query_rows, key_rows, value_rows, keep_mask):
    scores = jnp.einsum(
        "bnhd,bmhd->bhnm", query_rows, key_rows, preferred_element_type=jnp.float32
    ) * HD ** (-0.5)
    scores = jnp.where(keep_mask[:, None, None, :], scores, mask_floor)
    scores = scores - jnp.max(scores, axis=-1, keepdims=True)
    weights = jnp.exp(scores)
    probabilities = (weights / jnp.sum(weights, axis=-1, keepdims=True)).astype(jnp.bfloat16)
    blended = jnp.einsum(
        "bhnm,bmhd->bnhd", probabilities, value_rows, preferred_element_type=jnp.float32
    )
    return blended.astype(jnp.bfloat16).reshape(
        query_rows.shape[0], query_rows.shape[1], HEADS * HD
    )


def owner_work(received, flag_rows, whole_global):
    item_count = received.shape[0]
    slot_values = received.reshape(item_count, -1, received.shape[-1])
    projected = jnp.dot(
        slot_values.reshape(-1, slot_values.shape[-1]),
        whole_global,
        preferred_element_type=jnp.float32,
    )
    slot_values = projected.astype(jnp.bfloat16).reshape(item_count, -1, 3 * HEADS * HD)
    heads_split = slot_values.reshape(item_count, slot_values.shape[1], 3, HEADS, HD)
    keep_mask = flag_rows.reshape(item_count, -1) > 0
    return attend(heads_split[:, :, 0], heads_split[:, :, 1], heads_split[:, :, 2], keep_mask)


def owner_body(patches, kept_index, kept_count, embed_weight, local_qkv, local_out, global_qkv):
    lat_windows = patches.shape[1]
    lon_windows = patches.shape[2]
    windows = lat_windows * lon_windows
    window_tokens = patches.shape[3]
    kept_most = kept_index.shape[3]
    row_count = windows * kept_most
    inner_width = HEADS * HD
    patch_rows = patches.reshape(windows, window_tokens, patches.shape[4])
    index_rows = kept_index.reshape(windows, kept_most)
    kept_mask = lax.broadcasted_iota(jnp.int32, (windows, kept_most), 1) < kept_count.reshape(
        windows, 1
    )
    picked = jnp.take_along_axis(patch_rows, index_rows[:, :, None], axis=1).reshape(row_count, -1)
    embedded = fold_product(
        picked, lax.all_gather(embed_weight, "batch", axis=0, tiled=True)
    ).astype(jnp.bfloat16)
    normed = layer_norm(embedded.astype(jnp.float32)).astype(jnp.bfloat16)
    local_proj = fold_product(
        normed, lax.all_gather(local_qkv, "batch", axis=0, tiled=True)
    ).astype(jnp.bfloat16)
    local_split = local_proj.reshape(windows, kept_most, 3, HEADS, HD)
    local_mix = attend(
        local_split[:, :, 0], local_split[:, :, 1], local_split[:, :, 2], kept_mask
    ).reshape(row_count, inner_width)
    back_sum = fold_product(local_mix, lax.all_gather(local_out, "batch", axis=0, tiled=True))
    hidden = (embedded.astype(jnp.float32) + back_sum).astype(jnp.bfloat16)
    normed_global = layer_norm(hidden.astype(jnp.float32)).astype(jnp.bfloat16)
    whole_global = lax.all_gather(global_qkv, "batch", axis=0, tiled=True)
    sent_width = normed_global.shape[1]
    window_ids = lax.broadcasted_iota(jnp.int32, (windows, kept_most), 0)
    slot_rows = (
        jnp.zeros((window_tokens, windows, sent_width), jnp.bfloat16)
        .at[index_rows, window_ids]
        .set(normed_global.reshape(windows, kept_most, sent_width))
    )
    flag_slots = (
        jnp.zeros((window_tokens, windows), jnp.bfloat16)
        .at[index_rows, window_ids]
        .set(kept_mask.astype(jnp.bfloat16))
    )
    owners = lax.axis_size("lat") * lax.axis_size("lon")
    owned_count = window_tokens // owners
    blended = owner_work(
        lax.all_to_all(
            slot_rows.reshape(owned_count, owners, windows, sent_width),
            ("lat", "lon"),
            split_axis=1,
            concat_axis=2,
            tiled=True,
        ),
        lax.all_to_all(
            flag_slots.reshape(owned_count, owners, windows),
            ("lat", "lon"),
            split_axis=1,
            concat_axis=2,
            tiled=True,
        ),
        whole_global,
    )
    shaped = blended.reshape(blended.shape[0], 1, -1, inner_width)
    returned = lax.all_to_all(shaped, ("lat", "lon"), split_axis=2, concat_axis=1, tiled=True)
    out_slots = returned.reshape(window_tokens, windows, inner_width)
    gathered = out_slots[index_rows, window_ids]
    result = jnp.where(kept_mask[:, :, None], gathered, jnp.zeros_like(gathered))
    return result.reshape(1, lat_windows, lon_windows, kept_most, inner_width)


MAIN = 128
TAIL = HD - MAIN
GROUP = MAIN // TAIL
WIDE = GROUP * HD


def whole_block(array):
    zeros = (0,) * array.ndim
    return pl.BlockSpec(array.shape, lambda *_: zeros, pipeline_mode=pl.Buffered(1))


def parts_of(pieces, high):
    return [piece.at[pl.ds(at, high)] for piece in pieces for at in range(0, piece.shape[0], high)]


def first_row(offset_ref, at, unit):
    return pl.multiple_of(offset_ref[at], unit)


def reorder(source, start, target, at):
    for head in range(GROUP):
        first = start + head * HD
        target[:, pl.ds(at + head * MAIN, MAIN)] = source[:, pl.ds(first, MAIN)]
        target[:, pl.ds(at + GROUP * MAIN + head * TAIL, TAIL)] = source[:, pl.ds(first + MAIN, TAIL)]


def pick_kernel(_, patch_ref, code_ref, partner_ref, *sent_refs):
    window_tokens = patch_ref.shape[1]
    windows, kept_most = code_ref.shape
    count = windows // len(sent_refs)
    rows = count * kept_most
    offsets = lax.broadcasted_iota(jnp.int32, (window_tokens, kept_most), 0)
    for which, sent_ref in enumerate(sent_refs):
        tile = sent_ref.shape[1] - rows
        sent_ref[0, pl.ds(rows, tile), :] = jnp.zeros((tile, sent_ref.shape[2]), jnp.bfloat16)
        for at in range(count):
            window = which * count + at
            chosen = (offsets == code_ref[pl.ds(window, 1), :]).astype(jnp.float32)
            picked = lax.dot_general(
                chosen.astype(jnp.bfloat16),
                patch_ref[window],
                (((0,), (0,)), ((), ())),
                preferred_element_type=jnp.float32,
            )
            sent_ref[0, pl.ds(at * kept_most, kept_most), :] = picked.astype(jnp.bfloat16)
        part = pl.ds(which * count, count)
        codes = jnp.concatenate([code_ref[part, :], partner_ref[part, :]], axis=0)
        sent_ref[0, pl.ds(rows, 2 * count), pl.ds(0, kept_most)] = codes.astype(jnp.float32).astype(
            jnp.bfloat16
        )
        for copy in range(1, sent_ref.shape[0]):
            sent_ref[copy] = sent_ref[0]


def pack_columns(column_refs, full_ref):
    for which, column_ref in enumerate(column_refs):
        reorder(column_ref, 0, full_ref, which * WIDE)


def own_half(core_ref, full_ref, half_ref):
    half = half_ref.shape[0]
    half_ref[...] = full_ref[pl.ds(pl.multiple_of(core_ref[0] * half, 16), half), :]


def pack_first_kernel(core_ref, query_ref, key_ref, value_ref, embed_ref, full_ref, half_ref):
    pack_columns((query_ref, key_ref, value_ref), full_ref)
    quarter = half_ref.shape[0] // 2
    wide = embed_ref.shape[1] // 2
    for at in range(4):
        core, side = at // 2, at % 2
        full_ref[pl.ds(at * quarter, quarter), pl.ds(3 * WIDE, wide)] = embed_ref[
            pl.ds(core * quarter, quarter), pl.ds(side * wide, wide)
        ]
    own_half(core_ref, full_ref, half_ref)


def pack_second_kernel(core_ref, query_ref, key_ref, value_ref, out_ref, full_ref, half_ref):
    pack_columns((query_ref, key_ref, value_ref), full_ref)
    full_ref[:, pl.ds(3 * WIDE, out_ref.shape[1])] = out_ref[...]
    own_half(core_ref, full_ref, half_ref)


def prepare_global_kernel(core_ref, query_ref, key_ref, value_ref, first_ref, second_ref):
    reorder(key_ref, 0, first_ref, 0)
    reorder(query_ref, 0, first_ref, WIDE)
    reorder(value_ref, 0, second_ref, 0)


def lane_head():
    return lax.broadcasted_iota(jnp.int32, (1, MAIN), 1) // TAIL


def head_tiles(ref, rows, at, head):
    main = ref[rows, pl.ds(at + head * MAIN, MAIN)]
    tail = ref[rows, pl.ds(at + GROUP * MAIN, MAIN)]
    return main, tail


def head_query(ref, rows, at, head):
    main, tail = head_tiles(ref, rows, at, head)
    return jnp.concatenate([main, jnp.where(lane_head() == head, tail, jnp.zeros_like(tail))], axis=1)


def head_pair(ref, rows, at, head):
    return jnp.concatenate(head_tiles(ref, rows, at, head), axis=1)


def masked_scores(query, key, mask):
    scores = lax.dot_general(
        query, key, (((1,), (1,)), ((), ())), preferred_element_type=jnp.float32
    )
    return jnp.where(mask, scores, mask_floor)


def code_row(tile, at, kept_most):
    return tile[at : at + 1, :kept_most]


def mix_heads(proj_ref, code_ref, mix_ref, count, kept_most, at_once):
    rows = proj_ref.shape[0]
    own_window = lax.broadcasted_iota(jnp.int32, (at_once, 1), 0) // kept_most
    key_window = lax.broadcasted_iota(jnp.int32, (1, at_once), 1) // kept_most
    tiles = [code_ref[at].astype(jnp.float32) for at in range(code_ref.shape[0])]
    codes = [code_row(tile, at, kept_most) for tile in tiles for at in range(count)]
    for start in range(0, rows, at_once):
        part = pl.ds(start, at_once)
        first = start // kept_most
        key_codes = jnp.concatenate(codes[first : first + at_once // kept_most], axis=1)
        mask = own_window == jnp.where(key_codes >= 0, key_window, -1)
        tails = None
        for head in range(GROUP):
            scores = masked_scores(
                head_query(proj_ref, part, 0, head), head_pair(proj_ref, part, WIDE, head), mask
            )
            top = jnp.max(scores, axis=-1, keepdims=True)
            weights = jnp.exp2((scores - top) * exp2_scale)
            total = jnp.sum(weights, axis=-1, keepdims=True)
            mixed = (
                fold_product(
                    weights.astype(jnp.bfloat16), head_pair(proj_ref, part, 2 * WIDE, head)
                )
                / total
            )
            mix_ref[part, pl.ds(head * MAIN, MAIN)] = mixed[:, :MAIN].astype(jnp.bfloat16)
            tail = mixed[:, MAIN:]
            tails = tail if tails is None else jnp.where(lane_head() == head, tail, tails)
        mix_ref[part, pl.ds(GROUP * MAIN, MAIN)] = tails.astype(jnp.bfloat16)


def embed_window_kernel(
    mix,
    offset_ref,
    picked_ref,
    code_ref,
    *refs,
):
    *pieces, embedded_ref, normed_ref, mix_ref, weight_ref, embed_ref, proj_ref = refs

    @pl.when(pl.program_id(0) == 0)
    def _():
        high = pieces[0].shape[0] // 2
        quarter = high // 2
        wide = embed_ref.shape[1] // 2
        for at, part in enumerate(parts_of(pieces, high)):
            start = first_row(offset_ref, 3 * at, 32)
            weight_ref[pl.ds(start, high), :] = part[:, pl.ds(0, 3 * WIDE)]
            start = pl.multiple_of(start // 2, 16)
            for side in range(2):
                embed_ref[pl.ds(start, quarter), pl.ds(side * wide, wide)] = part[
                    pl.ds(side * quarter, quarter), pl.ds(3 * WIDE, wide)
                ]

    picked = picked_ref[...].reshape(proj_ref.shape[0], picked_ref.shape[2])
    embedded = fold_product(picked, embed_ref[...]).astype(jnp.bfloat16)
    embedded_ref[...] = embedded
    normed = layer_norm(embedded.astype(jnp.float32)).astype(jnp.bfloat16)
    normed_ref[...] = normed
    proj_ref[...] = fold_product(normed, weight_ref[...]).astype(jnp.bfloat16)
    mix(proj_ref, code_ref, mix_ref)


def window_out_kernel(
    mix,
    offset_ref,
    embedded_ref,
    normed_ref,
    mix_ref,
    code_ref,
    *refs,
):
    *pieces, result_ref, weight_ref, proj_ref, own_mix_ref, row_ref = refs

    @pl.when(pl.program_id(0) == 0)
    def _():
        wide = row_ref.shape[1]
        for at, part in enumerate(parts_of(pieces, HD)):
            weight_ref[pl.ds(first_row(offset_ref, 3 * at, 32), HD), :] = part[:, pl.ds(0, 3 * WIDE)]
            row_ref[pl.ds(first_row(offset_ref, 3 * at + 1, 32), MAIN), :] = part[
                pl.ds(0, MAIN), pl.ds(3 * WIDE, wide)
            ]
            row_ref[pl.ds(first_row(offset_ref, 3 * at + 2, 32), TAIL), :] = part[
                pl.ds(MAIN, TAIL), pl.ds(3 * WIDE, wide)
            ]

    proj_ref[...] = fold_product(normed_ref[...], weight_ref[...]).astype(jnp.bfloat16)
    mix(proj_ref, code_ref, own_mix_ref)
    hidden = embedded_ref[...].astype(jnp.float32)
    hidden += fold_product(mix_ref[...], row_ref[pl.ds(0, WIDE), :])
    hidden += fold_product(own_mix_ref[...], row_ref[pl.ds(WIDE, WIDE), :])
    hidden = hidden.astype(jnp.bfloat16).astype(jnp.float32)
    result_ref[...] = layer_norm(hidden).astype(jnp.bfloat16)


def group_kernel(steps, parts, count, kept_most, key_chunk, offset_ref, *refs):
    many = 2 * parts
    normed_refs, refs = refs[:many], refs[many:]
    tile_refs, refs = refs[:parts], refs[parts:]
    code_ref, *pieces, mixed_ref, first_ref, second_ref, key_ref, query_ref, value_ref, key_code_ref = refs
    step = pl.program_id(0)
    block = normed_refs[0].shape[0]
    query_block = mixed_ref.shape[0]
    part_rows = count * kept_most
    shared = block // part_rows

    @pl.when(step == 0)
    def _():
        for target, arrays in ((first_ref, pieces[:4]), (second_ref, pieces[4:])):
            for at, array in enumerate(arrays):
                target[pl.ds(first_row(offset_ref, at, 32), array.shape[0]), :] = array[...]
        at = 0
        for core in range(2):
            for tile_ref in tile_refs:
                for device in range(tile_ref.shape[0]):
                    tile = tile_ref[device].astype(jnp.float32)
                    for window in range(count):
                        key_code_ref[:, pl.ds(at, kept_most)] = code_row(
                            tile, core * count + window, kept_most
                        )
                        at += kept_most

    for which, normed_ref in enumerate(normed_refs):

        @pl.when((step >= which * steps) & (step < (which + 1) * steps))
        def _():
            normed = normed_ref[...]
            part = pl.ds(pl.multiple_of(step * block, 16), block)
            key_ref[part, :] = fold_product(normed, first_ref[:, pl.ds(0, WIDE)]).astype(jnp.bfloat16)
            value_ref[part, :] = fold_product(normed, second_ref[...]).astype(jnp.bfloat16)

        @pl.when(step == which * steps + offset_ref[4] // shared)
        def _():
            start = pl.multiple_of(offset_ref[4] % shared * part_rows, 16)
            query_ref[pl.ds(which * part_rows, part_rows), :] = fold_product(
                normed_ref[pl.ds(start, part_rows), :], first_ref[:, pl.ds(WIDE, WIDE)]
            ).astype(jnp.bfloat16)

    @pl.when(step >= many * steps)
    def _():
        part = pl.ds(pl.multiple_of((step - many * steps) * query_block, 16), query_block)
        codes = code_ref[...]
        key_parts = [pl.ds(at, key_chunk) for at in range(0, key_ref.shape[0], key_chunk)]
        for head in range(GROUP):
            query = head_query(query_ref, part, 0, head)
            scores = [
                masked_scores(query, head_pair(key_ref, p, 0, head), codes == key_code_ref[:, p])
                for p in key_parts
            ]
            top = functools.reduce(
                jnp.maximum, [jnp.max(s, axis=-1, keepdims=True) for s in scores]
            )
            total = 0.0
            mixed = 0.0
            for p, s in zip(key_parts, scores):
                weights = jnp.exp2((s - top) * exp2_scale)
                total += jnp.sum(weights, axis=-1, keepdims=True)
                mixed += fold_product(
                    weights.astype(jnp.bfloat16), head_pair(value_ref, p, 0, head)
                )
            mixed = jnp.where(codes >= 0, mixed / total, 0.0).astype(jnp.bfloat16)
            mixed_ref[:, pl.ds(head * HD, MAIN)] = mixed[:, :MAIN]
            at = MAIN + head * TAIL
            mixed_ref[:, pl.ds(head * HD + MAIN, TAIL)] = mixed[:, at : at + TAIL]


def swap_perm(size, mask):
    return [(i, i ^ mask) for i in range(size)]


def after(value, earlier):
    return lax.optimization_barrier((value, earlier))[0]


def run(kernel, steps, scalars, specs, arrays, outs, out_specs, scratch, flops, name):
    moved = sum(a.size * a.dtype.itemsize for a in arrays)
    return pl.pallas_call(
        kernel,
        grid_spec=pltpu.PrefetchScalarGridSpec(
            num_scalar_prefetch=1,
            grid=(steps,),
            in_specs=specs,
            out_specs=out_specs,
            scratch_shapes=[
                pltpu.VMEM(shape, jnp.bfloat16) if isinstance(shape, tuple) else shape
                for shape in scratch
            ],
        ),
        out_shape=[jax.ShapeDtypeStruct(shape, jnp.bfloat16) for shape in outs],
        compiler_params=pltpu.CompilerParams(vmem_limit_bytes=vmem_limit),
        cost_estimate=pl.CostEstimate(flops=flops, bytes_accessed=moved if flops else 0, transcendentals=0),
        name=name,
    )(scalars, *arrays)


def sample_body(patches, kept_index, kept_count, embed_weight, local_qkv, local_out, global_qkv):
    lat_windows, lon_windows, window_tokens, pin = patches.shape[1:]
    windows = lat_windows * lon_windows
    kept_most = kept_index.shape[3]
    rows = windows * kept_most
    inner = HEADS * HD
    width = embed_weight.shape[1]
    lon_size = lax.axis_size("lon")
    batch_size = lax.axis_size("batch")
    core = lax.axis_index("lat")
    chip = lax.axis_index("batch")
    place = lax.axis_index("lon")
    core_scalar = core.reshape(1).astype(jnp.int32)

    def other_core(value):
        return lax.ppermute(value, "lat", swap_perm(2, 1))

    diagonal = []
    for b in range(batch_size):
        diagonal += [(2 * b, 2 * (b ^ 1)), (2 * b + 1, 2 * (b ^ 2) + 1)]

    def sides(part):
        along_x = lax.ppermute(part, "batch", swap_perm(batch_size, 1))
        along_y = lax.ppermute(part, "batch", swap_perm(batch_size, 2))
        return along_x, along_y

    def across(along_x, along_y):
        forwarded = jnp.where(core == 0, along_y, along_x)
        return lax.ppermute(forwarded, ("batch", "lat"), diagonal)

    def across_of(joined):
        forwarded = lax.dynamic_slice_in_dim(joined, (1 - core) * half, half, axis=0)
        return lax.ppermute(forwarded, ("batch", "lat"), diagonal)

    high = local_qkv.shape[0]
    half = high // 2
    first_wide = 3 * WIDE + width // 2
    second_wide = 3 * WIDE + width

    def pack(kernel, group, scalar, other, wide, name):
        shapes = [(high, wide), (half, wide)]
        return run(
            kernel,
            1,
            scalar,
            [
                *[
                    pl.BlockSpec((high, WIDE), lambda i, c, at=2 * which + group: (0, at))
                    for which in range(3)
                ],
                whole_block(other),
            ],
            [local_qkv] * 3 + [other],
            shapes,
            [pl.BlockSpec(shape, lambda *_: (0, 0)) for shape in shapes],
            [],
            0,
            name,
        )

    local_first, half_first = pack(
        pack_first_kernel, 0, core_scalar, embed_weight, first_wide, "pack_first"
    )

    parts = 1
    count = windows // parts
    part_rows = count * kept_most
    code_tile = -(-2 * count // 16) * 16
    sent_shape = (lon_size, part_rows + code_tile, pin)
    patch_rows = patches.reshape(windows, window_tokens, pin)
    kept_mask = lax.broadcasted_iota(jnp.int32, (windows, kept_most), 1) < kept_count.reshape(
        windows, 1
    )
    codes = jnp.where(kept_mask, kept_index.reshape(windows, kept_most), -1)
    partner_codes = other_core(codes)
    query_codes = jnp.concatenate([codes, partner_codes], axis=0).astype(jnp.float32)
    query_codes = query_codes.reshape(2 * rows, 1)
    global_starts = [(chip ^ which) * high for which in range(4)]
    global_offsets = jnp.stack([*global_starts, place]).astype(jnp.int32)
    sent = run(
        pick_kernel,
        1,
        after(core_scalar, half_first),
        [whole_block(patch_rows), whole_block(codes), whole_block(partner_codes)],
        [patch_rows, codes, partner_codes],
        [sent_shape] * parts,
        [pl.BlockSpec(sent_shape, lambda *_: (0, 0, 0))] * parts,
        [],
        0,
        "pick",
    )
    query_codes, global_offsets = after((query_codes, global_offsets), sent)
    got = []
    for value in sent:
        value = after(value, got[-1]) if got else value
        got.append(lax.all_to_all(value, "lon", 0, 0, tiled=True))

    local_second, half_second = pack(
        pack_second_kernel, 1, after(core_scalar, sent), local_out, second_wide, "pack_second"
    )
    global_first, global_second = run(
        prepare_global_kernel,
        1,
        after(core_scalar, half_second),
        [
            pl.BlockSpec((high, WIDE), lambda i, c, which=which: (0, 2 * which + c[0]))
            for which in range(3)
        ],
        [global_qkv] * 3,
        [(high, 2 * WIDE), (high, WIDE)],
        [pl.BlockSpec((high, w), lambda *_: (0, 0)) for w in (2 * WIDE, WIDE)],
        [],
        0,
        "order_global",
    )
    sides_first = sides(half_first)
    sides_first = after(sides_first, (sent, global_first))
    sides_second = sides(after(half_second, sides_first))
    joined_first = lax.optimization_barrier(jnp.concatenate(sides_first, axis=0))
    across_first = across_of(joined_first)
    global_sides = sides(after(global_first, sides_second))
    joined_second = lax.optimization_barrier(jnp.concatenate(sides_second, axis=0))
    across_second = across_of(joined_second)

    def shared(shard, joined, diagonal_part, earlier):
        pieces = [shard, joined, other_core(joined), diagonal_part]
        pieces.append(other_core(after(diagonal_part, earlier)))
        bases = [(chip ^ which) * high for which in (1, 2, 3)]
        firsts = [chip * high, chip * high + half]
        for group in (bases[:2], bases[2:]):
            firsts += [base + core * half for base in group]
            firsts += [base + (1 - core) * half for base in group]
        firsts = jnp.stack(firsts).astype(jnp.int32)
        head = firsts // HD
        group_start = head // GROUP * WIDE
        main = group_start + head % GROUP * MAIN
        tail = group_start + GROUP * MAIN + head % GROUP * TAIL
        return pieces, jnp.stack([firsts, main, tail], axis=1).reshape(-1)

    shared_by = 1
    block = shared_by * part_rows
    steps = lon_size // shared_by
    many_rows = lon_size * part_rows
    at_once = 2 * kept_most if block % (2 * kept_most) == 0 else kept_most
    mix = functools.partial(mix_heads, count=count, kept_most=kept_most, at_once=at_once)
    row_spec = lambda wide: pl.BlockSpec((block, wide), lambda i, _: (i, 0))
    tile_spec = pl.BlockSpec((shared_by, code_tile, MAIN), lambda i, _: (i, part_rows // code_tile, 0))

    pieces, offsets = shared(local_first, joined_first, across_first, core_scalar)
    embedded, normed, mixes = [], [], []
    for which in range(parts):
        if which == parts - 1:
            pieces = after(pieces, (joined_second, mixes))
        result = run(
            functools.partial(embed_window_kernel, mix),
            steps,
            offsets,
            [
                pl.BlockSpec((shared_by, part_rows, pin), lambda i, _: (i, 0, 0)),
                tile_spec,
                *map(whole_block, pieces),
            ],
            [got[which], got[which], *pieces],
            [(many_rows, width), (many_rows, width), (many_rows, WIDE)],
            [row_spec(width), row_spec(width), row_spec(WIDE)],
            [(width, 3 * WIDE), (pin, width), (block, 3 * WIDE)],
            0,
            "embed_windows",
        )
        for values, value in zip((embedded, normed, mixes), result):
            values.append(value)

    pieces, offsets = shared(local_second, joined_second, across_second, mixes[0])
    own, partner = [], []
    for which in range(parts):
        if which == parts - 1:
            pieces = after(pieces, (global_sides, own))
            global_sides, _ = after((global_sides, 0), own or mixes)
            global_across = across(*global_sides)
            value_sides = sides(after(global_second, global_sides))
        (result,) = run(
            functools.partial(window_out_kernel, mix),
            steps,
            offsets,
            [row_spec(width), row_spec(width), row_spec(WIDE), tile_spec, *map(whole_block, pieces)],
            [embedded[which], normed[which], mixes[which], got[which], *pieces],
            [(many_rows, width)],
            [row_spec(width)],
            [(width, 3 * WIDE), (block, 3 * WIDE), (block, WIDE), (inner, width)],
            2 * many_rows * (inner * width + width * 3 * WIDE),
            "windows_out",
        )
        own.append(result)
        if which == parts - 1:
            result = after(result, (global_across, value_sides))
        partner.append(other_core(result))
    value_across = across(*value_sides)

    all_rows = lon_size * rows
    query_block = 256 if (2 * rows) % 256 == 0 else 2 * rows
    query_steps = 2 * rows // query_block
    project_steps = 2 * parts * steps
    pieces = [global_first, *global_sides, global_across, global_second, *value_sides, value_across]
    key_chunk = 512 if (2 * all_rows) % 512 == 0 else block
    late = lambda i: jnp.clip(i - project_steps, 0, query_steps - 1)
    normed_specs = [
        pl.BlockSpec((block, width), lambda i, _, at=at: (jnp.clip(i - at * steps, 0, steps - 1), 0))
        for at in range(2 * parts)
    ]
    whole_tile = pl.BlockSpec(
        (lon_size, code_tile, MAIN), lambda *_: (0, part_rows // code_tile, 0)
    )
    (mixed,) = run(
        functools.partial(group_kernel, steps, parts, count, kept_most, key_chunk),
        project_steps + query_steps,
        global_offsets,
        [
            *normed_specs,
            *[whole_tile] * parts,
            pl.BlockSpec((query_block, 1), lambda i, _: (late(i), 0)),
            *map(whole_block, pieces),
        ],
        [*own, *partner, *got, query_codes, *pieces],
        [(2 * rows, WIDE)],
        [pl.BlockSpec((query_block, WIDE), lambda i, _: (late(i), 0))],
        [
            (width, 2 * WIDE),
            (width, WIDE),
            (2 * all_rows, WIDE),
            (2 * rows, WIDE),
            (2 * all_rows, WIDE),
            pltpu.VMEM((1, 2 * all_rows), jnp.float32),
        ],
        2 * WIDE * (2 * all_rows * 2 * width + 2 * rows * width + 4 * rows * 2 * all_rows),
        "groups",
    )

    mine, theirs = mixed[:rows], other_core(mixed[rows:])
    result = jnp.where(
        core == 0,
        jnp.concatenate([mine, theirs], axis=1),
        jnp.concatenate([theirs, mine], axis=1),
    )
    return result.reshape(1, lat_windows, lon_windows, kept_most, inner)


def body(patches, kept_index, kept_count, embed_weight, local_qkv, local_out, global_qkv):
    args = (patches, kept_index, kept_count, embed_weight, local_qkv, local_out, global_qkv)
    windows = patches.shape[1] * patches.shape[2]
    rows = windows * kept_index.shape[3]
    sample_rows = rows * lax.axis_size("lat") * lax.axis_size("lon")
    fits = patches.shape[3] <= 256 and windows % 2 == 0 and windows * kept_index.shape[3] % 32 == 0 and sample_rows * HEADS * HD * 2 <= vmem_limit // 4
    shards = embed_weight.shape[0] * 2 == local_qkv.shape[0] == local_out.shape[0] == 2 * HD
    if lax.axis_size("batch") == 4 and lax.axis_size("lat") == HEADS // GROUP == 2 and fits and shards:
        return sample_body(*args)
    return owner_body(*args)


def solution(mesh):
    return jax.shard_map(
        body,
        mesh=mesh,
        in_specs=(
            P("batch", "lat", "lon", None, None),
            P("batch", "lat", "lon", None),
            P("batch", "lat", "lon"),
            P("batch", None),
            P("batch", None),
            P("batch", None),
            P("batch", None),
        ),
        out_specs=P("batch", "lat", "lon", None, None),
        check_vma=False,
    )
```

```python
import functools

import jax
import jax.numpy as jnp
from jax import lax
from jax.experimental import pallas as pl
from jax.experimental.pallas import tpu as pltpu
from jax.sharding import PartitionSpec as P

HEADS = 8
HD = 160


norm_eps = 1e-05
mask_floor = -1e30
vmem_limit = 60 * 1024 * 1024
exp2_scale = HD ** (-0.5) * 1.4426950408889634


def layer_norm(values):
    centre = values - jnp.mean(values, axis=-1, keepdims=True)
    spread = jnp.mean(centre * centre, axis=-1, keepdims=True)
    return centre * lax.rsqrt(spread + norm_eps)


def fold_product(left_rows, shard_rows):
    return jnp.dot(left_rows, shard_rows, preferred_element_type=jnp.float32)


def attend(query_rows, key_rows, value_rows, keep_mask):
    scores = jnp.einsum(
        "bnhd,bmhd->bhnm", query_rows, key_rows, preferred_element_type=jnp.float32
    ) * HD ** (-0.5)
    scores = jnp.where(keep_mask[:, None, None, :], scores, mask_floor)
    scores = scores - jnp.max(scores, axis=-1, keepdims=True)
    weights = jnp.exp(scores)
    probabilities = (weights / jnp.sum(weights, axis=-1, keepdims=True)).astype(jnp.bfloat16)
    blended = jnp.einsum(
        "bhnm,bmhd->bnhd", probabilities, value_rows, preferred_element_type=jnp.float32
    )
    return blended.astype(jnp.bfloat16).reshape(
        query_rows.shape[0], query_rows.shape[1], HEADS * HD
    )


def owner_work(received, flag_rows, whole_global):
    item_count = received.shape[0]
    slot_values = received.reshape(item_count, -1, received.shape[-1])
    projected = jnp.dot(
        slot_values.reshape(-1, slot_values.shape[-1]),
        whole_global,
        preferred_element_type=jnp.float32,
    )
    slot_values = projected.astype(jnp.bfloat16).reshape(item_count, -1, 3 * HEADS * HD)
    heads_split = slot_values.reshape(item_count, slot_values.shape[1], 3, HEADS, HD)
    keep_mask = flag_rows.reshape(item_count, -1) > 0
    return attend(heads_split[:, :, 0], heads_split[:, :, 1], heads_split[:, :, 2], keep_mask)


def owner_body(patches, kept_index, kept_count, embed_weight, local_qkv, local_out, global_qkv):
    lat_windows = patches.shape[1]
    lon_windows = patches.shape[2]
    windows = lat_windows * lon_windows
    window_tokens = patches.shape[3]
    kept_most = kept_index.shape[3]
    row_count = windows * kept_most
    inner_width = HEADS * HD
    patch_rows = patches.reshape(windows, window_tokens, patches.shape[4])
    index_rows = kept_index.reshape(windows, kept_most)
    kept_mask = lax.broadcasted_iota(jnp.int32, (windows, kept_most), 1) < kept_count.reshape(
        windows, 1
    )
    picked = jnp.take_along_axis(patch_rows, index_rows[:, :, None], axis=1).reshape(row_count, -1)
    embedded = fold_product(
        picked, lax.all_gather(embed_weight, "batch", axis=0, tiled=True)
    ).astype(jnp.bfloat16)
    normed = layer_norm(embedded.astype(jnp.float32)).astype(jnp.bfloat16)
    local_proj = fold_product(
        normed, lax.all_gather(local_qkv, "batch", axis=0, tiled=True)
    ).astype(jnp.bfloat16)
    local_split = local_proj.reshape(windows, kept_most, 3, HEADS, HD)
    local_mix = attend(
        local_split[:, :, 0], local_split[:, :, 1], local_split[:, :, 2], kept_mask
    ).reshape(row_count, inner_width)
    back_sum = fold_product(local_mix, lax.all_gather(local_out, "batch", axis=0, tiled=True))
    hidden = (embedded.astype(jnp.float32) + back_sum).astype(jnp.bfloat16)
    normed_global = layer_norm(hidden.astype(jnp.float32)).astype(jnp.bfloat16)
    whole_global = lax.all_gather(global_qkv, "batch", axis=0, tiled=True)
    sent_width = normed_global.shape[1]
    window_ids = lax.broadcasted_iota(jnp.int32, (windows, kept_most), 0)
    slot_rows = (
        jnp.zeros((window_tokens, windows, sent_width), jnp.bfloat16)
        .at[index_rows, window_ids]
        .set(normed_global.reshape(windows, kept_most, sent_width))
    )
    flag_slots = (
        jnp.zeros((window_tokens, windows), jnp.bfloat16)
        .at[index_rows, window_ids]
        .set(kept_mask.astype(jnp.bfloat16))
    )
    owners = lax.axis_size("lat") * lax.axis_size("lon")
    owned_count = window_tokens // owners
    blended = owner_work(
        lax.all_to_all(
            slot_rows.reshape(owned_count, owners, windows, sent_width),
            ("lat", "lon"),
            split_axis=1,
            concat_axis=2,
            tiled=True,
        ),
        lax.all_to_all(
            flag_slots.reshape(owned_count, owners, windows),
            ("lat", "lon"),
            split_axis=1,
            concat_axis=2,
            tiled=True,
        ),
        whole_global,
    )
    shaped = blended.reshape(blended.shape[0], 1, -1, inner_width)
    returned = lax.all_to_all(shaped, ("lat", "lon"), split_axis=2, concat_axis=1, tiled=True)
    out_slots = returned.reshape(window_tokens, windows, inner_width)
    gathered = out_slots[index_rows, window_ids]
    result = jnp.where(kept_mask[:, :, None], gathered, jnp.zeros_like(gathered))
    return result.reshape(1, lat_windows, lon_windows, kept_most, inner_width)


MAIN = 128
TAIL = HD - MAIN
GROUP = MAIN // TAIL
WIDE = GROUP * HD


def whole_block(array):
    zeros = (0,) * array.ndim
    return pl.BlockSpec(array.shape, lambda *_: zeros, pipeline_mode=pl.Buffered(1))


def parts_of(pieces, high):
    return [piece.at[pl.ds(at, high)] for piece in pieces for at in range(0, piece.shape[0], high)]


def first_row(offset_ref, at, unit):
    return pl.multiple_of(offset_ref[at], unit)


def reorder(source, start, target, at):
    for head in range(GROUP):
        first = start + head * HD
        target[:, pl.ds(at + head * MAIN, MAIN)] = source[:, pl.ds(first, MAIN)]
        target[:, pl.ds(at + GROUP * MAIN + head * TAIL, TAIL)] = source[:, pl.ds(first + MAIN, TAIL)]


def pick_kernel(_, patch_ref, code_ref, *sent_refs):
    window_tokens = patch_ref.shape[1]
    windows, kept_most = code_ref.shape
    count = windows // len(sent_refs)
    rows = count * kept_most
    offsets = lax.broadcasted_iota(jnp.int32, (window_tokens, kept_most), 0)
    for which, sent_ref in enumerate(sent_refs):
        tile = sent_ref.shape[1] - rows
        sent_ref[0, pl.ds(rows, tile), :] = jnp.zeros((tile, sent_ref.shape[2]), jnp.bfloat16)
        for at in range(count):
            window = which * count + at
            chosen = (offsets == code_ref[pl.ds(window, 1), :]).astype(jnp.float32)
            picked = lax.dot_general(
                chosen.astype(jnp.bfloat16),
                patch_ref[window],
                (((0,), (0,)), ((), ())),
                preferred_element_type=jnp.float32,
            )
            sent_ref[0, pl.ds(at * kept_most, kept_most), :] = picked.astype(jnp.bfloat16)
        part = pl.ds(which * count, count)
        codes = code_ref[part, :].astype(jnp.float32).astype(jnp.bfloat16)
        sent_ref[0, pl.ds(rows, count), pl.ds(0, kept_most)] = codes
        for copy in range(1, sent_ref.shape[0]):
            sent_ref[copy] = sent_ref[0]


def pack_columns(column_refs, full_ref):
    for which, column_ref in enumerate(column_refs):
        reorder(column_ref, 0, full_ref, which * WIDE)


def own_half(core_ref, full_ref, half_ref):
    half = half_ref.shape[0]
    half_ref[...] = full_ref[pl.ds(pl.multiple_of(core_ref[0] * half, 16), half), :]


def pack_first_kernel(core_ref, query_ref, key_ref, value_ref, embed_ref, full_ref, half_ref):
    pack_columns((query_ref, key_ref, value_ref), full_ref)
    quarter = half_ref.shape[0] // 2
    wide = embed_ref.shape[1] // 2
    for at in range(4):
        core, side = at // 2, at % 2
        full_ref[pl.ds(at * quarter, quarter), pl.ds(3 * WIDE, wide)] = embed_ref[
            pl.ds(core * quarter, quarter), pl.ds(side * wide, wide)
        ]
    own_half(core_ref, full_ref, half_ref)


def pack_second_kernel(core_ref, query_ref, key_ref, value_ref, out_ref, full_ref, half_ref):
    pack_columns((query_ref, key_ref, value_ref), full_ref)
    full_ref[:, pl.ds(3 * WIDE, out_ref.shape[1])] = out_ref[...]
    own_half(core_ref, full_ref, half_ref)


def prepare_global_kernel(core_ref, query_ref, key_ref, value_ref, first_ref, second_ref):
    reorder(key_ref, 0, first_ref, 0)
    reorder(query_ref, 0, first_ref, WIDE)
    reorder(value_ref, 0, second_ref, 0)


def lane_head():
    return lax.broadcasted_iota(jnp.int32, (1, MAIN), 1) // TAIL


def head_tiles(ref, rows, at, head):
    main = ref[rows, pl.ds(at + head * MAIN, MAIN)]
    tail = ref[rows, pl.ds(at + GROUP * MAIN, MAIN)]
    return main, tail


def head_query(ref, rows, at, head):
    main, tail = head_tiles(ref, rows, at, head)
    return jnp.concatenate([main, jnp.where(lane_head() == head, tail, jnp.zeros_like(tail))], axis=1)


def head_pair(ref, rows, at, head):
    return jnp.concatenate(head_tiles(ref, rows, at, head), axis=1)


def masked_scores(query, key, mask):
    scores = lax.dot_general(
        query, key, (((1,), (1,)), ((), ())), preferred_element_type=jnp.float32
    )
    return jnp.where(mask, scores, mask_floor)


def code_row(tile, at, kept_most):
    return tile[at : at + 1, :kept_most]


def mix_heads(proj_ref, code_ref, mix_ref, count, kept_most, at_once):
    rows = proj_ref.shape[0]
    own_window = lax.broadcasted_iota(jnp.int32, (at_once, 1), 0) // kept_most
    key_window = lax.broadcasted_iota(jnp.int32, (1, at_once), 1) // kept_most
    tiles = [code_ref[at].astype(jnp.float32) for at in range(code_ref.shape[0])]
    codes = [code_row(tile, at, kept_most) for tile in tiles for at in range(count)]
    for start in range(0, rows, at_once):
        part = pl.ds(start, at_once)
        first = start // kept_most
        key_codes = jnp.concatenate(codes[first : first + at_once // kept_most], axis=1)
        mask = own_window == jnp.where(key_codes >= 0, key_window, -1)
        tails = None
        for head in range(GROUP):
            scores = masked_scores(
                head_query(proj_ref, part, 0, head), head_pair(proj_ref, part, WIDE, head), mask
            )
            top = jnp.max(scores, axis=-1, keepdims=True)
            weights = jnp.exp2((scores - top) * exp2_scale)
            total = jnp.sum(weights, axis=-1, keepdims=True)
            mixed = (
                fold_product(
                    weights.astype(jnp.bfloat16), head_pair(proj_ref, part, 2 * WIDE, head)
                )
                / total
            )
            mix_ref[part, pl.ds(head * MAIN, MAIN)] = mixed[:, :MAIN].astype(jnp.bfloat16)
            tail = mixed[:, MAIN:]
            tails = tail if tails is None else jnp.where(lane_head() == head, tail, tails)
        mix_ref[part, pl.ds(GROUP * MAIN, MAIN)] = tails.astype(jnp.bfloat16)


def embed_window_kernel(
    mix,
    offset_ref,
    picked_ref,
    code_ref,
    *refs,
):
    *pieces, embedded_ref, normed_ref, mix_ref, weight_ref, embed_ref, proj_ref = refs

    @pl.when(pl.program_id(0) == 0)
    def _():
        high = pieces[0].shape[0] // 2
        quarter = high // 2
        wide = embed_ref.shape[1] // 2
        for at, part in enumerate(parts_of(pieces, high)):
            start = first_row(offset_ref, 3 * at, 32)
            weight_ref[pl.ds(start, high), :] = part[:, pl.ds(0, 3 * WIDE)]
            start = pl.multiple_of(start // 2, 16)
            for side in range(2):
                embed_ref[pl.ds(start, quarter), pl.ds(side * wide, wide)] = part[
                    pl.ds(side * quarter, quarter), pl.ds(3 * WIDE, wide)
                ]

    picked = picked_ref[...].reshape(proj_ref.shape[0], picked_ref.shape[2])
    embedded = fold_product(picked, embed_ref[...]).astype(jnp.bfloat16)
    embedded_ref[...] = embedded
    normed = layer_norm(embedded.astype(jnp.float32)).astype(jnp.bfloat16)
    normed_ref[...] = normed
    proj_ref[...] = fold_product(normed, weight_ref[...]).astype(jnp.bfloat16)
    mix(proj_ref, code_ref, mix_ref)


def window_out_kernel(
    mix,
    offset_ref,
    embedded_ref,
    normed_ref,
    mix_ref,
    code_ref,
    *refs,
):
    *pieces, result_ref, weight_ref, proj_ref, own_mix_ref, row_ref = refs

    @pl.when(pl.program_id(0) == 0)
    def _():
        wide = row_ref.shape[1]
        for at, part in enumerate(parts_of(pieces, HD)):
            weight_ref[pl.ds(first_row(offset_ref, 3 * at, 32), HD), :] = part[:, pl.ds(0, 3 * WIDE)]
            row_ref[pl.ds(first_row(offset_ref, 3 * at + 1, 32), MAIN), :] = part[
                pl.ds(0, MAIN), pl.ds(3 * WIDE, wide)
            ]
            row_ref[pl.ds(first_row(offset_ref, 3 * at + 2, 32), TAIL), :] = part[
                pl.ds(MAIN, TAIL), pl.ds(3 * WIDE, wide)
            ]

    proj_ref[...] = fold_product(normed_ref[...], weight_ref[...]).astype(jnp.bfloat16)
    mix(proj_ref, code_ref, own_mix_ref)
    hidden = embedded_ref[...].astype(jnp.float32)
    hidden += fold_product(mix_ref[...], row_ref[pl.ds(0, WIDE), :])
    hidden += fold_product(own_mix_ref[...], row_ref[pl.ds(WIDE, WIDE), :])
    hidden = hidden.astype(jnp.bfloat16).astype(jnp.float32)
    result_ref[...] = layer_norm(hidden).astype(jnp.bfloat16)


def group_kernel(steps, parts, count, kept_most, key_chunk, offset_ref, *refs):
    many = 2 * parts
    normed_refs, refs = refs[:many], refs[many:]
    tile_refs, refs = refs[:many], refs[many:]
    code_ref, *pieces, mixed_ref, first_ref, second_ref, key_ref, query_ref, value_ref, key_code_ref = refs
    step = pl.program_id(0)
    block = normed_refs[0].shape[0]
    query_block = mixed_ref.shape[0]
    part_rows = count * kept_most
    shared = block // part_rows

    @pl.when(step == 0)
    def _():
        for target, arrays in ((first_ref, pieces[:4]), (second_ref, pieces[4:])):
            for at, array in enumerate(arrays):
                target[pl.ds(first_row(offset_ref, at, 32), array.shape[0]), :] = array[...]
        at = 0
        for tile_ref in tile_refs:
            for device in range(tile_ref.shape[0]):
                tile = tile_ref[device].astype(jnp.float32)
                for window in range(count):
                    key_code_ref[:, pl.ds(at, kept_most)] = code_row(tile, window, kept_most)
                    at += kept_most

    for which, normed_ref in enumerate(normed_refs):

        @pl.when((step >= which * steps) & (step < (which + 1) * steps))
        def _():
            normed = normed_ref[...]
            part = pl.ds(pl.multiple_of(step * block, 16), block)
            key_ref[part, :] = fold_product(normed, first_ref[:, pl.ds(0, WIDE)]).astype(jnp.bfloat16)
            value_ref[part, :] = fold_product(normed, second_ref[...]).astype(jnp.bfloat16)

        @pl.when(step == which * steps + offset_ref[4] // shared)
        def _():
            start = pl.multiple_of(offset_ref[4] % shared * part_rows, 16)
            query_ref[pl.ds(which * part_rows, part_rows), :] = fold_product(
                normed_ref[pl.ds(start, part_rows), :], first_ref[:, pl.ds(WIDE, WIDE)]
            ).astype(jnp.bfloat16)

    @pl.when(step >= many * steps)
    def _():
        part = pl.ds(pl.multiple_of((step - many * steps) * query_block, 16), query_block)
        codes = code_ref[...]
        key_parts = [pl.ds(at, key_chunk) for at in range(0, key_ref.shape[0], key_chunk)]
        for head in range(GROUP):
            query = head_query(query_ref, part, 0, head)
            scores = [
                masked_scores(query, head_pair(key_ref, p, 0, head), codes == key_code_ref[:, p])
                for p in key_parts
            ]
            top = functools.reduce(
                jnp.maximum, [jnp.max(s, axis=-1, keepdims=True) for s in scores]
            )
            total = 0.0
            mixed = 0.0
            for p, s in zip(key_parts, scores):
                weights = jnp.exp2((s - top) * exp2_scale)
                total += jnp.sum(weights, axis=-1, keepdims=True)
                mixed += fold_product(
                    weights.astype(jnp.bfloat16), head_pair(value_ref, p, 0, head)
                )
            mixed = jnp.where(codes >= 0, mixed / total, 0.0).astype(jnp.bfloat16)
            mixed_ref[:, pl.ds(head * HD, MAIN)] = mixed[:, :MAIN]
            at = MAIN + head * TAIL
            mixed_ref[:, pl.ds(head * HD + MAIN, TAIL)] = mixed[:, at : at + TAIL]


def swap_perm(size, mask):
    return [(i, i ^ mask) for i in range(size)]


def after(value, earlier):
    return lax.optimization_barrier((value, earlier))[0]


def run(kernel, steps, scalars, specs, arrays, outs, out_specs, scratch, flops, name):
    moved = sum(a.size * a.dtype.itemsize for a in arrays)
    return pl.pallas_call(
        kernel,
        grid_spec=pltpu.PrefetchScalarGridSpec(
            num_scalar_prefetch=1,
            grid=(steps,),
            in_specs=specs,
            out_specs=out_specs,
            scratch_shapes=[
                pltpu.VMEM(shape, jnp.bfloat16) if isinstance(shape, tuple) else shape
                for shape in scratch
            ],
        ),
        out_shape=[jax.ShapeDtypeStruct(shape, jnp.bfloat16) for shape in outs],
        compiler_params=pltpu.CompilerParams(vmem_limit_bytes=vmem_limit),
        cost_estimate=pl.CostEstimate(flops=flops, bytes_accessed=moved if flops else 0, transcendentals=0),
        name=name,
    )(scalars, *arrays)


def sample_body(patches, kept_index, kept_count, embed_weight, local_qkv, local_out, global_qkv):
    lat_windows, lon_windows, window_tokens, pin = patches.shape[1:]
    windows = lat_windows * lon_windows
    kept_most = kept_index.shape[3]
    rows = windows * kept_most
    inner = HEADS * HD
    width = embed_weight.shape[1]
    lon_size = lax.axis_size("lon")
    batch_size = lax.axis_size("batch")
    core = lax.axis_index("lat")
    chip = lax.axis_index("batch")
    place = lax.axis_index("lon")
    core_scalar = core.reshape(1).astype(jnp.int32)

    def other_core(value):
        return lax.ppermute(value, "lat", swap_perm(2, 1))

    diagonal = []
    for b in range(batch_size):
        diagonal += [(2 * b, 2 * (b ^ 1)), (2 * b + 1, 2 * (b ^ 2) + 1)]

    def sides(part):
        along_x = lax.ppermute(part, "batch", swap_perm(batch_size, 1))
        along_y = lax.ppermute(part, "batch", swap_perm(batch_size, 2))
        return along_x, along_y

    def across(along_x, along_y):
        forwarded = jnp.where(core == 0, along_y, along_x)
        return lax.ppermute(forwarded, ("batch", "lat"), diagonal)

    def across_of(joined):
        forwarded = lax.dynamic_slice_in_dim(joined, (1 - core) * half, half, axis=0)
        return lax.ppermute(forwarded, ("batch", "lat"), diagonal)

    high = local_qkv.shape[0]
    half = high // 2
    first_wide = 3 * WIDE + width // 2
    second_wide = 3 * WIDE + width

    def pack(kernel, group, scalar, other, wide, name):
        shapes = [(high, wide), (half, wide)]
        return run(
            kernel,
            1,
            scalar,
            [
                *[
                    pl.BlockSpec((high, WIDE), lambda i, c, at=2 * which + group: (0, at))
                    for which in range(3)
                ],
                whole_block(other),
            ],
            [local_qkv] * 3 + [other],
            shapes,
            [pl.BlockSpec(shape, lambda *_: (0, 0)) for shape in shapes],
            [],
            0,
            name,
        )

    local_first, half_first = pack(
        pack_first_kernel, 0, core_scalar, embed_weight, first_wide, "pack_first"
    )

    parts = 1
    count = windows // parts
    part_rows = count * kept_most
    code_tile = -(-count // 16) * 16
    sent_shape = (lon_size, part_rows + code_tile, pin)
    patch_rows = patches.reshape(windows, window_tokens, pin)
    kept_mask = lax.broadcasted_iota(jnp.int32, (windows, kept_most), 1) < kept_count.reshape(
        windows, 1
    )
    codes = jnp.where(kept_mask, kept_index.reshape(windows, kept_most), -1)
    partner_codes = other_core(codes)
    query_codes = jnp.concatenate([codes, partner_codes], axis=0).astype(jnp.float32)
    query_codes = query_codes.reshape(2 * rows, 1)
    global_starts = [(chip ^ which) * high for which in range(4)]
    global_offsets = jnp.stack([*global_starts, place]).astype(jnp.int32)
    sent = run(
        pick_kernel,
        1,
        after(core_scalar, half_first),
        [whole_block(patch_rows), whole_block(codes)],
        [patch_rows, codes],
        [sent_shape] * parts,
        [pl.BlockSpec(sent_shape, lambda *_: (0, 0, 0))] * parts,
        [],
        0,
        "pick",
    )
    query_codes, global_offsets = after((query_codes, global_offsets), sent)
    got = []
    for value in sent:
        value = after(value, got[-1]) if got else value
        got.append(lax.all_to_all(value, "lon", 0, 0, tiled=True))

    local_second, half_second = pack(
        pack_second_kernel, 1, after(core_scalar, sent), local_out, second_wide, "pack_second"
    )
    global_first, global_second = run(
        prepare_global_kernel,
        1,
        after(core_scalar, half_second),
        [
            pl.BlockSpec((high, WIDE), lambda i, c, which=which: (0, 2 * which + c[0]))
            for which in range(3)
        ],
        [global_qkv] * 3,
        [(high, 2 * WIDE), (high, WIDE)],
        [pl.BlockSpec((high, w), lambda *_: (0, 0)) for w in (2 * WIDE, WIDE)],
        [],
        0,
        "order_global",
    )
    sides_first = sides(half_first)
    sides_first = after(sides_first, (sent, global_first))
    sides_second = sides(after(half_second, sides_first))
    joined_first = lax.optimization_barrier(jnp.concatenate(sides_first, axis=0))
    across_first = across_of(joined_first)
    global_sides = sides(after(global_first, sides_second))
    joined_second = lax.optimization_barrier(jnp.concatenate(sides_second, axis=0))
    across_second = across_of(joined_second)

    def shared(shard, joined, diagonal_part, earlier):
        pieces = [shard, joined, other_core(joined), diagonal_part]
        pieces.append(other_core(after(diagonal_part, earlier)))
        bases = [(chip ^ which) * high for which in (1, 2, 3)]
        firsts = [chip * high, chip * high + half]
        for group in (bases[:2], bases[2:]):
            firsts += [base + core * half for base in group]
            firsts += [base + (1 - core) * half for base in group]
        firsts = jnp.stack(firsts).astype(jnp.int32)
        head = firsts // HD
        group_start = head // GROUP * WIDE
        main = group_start + head % GROUP * MAIN
        tail = group_start + GROUP * MAIN + head % GROUP * TAIL
        return pieces, jnp.stack([firsts, main, tail], axis=1).reshape(-1)

    shared_by = 1
    block = shared_by * part_rows
    steps = lon_size // shared_by
    many_rows = lon_size * part_rows
    at_once = 2 * kept_most if block % (2 * kept_most) == 0 else kept_most
    mix = functools.partial(mix_heads, count=count, kept_most=kept_most, at_once=at_once)
    row_spec = lambda wide: pl.BlockSpec((block, wide), lambda i, _: (i, 0))
    tile_spec = pl.BlockSpec((shared_by, code_tile, MAIN), lambda i, _: (i, part_rows // code_tile, 0))

    pieces, offsets = shared(local_first, joined_first, across_first, core_scalar)
    embedded, normed, mixes = [], [], []
    for which in range(parts):
        if which == parts - 1:
            pieces = after(pieces, (joined_second, mixes))
        result = run(
            functools.partial(embed_window_kernel, mix),
            steps,
            offsets,
            [
                pl.BlockSpec((shared_by, part_rows, pin), lambda i, _: (i, 0, 0)),
                tile_spec,
                *map(whole_block, pieces),
            ],
            [got[which], got[which], *pieces],
            [(many_rows, width), (many_rows, width), (many_rows, WIDE)],
            [row_spec(width), row_spec(width), row_spec(WIDE)],
            [(width, 3 * WIDE), (pin, width), (block, 3 * WIDE)],
            0,
            "embed_windows",
        )
        for values, value in zip((embedded, normed, mixes), result):
            values.append(value)

    pieces, offsets = shared(local_second, joined_second, across_second, mixes[0])
    own, partner = [], []
    for which in range(parts):
        if which == parts - 1:
            pieces = after(pieces, (global_sides, own))
            global_sides, _ = after((global_sides, 0), own or mixes)
            global_across = across(*global_sides)
            value_sides = sides(after(global_second, global_sides))
        (result,) = run(
            functools.partial(window_out_kernel, mix),
            steps,
            offsets,
            [row_spec(width), row_spec(width), row_spec(WIDE), tile_spec, *map(whole_block, pieces)],
            [embedded[which], normed[which], mixes[which], got[which], *pieces],
            [(many_rows, width)],
            [row_spec(width)],
            [(width, 3 * WIDE), (block, 3 * WIDE), (block, WIDE), (inner, width)],
            2 * many_rows * (inner * width + width * 3 * WIDE),
            "windows_out",
        )
        own.append(result)
        if which == parts - 1:
            result = after(result, (global_across, value_sides))
        partner.append(other_core(result))
    value_across = across(*value_sides)
    partner_tiles = [
        other_core(after(value, own)[:, part_rows : part_rows + code_tile, :MAIN]) for value in got
    ]

    all_rows = lon_size * rows
    query_block = 256 if (2 * rows) % 256 == 0 else 2 * rows
    query_steps = 2 * rows // query_block
    project_steps = 2 * parts * steps
    pieces = [global_first, *global_sides, global_across, global_second, *value_sides, value_across]
    key_chunk = 512 if (2 * all_rows) % 512 == 0 else block
    late = lambda i: jnp.clip(i - project_steps, 0, query_steps - 1)
    normed_specs = [
        pl.BlockSpec((block, width), lambda i, _, at=at: (jnp.clip(i - at * steps, 0, steps - 1), 0))
        for at in range(2 * parts)
    ]
    whole_tile = pl.BlockSpec(
        (lon_size, code_tile, MAIN), lambda *_: (0, part_rows // code_tile, 0)
    )
    (mixed,) = run(
        functools.partial(group_kernel, steps, parts, count, kept_most, key_chunk),
        project_steps + query_steps,
        global_offsets,
        [
            *normed_specs,
            *[whole_tile] * parts,
            *map(whole_block, partner_tiles),
            pl.BlockSpec((query_block, 1), lambda i, _: (late(i), 0)),
            *map(whole_block, pieces),
        ],
        [*own, *partner, *got, *partner_tiles, query_codes, *pieces],
        [(2 * rows, WIDE)],
        [pl.BlockSpec((query_block, WIDE), lambda i, _: (late(i), 0))],
        [
            (width, 2 * WIDE),
            (width, WIDE),
            (2 * all_rows, WIDE),
            (2 * rows, WIDE),
            (2 * all_rows, WIDE),
            pltpu.VMEM((1, 2 * all_rows), jnp.float32),
        ],
        2 * WIDE * (2 * all_rows * 2 * width + 2 * rows * width + 4 * rows * 2 * all_rows),
        "groups",
    )

    mine, theirs = mixed[:rows], other_core(mixed[rows:])
    result = jnp.where(
        core == 0,
        jnp.concatenate([mine, theirs], axis=1),
        jnp.concatenate([theirs, mine], axis=1),
    )
    return result.reshape(1, lat_windows, lon_windows, kept_most, inner)


def body(patches, kept_index, kept_count, embed_weight, local_qkv, local_out, global_qkv):
    args = (patches, kept_index, kept_count, embed_weight, local_qkv, local_out, global_qkv)
    windows = patches.shape[1] * patches.shape[2]
    rows = windows * kept_index.shape[3]
    sample_rows = rows * lax.axis_size("lat") * lax.axis_size("lon")
    fits = patches.shape[3] <= 256 and windows % 2 == 0 and windows * kept_index.shape[3] % 32 == 0 and sample_rows * HEADS * HD * 2 <= vmem_limit // 4
    shards = embed_weight.shape[0] * 2 == local_qkv.shape[0] == local_out.shape[0] == 2 * HD
    if lax.axis_size("batch") == 4 and lax.axis_size("lat") == HEADS // GROUP == 2 and fits and shards:
        return sample_body(*args)
    return owner_body(*args)


def solution(mesh):
    return jax.shard_map(
        body,
        mesh=mesh,
        in_specs=(
            P("batch", "lat", "lon", None, None),
            P("batch", "lat", "lon", None),
            P("batch", "lat", "lon"),
            P("batch", None),
            P("batch", None),
            P("batch", None),
            P("batch", None),
        ),
        out_specs=P("batch", "lat", "lon", None, None),
        check_vma=False,
    )
```

```python
import functools

import jax
import jax.numpy as jnp
from jax import lax
from jax.experimental import pallas as pl
from jax.experimental.pallas import tpu as pltpu
from jax.sharding import PartitionSpec as P

HEADS = 8
HD = 160


norm_eps = 1e-05
mask_floor = -1e30
vmem_limit = 60 * 1024 * 1024
exp2_scale = HD ** (-0.5) * 1.4426950408889634


def layer_norm(values):
    centre = values - jnp.mean(values, axis=-1, keepdims=True)
    spread = jnp.mean(centre * centre, axis=-1, keepdims=True)
    return centre * lax.rsqrt(spread + norm_eps)


def fold_product(left_rows, shard_rows):
    return jnp.dot(left_rows, shard_rows, preferred_element_type=jnp.float32)


def attend(query_rows, key_rows, value_rows, keep_mask):
    scores = jnp.einsum(
        "bnhd,bmhd->bhnm", query_rows, key_rows, preferred_element_type=jnp.float32
    ) * HD ** (-0.5)
    scores = jnp.where(keep_mask[:, None, None, :], scores, mask_floor)
    scores = scores - jnp.max(scores, axis=-1, keepdims=True)
    weights = jnp.exp(scores)
    probabilities = (weights / jnp.sum(weights, axis=-1, keepdims=True)).astype(jnp.bfloat16)
    blended = jnp.einsum(
        "bhnm,bmhd->bnhd", probabilities, value_rows, preferred_element_type=jnp.float32
    )
    return blended.astype(jnp.bfloat16).reshape(
        query_rows.shape[0], query_rows.shape[1], HEADS * HD
    )


def owner_work(received, flag_rows, whole_global):
    item_count = received.shape[0]
    slot_values = received.reshape(item_count, -1, received.shape[-1])
    projected = jnp.dot(
        slot_values.reshape(-1, slot_values.shape[-1]),
        whole_global,
        preferred_element_type=jnp.float32,
    )
    slot_values = projected.astype(jnp.bfloat16).reshape(item_count, -1, 3 * HEADS * HD)
    heads_split = slot_values.reshape(item_count, slot_values.shape[1], 3, HEADS, HD)
    keep_mask = flag_rows.reshape(item_count, -1) > 0
    return attend(heads_split[:, :, 0], heads_split[:, :, 1], heads_split[:, :, 2], keep_mask)


def owner_body(patches, kept_index, kept_count, embed_weight, local_qkv, local_out, global_qkv):
    lat_windows = patches.shape[1]
    lon_windows = patches.shape[2]
    windows = lat_windows * lon_windows
    window_tokens = patches.shape[3]
    kept_most = kept_index.shape[3]
    row_count = windows * kept_most
    inner_width = HEADS * HD
    patch_rows = patches.reshape(windows, window_tokens, patches.shape[4])
    index_rows = kept_index.reshape(windows, kept_most)
    kept_mask = lax.broadcasted_iota(jnp.int32, (windows, kept_most), 1) < kept_count.reshape(
        windows, 1
    )
    picked = jnp.take_along_axis(patch_rows, index_rows[:, :, None], axis=1).reshape(row_count, -1)
    embedded = fold_product(
        picked, lax.all_gather(embed_weight, "batch", axis=0, tiled=True)
    ).astype(jnp.bfloat16)
    normed = layer_norm(embedded.astype(jnp.float32)).astype(jnp.bfloat16)
    local_proj = fold_product(
        normed, lax.all_gather(local_qkv, "batch", axis=0, tiled=True)
    ).astype(jnp.bfloat16)
    local_split = local_proj.reshape(windows, kept_most, 3, HEADS, HD)
    local_mix = attend(
        local_split[:, :, 0], local_split[:, :, 1], local_split[:, :, 2], kept_mask
    ).reshape(row_count, inner_width)
    back_sum = fold_product(local_mix, lax.all_gather(local_out, "batch", axis=0, tiled=True))
    hidden = (embedded.astype(jnp.float32) + back_sum).astype(jnp.bfloat16)
    normed_global = layer_norm(hidden.astype(jnp.float32)).astype(jnp.bfloat16)
    whole_global = lax.all_gather(global_qkv, "batch", axis=0, tiled=True)
    sent_width = normed_global.shape[1]
    window_ids = lax.broadcasted_iota(jnp.int32, (windows, kept_most), 0)
    slot_rows = (
        jnp.zeros((window_tokens, windows, sent_width), jnp.bfloat16)
        .at[index_rows, window_ids]
        .set(normed_global.reshape(windows, kept_most, sent_width))
    )
    flag_slots = (
        jnp.zeros((window_tokens, windows), jnp.bfloat16)
        .at[index_rows, window_ids]
        .set(kept_mask.astype(jnp.bfloat16))
    )
    owners = lax.axis_size("lat") * lax.axis_size("lon")
    owned_count = window_tokens // owners
    blended = owner_work(
        lax.all_to_all(
            slot_rows.reshape(owned_count, owners, windows, sent_width),
            ("lat", "lon"),
            split_axis=1,
            concat_axis=2,
            tiled=True,
        ),
        lax.all_to_all(
            flag_slots.reshape(owned_count, owners, windows),
            ("lat", "lon"),
            split_axis=1,
            concat_axis=2,
            tiled=True,
        ),
        whole_global,
    )
    shaped = blended.reshape(blended.shape[0], 1, -1, inner_width)
    returned = lax.all_to_all(shaped, ("lat", "lon"), split_axis=2, concat_axis=1, tiled=True)
    out_slots = returned.reshape(window_tokens, windows, inner_width)
    gathered = out_slots[index_rows, window_ids]
    result = jnp.where(kept_mask[:, :, None], gathered, jnp.zeros_like(gathered))
    return result.reshape(1, lat_windows, lon_windows, kept_most, inner_width)


MAIN = 128
TAIL = HD - MAIN
GROUP = MAIN // TAIL
WIDE = GROUP * HD


def whole_block(array):
    zeros = (0,) * array.ndim
    return pl.BlockSpec(array.shape, lambda *_: zeros, pipeline_mode=pl.Buffered(1))


def parts_of(pieces, high):
    return [piece.at[pl.ds(at, high)] for piece in pieces for at in range(0, piece.shape[0], high)]


def first_row(offset_ref, at, unit):
    return pl.multiple_of(offset_ref[at], unit)


def reorder(source, start, target, at):
    for head in range(GROUP):
        first = start + head * HD
        target[:, pl.ds(at + head * MAIN, MAIN)] = source[:, pl.ds(first, MAIN)]
        target[:, pl.ds(at + GROUP * MAIN + head * TAIL, TAIL)] = source[:, pl.ds(first + MAIN, TAIL)]


def pick_kernel(_, patch_ref, code_ref, *sent_refs):
    window_tokens = patch_ref.shape[1]
    windows, kept_most = code_ref.shape
    count = windows // len(sent_refs)
    rows = count * kept_most
    offsets = lax.broadcasted_iota(jnp.int32, (window_tokens, kept_most), 0)
    for which, sent_ref in enumerate(sent_refs):
        tile = sent_ref.shape[1] - rows
        sent_ref[0, pl.ds(rows, tile), :] = jnp.zeros((tile, sent_ref.shape[2]), jnp.bfloat16)
        for at in range(count):
            window = which * count + at
            chosen = (offsets == code_ref[pl.ds(window, 1), :]).astype(jnp.float32)
            picked = lax.dot_general(
                chosen.astype(jnp.bfloat16),
                patch_ref[window],
                (((0,), (0,)), ((), ())),
                preferred_element_type=jnp.float32,
            )
            sent_ref[0, pl.ds(at * kept_most, kept_most), :] = picked.astype(jnp.bfloat16)
        part = pl.ds(which * count, count)
        codes = code_ref[part, :].astype(jnp.float32).astype(jnp.bfloat16)
        sent_ref[0, pl.ds(rows, count), pl.ds(0, kept_most)] = codes
        for copy in range(1, sent_ref.shape[0]):
            sent_ref[copy] = sent_ref[0]


def pack_columns(column_refs, full_ref):
    for which, column_ref in enumerate(column_refs):
        reorder(column_ref, 0, full_ref, which * WIDE)


def own_half(core_ref, full_ref, half_ref):
    half = half_ref.shape[0]
    half_ref[...] = full_ref[pl.ds(pl.multiple_of(core_ref[0] * half, 16), half), :]


def pack_first_kernel(core_ref, query_ref, key_ref, value_ref, embed_ref, full_ref, half_ref):
    pack_columns((query_ref, key_ref, value_ref), full_ref)
    quarter = half_ref.shape[0] // 2
    wide = embed_ref.shape[1] // 2
    for at in range(4):
        core, side = at // 2, at % 2
        full_ref[pl.ds(at * quarter, quarter), pl.ds(3 * WIDE, wide)] = embed_ref[
            pl.ds(core * quarter, quarter), pl.ds(side * wide, wide)
        ]
    own_half(core_ref, full_ref, half_ref)


def pack_second_kernel(core_ref, query_ref, key_ref, value_ref, out_ref, full_ref, half_ref):
    pack_columns((query_ref, key_ref, value_ref), full_ref)
    full_ref[:, pl.ds(3 * WIDE, out_ref.shape[1])] = out_ref[...]
    own_half(core_ref, full_ref, half_ref)


def prepare_global_kernel(core_ref, query_ref, key_ref, value_ref, first_ref, second_ref):
    reorder(key_ref, 0, first_ref, 0)
    reorder(query_ref, 0, first_ref, WIDE)
    reorder(value_ref, 0, second_ref, 0)


def lane_head():
    return lax.broadcasted_iota(jnp.int32, (1, MAIN), 1) // TAIL


def head_tiles(ref, rows, at, head):
    main = ref[rows, pl.ds(at + head * MAIN, MAIN)]
    tail = ref[rows, pl.ds(at + GROUP * MAIN, MAIN)]
    return main, tail


def head_query(ref, rows, at, head):
    main, tail = head_tiles(ref, rows, at, head)
    return jnp.concatenate([main, jnp.where(lane_head() == head, tail, jnp.zeros_like(tail))], axis=1)


def head_pair(ref, rows, at, head):
    return jnp.concatenate(head_tiles(ref, rows, at, head), axis=1)


def masked_scores(query, key, mask):
    scores = lax.dot_general(
        query, key, (((1,), (1,)), ((), ())), preferred_element_type=jnp.float32
    )
    return jnp.where(mask, scores, mask_floor)


def code_row(tile, at, kept_most):
    return tile[at : at + 1, :kept_most]


def mix_heads(proj_ref, code_ref, mix_ref, count, kept_most, at_once):
    rows = proj_ref.shape[0]
    own_window = lax.broadcasted_iota(jnp.int32, (at_once, 1), 0) // kept_most
    key_window = lax.broadcasted_iota(jnp.int32, (1, at_once), 1) // kept_most
    tiles = [code_ref[at].astype(jnp.float32) for at in range(code_ref.shape[0])]
    codes = [code_row(tile, at, kept_most) for tile in tiles for at in range(count)]
    for start in range(0, rows, at_once):
        part = pl.ds(start, at_once)
        first = start // kept_most
        key_codes = jnp.concatenate(codes[first : first + at_once // kept_most], axis=1)
        mask = own_window == jnp.where(key_codes >= 0, key_window, -1)
        tails = None
        for head in range(GROUP):
            scores = masked_scores(
                head_query(proj_ref, part, 0, head), head_pair(proj_ref, part, WIDE, head), mask
            )
            top = jnp.max(scores, axis=-1, keepdims=True)
            weights = jnp.exp2((scores - top) * exp2_scale)
            total = jnp.sum(weights, axis=-1, keepdims=True)
            mixed = (
                fold_product(
                    weights.astype(jnp.bfloat16), head_pair(proj_ref, part, 2 * WIDE, head)
                )
                / total
            )
            mix_ref[part, pl.ds(head * MAIN, MAIN)] = mixed[:, :MAIN].astype(jnp.bfloat16)
            tail = mixed[:, MAIN:]
            tails = tail if tails is None else jnp.where(lane_head() == head, tail, tails)
        mix_ref[part, pl.ds(GROUP * MAIN, MAIN)] = tails.astype(jnp.bfloat16)


def embed_window_kernel(
    mix,
    offset_ref,
    picked_ref,
    code_ref,
    *refs,
):
    *pieces, embedded_ref, normed_ref, mix_ref, weight_ref, embed_ref, proj_ref = refs

    @pl.when(pl.program_id(0) == 0)
    def _():
        high = pieces[0].shape[0] // 2
        quarter = high // 2
        wide = embed_ref.shape[1] // 2
        for at, part in enumerate(parts_of(pieces, high)):
            start = first_row(offset_ref, 3 * at, 32)
            weight_ref[pl.ds(start, high), :] = part[:, pl.ds(0, 3 * WIDE)]
            start = pl.multiple_of(start // 2, 16)
            for side in range(2):
                embed_ref[pl.ds(start, quarter), pl.ds(side * wide, wide)] = part[
                    pl.ds(side * quarter, quarter), pl.ds(3 * WIDE, wide)
                ]

    picked = picked_ref[...].reshape(proj_ref.shape[0], picked_ref.shape[2])
    embedded = fold_product(picked, embed_ref[...]).astype(jnp.bfloat16)
    embedded_ref[...] = embedded
    normed = layer_norm(embedded.astype(jnp.float32)).astype(jnp.bfloat16)
    normed_ref[...] = normed
    proj_ref[...] = fold_product(normed, weight_ref[...]).astype(jnp.bfloat16)
    mix(proj_ref, code_ref, mix_ref)


def window_out_kernel(
    mix,
    offset_ref,
    embedded_ref,
    normed_ref,
    mix_ref,
    code_ref,
    *refs,
):
    *pieces, result_ref, weight_ref, proj_ref, own_mix_ref, row_ref = refs

    @pl.when(pl.program_id(0) == 0)
    def _():
        wide = row_ref.shape[1]
        for at, part in enumerate(parts_of(pieces, HD)):
            weight_ref[pl.ds(first_row(offset_ref, 3 * at, 32), HD), :] = part[:, pl.ds(0, 3 * WIDE)]
            row_ref[pl.ds(first_row(offset_ref, 3 * at + 1, 32), MAIN), :] = part[
                pl.ds(0, MAIN), pl.ds(3 * WIDE, wide)
            ]
            row_ref[pl.ds(first_row(offset_ref, 3 * at + 2, 32), TAIL), :] = part[
                pl.ds(MAIN, TAIL), pl.ds(3 * WIDE, wide)
            ]

    proj_ref[...] = fold_product(normed_ref[...], weight_ref[...]).astype(jnp.bfloat16)
    mix(proj_ref, code_ref, own_mix_ref)
    hidden = embedded_ref[...].astype(jnp.float32)
    hidden += fold_product(mix_ref[...], row_ref[pl.ds(0, WIDE), :])
    hidden += fold_product(own_mix_ref[...], row_ref[pl.ds(WIDE, WIDE), :])
    hidden = hidden.astype(jnp.bfloat16).astype(jnp.float32)
    result_ref[...] = layer_norm(hidden).astype(jnp.bfloat16)


def group_kernel(steps, parts, count, kept_most, key_chunk, offset_ref, *refs):
    many = 2 * parts
    normed_refs, refs = refs[:many], refs[many:]
    tile_refs, refs = refs[:many], refs[many:]
    code_ref, *pieces, mixed_ref, first_ref, second_ref, key_ref, query_ref, value_ref, key_code_ref = refs
    step = pl.program_id(0)
    block = normed_refs[0].shape[0]
    query_block = mixed_ref.shape[0]
    part_rows = count * kept_most
    shared = block // part_rows

    @pl.when(step == 0)
    def _():
        for target, arrays in ((first_ref, pieces[:4]), (second_ref, pieces[4:])):
            for at, array in enumerate(arrays):
                target[pl.ds(first_row(offset_ref, at, 32), array.shape[0]), :] = array[...]
        at = 0
        for tile_ref in tile_refs:
            for device in range(tile_ref.shape[0]):
                tile = tile_ref[device].astype(jnp.float32)
                for window in range(count):
                    key_code_ref[:, pl.ds(at, kept_most)] = code_row(tile, window, kept_most)
                    at += kept_most

    for which, normed_ref in enumerate(normed_refs):

        @pl.when((step >= which * steps) & (step < (which + 1) * steps))
        def _():
            normed = normed_ref[...]
            part = pl.ds(pl.multiple_of(step * block, 16), block)
            key_ref[part, :] = fold_product(normed, first_ref[:, pl.ds(0, WIDE)]).astype(jnp.bfloat16)
            value_ref[part, :] = fold_product(normed, second_ref[...]).astype(jnp.bfloat16)

        @pl.when(step == which * steps + offset_ref[4] // shared)
        def _():
            start = pl.multiple_of(offset_ref[4] % shared * part_rows, 16)
            query_ref[pl.ds(which * part_rows, part_rows), :] = fold_product(
                normed_ref[pl.ds(start, part_rows), :], first_ref[:, pl.ds(WIDE, WIDE)]
            ).astype(jnp.bfloat16)

    @pl.when(step >= many * steps)
    def _():
        part = pl.ds(pl.multiple_of((step - many * steps) * query_block, 16), query_block)
        codes = code_ref[...]
        key_parts = [pl.ds(at, key_chunk) for at in range(0, key_ref.shape[0], key_chunk)]
        for head in range(GROUP):
            query = head_query(query_ref, part, 0, head)
            scores = [
                masked_scores(query, head_pair(key_ref, p, 0, head), codes == key_code_ref[:, p])
                for p in key_parts
            ]
            top = functools.reduce(
                jnp.maximum, [jnp.max(s, axis=-1, keepdims=True) for s in scores]
            )
            total = 0.0
            mixed = 0.0
            for p, s in zip(key_parts, scores):
                weights = jnp.exp2((s - top) * exp2_scale)
                total += jnp.sum(weights, axis=-1, keepdims=True)
                mixed += fold_product(
                    weights.astype(jnp.bfloat16), head_pair(value_ref, p, 0, head)
                )
            mixed = jnp.where(codes >= 0, mixed / total, 0.0).astype(jnp.bfloat16)
            mixed_ref[:, pl.ds(head * HD, MAIN)] = mixed[:, :MAIN]
            at = MAIN + head * TAIL
            mixed_ref[:, pl.ds(head * HD + MAIN, TAIL)] = mixed[:, at : at + TAIL]


def swap_perm(size, mask):
    return [(i, i ^ mask) for i in range(size)]


def after(value, earlier):
    return lax.optimization_barrier((value, earlier))[0]


def run(kernel, steps, scalars, specs, arrays, outs, out_specs, scratch, flops, name):
    moved = sum(a.size * a.dtype.itemsize for a in arrays)
    return pl.pallas_call(
        kernel,
        grid_spec=pltpu.PrefetchScalarGridSpec(
            num_scalar_prefetch=1,
            grid=(steps,),
            in_specs=specs,
            out_specs=out_specs,
            scratch_shapes=[
                pltpu.VMEM(shape, jnp.bfloat16) if isinstance(shape, tuple) else shape
                for shape in scratch
            ],
        ),
        out_shape=[jax.ShapeDtypeStruct(shape, jnp.bfloat16) for shape in outs],
        compiler_params=pltpu.CompilerParams(vmem_limit_bytes=vmem_limit),
        cost_estimate=pl.CostEstimate(flops=flops, bytes_accessed=moved if flops else 0, transcendentals=0),
        name=name,
    )(scalars, *arrays)


def sample_body(patches, kept_index, kept_count, embed_weight, local_qkv, local_out, global_qkv):
    lat_windows, lon_windows, window_tokens, pin = patches.shape[1:]
    windows = lat_windows * lon_windows
    kept_most = kept_index.shape[3]
    rows = windows * kept_most
    inner = HEADS * HD
    width = embed_weight.shape[1]
    lon_size = lax.axis_size("lon")
    batch_size = lax.axis_size("batch")
    core = lax.axis_index("lat")
    chip = lax.axis_index("batch")
    place = lax.axis_index("lon")
    core_scalar = core.reshape(1).astype(jnp.int32)

    def other_core(value):
        return lax.ppermute(value, "lat", swap_perm(2, 1))

    diagonal = []
    for b in range(batch_size):
        diagonal += [(2 * b, 2 * (b ^ 1)), (2 * b + 1, 2 * (b ^ 2) + 1)]

    def sides(part):
        along_x = lax.ppermute(part, "batch", swap_perm(batch_size, 1))
        along_y = lax.ppermute(part, "batch", swap_perm(batch_size, 2))
        return along_x, along_y

    def across(along_x, along_y):
        forwarded = jnp.where(core == 0, along_y, along_x)
        return lax.ppermute(forwarded, ("batch", "lat"), diagonal)

    def across_of(joined):
        forwarded = lax.dynamic_slice_in_dim(joined, (1 - core) * half, half, axis=0)
        return lax.ppermute(forwarded, ("batch", "lat"), diagonal)

    high = local_qkv.shape[0]
    half = high // 2
    first_wide = 3 * WIDE + width // 2
    second_wide = 3 * WIDE + width

    def pack(kernel, group, scalar, other, wide, name):
        shapes = [(high, wide), (half, wide)]
        return run(
            kernel,
            1,
            scalar,
            [
                *[
                    pl.BlockSpec((high, WIDE), lambda i, c, at=2 * which + group: (0, at))
                    for which in range(3)
                ],
                whole_block(other),
            ],
            [local_qkv] * 3 + [other],
            shapes,
            [pl.BlockSpec(shape, lambda *_: (0, 0)) for shape in shapes],
            [],
            0,
            name,
        )

    local_first, half_first = pack(
        pack_first_kernel, 0, core_scalar, embed_weight, first_wide, "pack_first"
    )

    parts = 1
    count = windows // parts
    part_rows = count * kept_most
    code_tile = -(-count // 16) * 16
    sent_shape = (lon_size, part_rows + code_tile, pin)
    patch_rows = patches.reshape(windows, window_tokens, pin)
    kept_mask = lax.broadcasted_iota(jnp.int32, (windows, kept_most), 1) < kept_count.reshape(
        windows, 1
    )
    codes = jnp.where(kept_mask, kept_index.reshape(windows, kept_most), -1)
    partner_codes = other_core(codes)
    query_codes = jnp.concatenate([codes, partner_codes], axis=0).astype(jnp.float32)
    query_codes = query_codes.reshape(2 * rows, 1)
    global_starts = [(chip ^ which) * high for which in range(4)]
    global_offsets = jnp.stack([*global_starts, place]).astype(jnp.int32)
    sent = run(
        pick_kernel,
        1,
        after(core_scalar, half_first),
        [whole_block(patch_rows), whole_block(codes)],
        [patch_rows, codes],
        [sent_shape] * parts,
        [pl.BlockSpec(sent_shape, lambda *_: (0, 0, 0))] * parts,
        [],
        0,
        "pick",
    )
    query_codes, global_offsets = after((query_codes, global_offsets), sent)
    got = []
    for value in sent:
        value = after(value, got[-1]) if got else value
        got.append(lax.all_to_all(value, "lon", 0, 0, tiled=True))

    local_second, half_second = pack(
        pack_second_kernel, 1, after(core_scalar, sent), local_out, second_wide, "pack_second"
    )
    global_first, global_second = run(
        prepare_global_kernel,
        1,
        after(core_scalar, half_second),
        [
            pl.BlockSpec((high, WIDE), lambda i, c, which=which: (0, 2 * which + c[0]))
            for which in range(3)
        ],
        [global_qkv] * 3,
        [(high, 2 * WIDE), (high, WIDE)],
        [pl.BlockSpec((high, w), lambda *_: (0, 0)) for w in (2 * WIDE, WIDE)],
        [],
        0,
        "order_global",
    )
    sides_first = sides(half_first)
    sides_first = after(sides_first, (sent, global_first))
    sides_second = sides(after(half_second, sides_first))
    joined_first = lax.optimization_barrier(jnp.concatenate(sides_first, axis=0))
    across_first = across_of(joined_first)
    global_sides = sides(after(global_first, sides_second))
    joined_second = lax.optimization_barrier(jnp.concatenate(sides_second, axis=0))
    across_second = across_of(joined_second)

    def shared(shard, joined, diagonal_part, earlier):
        pieces = [shard, joined, other_core(joined), diagonal_part]
        pieces.append(other_core(after(diagonal_part, earlier)))
        bases = [(chip ^ which) * high for which in (1, 2, 3)]
        firsts = [chip * high, chip * high + half]
        for group in (bases[:2], bases[2:]):
            firsts += [base + core * half for base in group]
            firsts += [base + (1 - core) * half for base in group]
        firsts = jnp.stack(firsts).astype(jnp.int32)
        head = firsts // HD
        group_start = head // GROUP * WIDE
        main = group_start + head % GROUP * MAIN
        tail = group_start + GROUP * MAIN + head % GROUP * TAIL
        return pieces, jnp.stack([firsts, main, tail], axis=1).reshape(-1)

    shared_by = 2 if lon_size % 2 == 0 else 1
    block = shared_by * part_rows
    steps = lon_size // shared_by
    many_rows = lon_size * part_rows
    at_once = 2 * kept_most if block % (2 * kept_most) == 0 else kept_most
    mix = functools.partial(mix_heads, count=count, kept_most=kept_most, at_once=at_once)
    row_spec = lambda wide: pl.BlockSpec((block, wide), lambda i, _: (i, 0))
    tile_spec = pl.BlockSpec((shared_by, code_tile, MAIN), lambda i, _: (i, part_rows // code_tile, 0))

    pieces, offsets = shared(local_first, joined_first, across_first, core_scalar)
    embedded, normed, mixes = [], [], []
    for which in range(parts):
        if which == parts - 1:
            pieces = after(pieces, (joined_second, mixes))
        result = run(
            functools.partial(embed_window_kernel, mix),
            steps,
            offsets,
            [
                pl.BlockSpec((shared_by, part_rows, pin), lambda i, _: (i, 0, 0)),
                tile_spec,
                *map(whole_block, pieces),
            ],
            [got[which], got[which], *pieces],
            [(many_rows, width), (many_rows, width), (many_rows, WIDE)],
            [row_spec(width), row_spec(width), row_spec(WIDE)],
            [(width, 3 * WIDE), (pin, width), (block, 3 * WIDE)],
            0,
            "embed_windows",
        )
        for values, value in zip((embedded, normed, mixes), result):
            values.append(value)

    pieces, offsets = shared(local_second, joined_second, across_second, mixes[0])
    own, partner = [], []
    for which in range(parts):
        if which == parts - 1:
            pieces = after(pieces, (global_sides, own))
            global_sides, _ = after((global_sides, 0), own or mixes)
            global_across = across(*global_sides)
            value_sides = sides(after(global_second, global_sides))
        (result,) = run(
            functools.partial(window_out_kernel, mix),
            steps,
            offsets,
            [row_spec(width), row_spec(width), row_spec(WIDE), tile_spec, *map(whole_block, pieces)],
            [embedded[which], normed[which], mixes[which], got[which], *pieces],
            [(many_rows, width)],
            [row_spec(width)],
            [(width, 3 * WIDE), (block, 3 * WIDE), (block, WIDE), (inner, width)],
            2 * many_rows * (inner * width + width * 3 * WIDE),
            "windows_out",
        )
        own.append(result)
        if which == parts - 1:
            result = after(result, (global_across, value_sides))
        partner.append(other_core(result))
    value_across = across(*value_sides)
    partner_tiles = [
        other_core(after(value, own)[:, part_rows : part_rows + code_tile, :MAIN]) for value in got
    ]

    all_rows = lon_size * rows
    query_block = 256 if (2 * rows) % 256 == 0 else 2 * rows
    query_steps = 2 * rows // query_block
    project_steps = 2 * parts * steps
    pieces = [global_first, *global_sides, global_across, global_second, *value_sides, value_across]
    key_chunk = 512 if (2 * all_rows) % 512 == 0 else block
    late = lambda i: jnp.clip(i - project_steps, 0, query_steps - 1)
    normed_specs = [
        pl.BlockSpec((block, width), lambda i, _, at=at: (jnp.clip(i - at * steps, 0, steps - 1), 0))
        for at in range(2 * parts)
    ]
    whole_tile = pl.BlockSpec(
        (lon_size, code_tile, MAIN), lambda *_: (0, part_rows // code_tile, 0)
    )
    (mixed,) = run(
        functools.partial(group_kernel, steps, parts, count, kept_most, key_chunk),
        project_steps + query_steps,
        global_offsets,
        [
            *normed_specs,
            *[whole_tile] * parts,
            *map(whole_block, partner_tiles),
            pl.BlockSpec((query_block, 1), lambda i, _: (late(i), 0)),
            *map(whole_block, pieces),
        ],
        [*own, *partner, *got, *partner_tiles, query_codes, *pieces],
        [(2 * rows, WIDE)],
        [pl.BlockSpec((query_block, WIDE), lambda i, _: (late(i), 0))],
        [
            (width, 2 * WIDE),
            (width, WIDE),
            (2 * all_rows, WIDE),
            (2 * rows, WIDE),
            (2 * all_rows, WIDE),
            pltpu.VMEM((1, 2 * all_rows), jnp.float32),
        ],
        2 * WIDE * (2 * all_rows * 2 * width + 2 * rows * width + 4 * rows * 2 * all_rows),
        "groups",
    )

    mine, theirs = mixed[:rows], other_core(mixed[rows:])
    result = jnp.where(
        core == 0,
        jnp.concatenate([mine, theirs], axis=1),
        jnp.concatenate([theirs, mine], axis=1),
    )
    return result.reshape(1, lat_windows, lon_windows, kept_most, inner)


def body(patches, kept_index, kept_count, embed_weight, local_qkv, local_out, global_qkv):
    args = (patches, kept_index, kept_count, embed_weight, local_qkv, local_out, global_qkv)
    windows = patches.shape[1] * patches.shape[2]
    rows = windows * kept_index.shape[3]
    sample_rows = rows * lax.axis_size("lat") * lax.axis_size("lon")
    fits = patches.shape[3] <= 256 and windows % 2 == 0 and windows * kept_index.shape[3] % 32 == 0 and sample_rows * HEADS * HD * 2 <= vmem_limit // 4
    shards = embed_weight.shape[0] * 2 == local_qkv.shape[0] == local_out.shape[0] == 2 * HD
    if lax.axis_size("batch") == 4 and lax.axis_size("lat") == HEADS // GROUP == 2 and fits and shards:
        return sample_body(*args)
    return owner_body(*args)


def solution(mesh):
    return jax.shard_map(
        body,
        mesh=mesh,
        in_specs=(
            P("batch", "lat", "lon", None, None),
            P("batch", "lat", "lon", None),
            P("batch", "lat", "lon"),
            P("batch", None),
            P("batch", None),
            P("batch", None),
            P("batch", None),
        ),
        out_specs=P("batch", "lat", "lon", None, None),
        check_vma=False,
    )
```
